32 devices in a mesh: dp: 8 (over z, x), sp: 4 (over y, core).
Axes of the slice: x: 2, y: 2, z: 4, core: 2. Of those that a mesh axis runs over, the one named last changes fastest.
Arguments:
- tokens: bfloat16 [512, 32, 768], P('sp', 'dp'), may hold values from -6 to 6
- lengths: int32 [32], P('dp'), may hold values from 1 to 512, as said below
- w_query: bfloat16 [768, 768], replicated, may hold values from -0.21875 to 0.21875
- b_query: bfloat16 [768], replicated, may hold values from -2 to 2
- w_key: bfloat16 [768, 768], replicated, may hold values from -0.21875 to 0.21875
- w_value: bfloat16 [768, 768], replicated, may hold values from -0.21875 to 0.21875
- b_value: bfloat16 [768], replicated, may hold values from -2 to 2
- w_out: bfloat16 [768, 768], replicated, may hold values from -1.75 to 1.75
- b_out: bfloat16 [768], replicated, may hold values from -2 to 2
- gain_attn: bfloat16 [768], replicated, may hold values from 0.5 to 1.5
- shift_attn: bfloat16 [768], replicated, may hold values from -2 to 2
- w_up: bfloat16 [768, 3072], replicated, may hold values from -0.21875 to 0.21875
- b_up: bfloat16 [3072], replicated, may hold values from -3 to 3
- w_down: bfloat16 [3072, 768], replicated, may hold values from -0.109375 to 0.109375
- b_down: bfloat16 [768], replicated, may hold values from -2 to 2
- gain_ffn: bfloat16 [768], replicated, may hold values from 0.5 to 1.5
- shift_ffn: bfloat16 [768], replicated, may hold values from -2 to 2
- cotangent: bfloat16 [512, 32, 768], P('sp', 'dp'), may hold values from -6 to 6
Outputs:
- mixed: bfloat16 [512, 32, 768], P('sp', 'dp')
- grad_tokens: bfloat16 [512, 32, 768], P('sp', 'dp')
- grad_w_query: float32 [768, 768], P('dp')
- grad_b_query: float32 [768], P('dp')
- grad_w_key: float32 [768, 768], P('dp')
- grad_w_value: float32 [768, 768], P('dp')
- grad_b_value: float32 [768], P('dp')
- grad_w_out: float32 [768, 768], P('dp')
- grad_b_out: float32 [768], P('dp')
- grad_gain_attn: float32 [768], P('dp')
- grad_shift_attn: float32 [768], P('dp')
- grad_w_up: float32 [768, 3072], P('dp')
- grad_b_up: float32 [3072], P('dp')
- grad_w_down: float32 [3072, 768], P('dp')
- grad_b_down: float32 [768], P('dp')
- grad_gain_ffn: float32 [768], P('dp')
- grad_shift_ffn: float32 [768], P('dp')
The draws below stay inside these ranges and needn't reach their ends.
Inputs may be any that keep to these rules, and one draw needn't show every extreme that they name: Each pair's first lengths slots are live keys; in every aligned block of 4 pairs (those of one index of dp) at least one pair has all 512 slots live.
All inputs are finite; a program needn't handle non-finite values.
Results may differ from the reference program's by a relative error of at most 0.018.
Values may be sent and summed in bfloat16 or wider, within the bound.
A program may use at most 192 MiB of HBM per device.

```python
import jax
import jax.numpy as jnp
from jax import lax

D = 768
HEADS = 12
HD = 64
FF = 3072
LENGTH = 512
PAIRS_DEV = 4
PAIRS = 32


def draw_lengths(key, part):
    key = jax.random.fold_in(key, 7)
    key_shift, key_cut, key_full = jax.random.split(key, 3)
    shifts = jax.random.randint(key_shift, (PAIRS,), 0, 5)
    tops = jnp.maximum(jnp.right_shift(jnp.full((PAIRS,), LENGTH, jnp.int32), shifts), 1)
    cuts = jax.random.randint(key_cut, (PAIRS,), 0, jnp.maximum(tops // 2, 1))
    spans = jnp.maximum(tops - cuts, 1)
    full_slot = jax.random.randint(key_full, (PAIRS // PAIRS_DEV,), 0, PAIRS_DEV)
    indices = jnp.arange(PAIRS)
    chosen = full_slot[indices // PAIRS_DEV]
    spans = jnp.where(indices % PAIRS_DEV == chosen, LENGTH, spans)
    return spans.astype(jnp.int32)


def with_spikes(values, own_key, source, target, blocks, factor):
    owner, partner = [(jnp.arange(values.shape[dim]) // (values.shape[dim] // blocks)).reshape([-1 if axis == dim else 1 for axis in range(values.ndim)]) for dim in (source, target)]
    chosen = jax.random.permutation(own_key, blocks)[partner]
    strong = (owner == chosen) | (owner == (partner + blocks // 2) % blocks)
    return jnp.where(strong, factor * values, values)


def block_scale(stream_key, extent, cuts, low, top_value):
    loudness = 1.0
    for axis_at, shards_of in cuts:
        draws = jax.random.uniform(jax.random.fold_in(jax.random.fold_in(stream_key, 6), axis_at), (shards_of,), jnp.float32, low / len(cuts), top_value / len(cuts))
        loudness = loudness * jnp.repeat(jnp.exp(draws), extent[axis_at] // shards_of).reshape((-1,) + (1,) * (len(extent) - 1 - axis_at))
    return loudness


def scatter_about(key, dims, scale, bound, cuts=(), kind=jnp.bfloat16):
    result = jax.random.normal(key, dims, jnp.float32) * scale
    if len(cuts) > 0:
        result = block_scale(key, dims, cuts, -0.22, 0.18) * result
    return jnp.clip(result, min=-bound, max=bound).astype(kind)


def heavy_noise(own_key, shape, width, bound, shards, heavy, dtype=jnp.bfloat16):
    entries = width * jax.random.normal(own_key, shape, jnp.float32)
    if shards:
        entries = entries * block_scale(own_key, shape, shards, -0.22, 0.18)
    return jnp.clip(with_spikes(entries, jax.random.fold_in(own_key, 3), *heavy), -bound, bound).astype(dtype)


def setup_inputs(seed: int = 0) -> dict:
    seeds = jax.random.split(jax.random.key(seed), 19)
    tokens = scatter_about(seeds[0], (LENGTH, PAIRS, D), 1.0, 6.0, ((0, 4), (1, 8)))
    lengths = draw_lengths(jax.random.fold_in(seeds[18], 71), 0)
    w_query = scatter_about(seeds[2], (D, D), D ** -0.5, 0.21875)
    b_query = scatter_about(seeds[3], (D,), 0.3, 2.0)
    w_key = scatter_about(seeds[4], (D, D), D ** -0.5, 0.21875)
    w_value = scatter_about(seeds[5], (D, D), D ** -0.5, 0.21875)
    b_value = scatter_about(seeds[6], (D,), 0.3, 2.0)
    w_out = scatter_about(seeds[7], (D, D), (max(D // 64, 2)) ** -0.5, 1.75)
    b_out = scatter_about(seeds[8], (D,), 0.3, 2.0)
    gain_attn = jnp.clip(1.0 + 0.1 * jax.random.normal(seeds[9], (D,), jnp.float32), 0.5, 1.5).astype(jnp.bfloat16)
    shift_attn = scatter_about(seeds[10], (D,), 0.3, 2.0)
    w_up = scatter_about(seeds[11], (D, FF), D ** -0.5, 0.21875)
    b_up = scatter_about(seeds[12], (FF,), 0.5, 3.0)
    w_down = scatter_about(seeds[13], (FF, D), FF ** -0.5, 0.109375)
    b_down = scatter_about(seeds[14], (D,), 0.3, 2.0)
    gain_ffn = jnp.clip(1.0 + 0.1 * jax.random.normal(seeds[15], (D,), jnp.float32), 0.5, 1.5).astype(jnp.bfloat16)
    shift_ffn = scatter_about(seeds[16], (D,), 0.3, 2.0)
    cotangent = heavy_noise(seeds[17], (LENGTH, PAIRS, D), 1.0, 6.0, ((0, 4), (1, 8)), (1, 2, 8, 2.0))
    return {"tokens": tokens, "lengths": lengths, "w_query": w_query, "b_query": b_query, "w_key": w_key, "w_value": w_value, "b_value": b_value, "w_out": w_out, "b_out": b_out, "gain_attn": gain_attn, "shift_attn": shift_attn, "w_up": w_up, "b_up": b_up, "w_down": w_down, "b_down": b_down, "gain_ffn": gain_ffn, "shift_ffn": shift_ffn, "cotangent": cotangent}


@jax.custom_vjp
def low(v):
    return lax.optimization_barrier(v.astype(jnp.bfloat16)).astype(jnp.float32)

@jax.custom_vjp
def low_back(v):
    return v

def low_keep(v):
    return (low(v), None)

def low_pass(kept, grad):
    return (grad,)

def back_keep(v):
    return (v, None)

def back_low(kept, grad):
    return (low(grad),)
low.defvjp(low_keep, low_pass)
low_back.defvjp(back_keep, back_low)

def both_ways(value):
    return low(low_back(value))

def norm_layer(resid, gain, shift):
    center = resid - lax.optimization_barrier(jnp.mean(resid, axis=-1, keepdims=True))
    spread = lax.optimization_barrier(jnp.mean(center * center, axis=-1, keepdims=True))
    return center * lax.rsqrt(spread + 1e-05) * gain + shift

def project(left, weight):
    return jnp.einsum('lbd,de->lbe', left, weight, precision=lax.Precision.HIGHEST)

def layer(block, lens, w_query, b_query, w_key, w_value, b_value, w_out, b_out, gain_attn, shift_attn, w_up, b_up, w_down, b_down, gain_ffn, shift_ffn):
    span = block.shape[0]
    batch = block.shape[1]
    queries = both_ways(project(block, w_query) + b_query)
    keys = both_ways(project(block, w_key))
    values = both_ways(project(block, w_value) + b_value)
    query_heads = queries.reshape(span, batch, HEADS, HD)
    key_heads = keys.reshape(span, batch, HEADS, HD)
    value_heads = values.reshape(span, batch, HEADS, HD)
    scores = jnp.einsum('ibhe,jbhe->bhij', query_heads, key_heads, precision=lax.Precision.HIGHEST) * HD ** (-0.5)
    key_valid = jnp.arange(span)[None, :] < lens[:, None]
    scores = low_back(jnp.where(key_valid[:, None, None, :], scores, -1e+30))
    top_score = lax.optimization_barrier(jnp.max(scores, axis=-1, keepdims=True))
    expo = jnp.exp(scores - top_score)
    probs = low(expo / lax.optimization_barrier(jnp.sum(expo, axis=-1, keepdims=True)))
    attended = jnp.einsum('bhij,jbhe->ibhe', probs, value_heads, precision=lax.Precision.HIGHEST)
    attended = both_ways(attended.reshape(span, batch, HEADS * HD))
    branch = low_back(project(attended, w_out) + b_out)
    hidden = norm_layer(block + branch, gain_attn, shift_attn)
    inner = low_back(project(low(hidden), w_up) + b_up)
    activated = low(jax.nn.gelu(inner, approximate=False))
    ffn_out = low_back(project(activated, w_down) + b_down)
    return norm_layer(hidden + ffn_out, gain_ffn, shift_ffn)

def reference(tokens, lengths, w_query, b_query, w_key, w_value, b_value, w_out, b_out, gain_attn, shift_attn, w_up, b_up, w_down, b_down, gain_ffn, shift_ffn, cotangent):
    params = tuple((param.astype(jnp.float32) for param in (w_query, b_query, w_key, w_value, b_value, w_out, b_out, gain_attn, shift_attn, w_up, b_up, w_down, b_down, gain_ffn, shift_ffn)))
    span = tokens.shape[0]
    blocks = PAIRS // PAIRS_DEV
    tok_blocks = tokens.astype(jnp.float32).reshape(span, blocks, PAIRS_DEV, D).transpose(1, 0, 2, 3)
    cot_blocks = cotangent.astype(jnp.float32).reshape(span, blocks, PAIRS_DEV, D).transpose(1, 0, 2, 3)
    len_blocks = lengths.reshape(blocks, PAIRS_DEV)

    def step(totals, inputs):
        block, lens, cot_block = inputs

        def forward(block_in, *weights):
            return layer(block_in, lens, *weights)
        mixed_block, pullback = jax.vjp(forward, block, *params)
        grads = pullback(cot_block)
        totals = tuple((total_sum + grad_term for total_sum, grad_term in zip(totals, grads[1:])))
        return (totals, (mixed_block.astype(jnp.bfloat16), grads[0].astype(jnp.bfloat16)))
    zeros = tuple((jnp.zeros_like(param) for param in params))
    totals, outputs = lax.scan(step, zeros, (tok_blocks, len_blocks, cot_blocks))
    mixed = outputs[0].transpose(1, 0, 2, 3).reshape(span, PAIRS, D)
    grad_tokens = outputs[1].transpose(1, 0, 2, 3).reshape(span, PAIRS, D)
    return (mixed, grad_tokens, totals[0], totals[1], totals[2], totals[3], totals[4], totals[5], totals[6], totals[7], totals[8], totals[9], totals[10], totals[11], totals[12], totals[13], totals[14])
```

```python
import functools

import jax
import jax.numpy as jnp
from jax import lax
from jax.experimental import pallas as pl
from jax.experimental.pallas import tpu as pltpu
from jax.sharding import PartitionSpec as P

HEADS = 12
HD = 64
EPS = 1e-05
MESH_ID = pl.DeviceIdType.MESH
BF = jnp.bfloat16
F32 = jnp.float32


def nn(left, right):
    return jnp.dot(left, right, preferred_element_type=F32)


def nt(left, right):
    return lax.dot_general(left, right, (((1,), (1,)), ((), ())), preferred_element_type=F32)


def tn(left, right):
    return lax.dot_general(left, right, (((0,), (0,)), ((), ())), preferred_element_type=F32)


def aligned(start, step=128):
    return pl.multiple_of(start, step)


ROUTES = {
    "A": ("c", "0", "1", "2", "Y"),
    "B": ("c", "y", "0", "1", "2"),
    "C": ("c", "1", "2", "0", "Y"),
}
UNITS = (
    ("d", 0), ("d", 1), ("d", 2), ("u", 0), ("u", 1), ("u", 2),
    ("a", 3), ("a", 0), ("a", 1), ("a", 2),
)
PATH = ("A", "B", "A", "C", "B", "A", "B", "A", "B", "A")
ROWS_VEC = 16
STAGES = 7


def land_shape(rows, cols, route, stage):
    lead, r, c = [2, 2, 2], rows, cols
    for kind in ROUTES[route][: stage + 1]:
        if kind == "c":
            c //= 2
        elif kind == "y":
            r //= 2
        elif kind != "Y":
            lead[2 - int(kind)] = 0
    return tuple(n for n in lead if n) + (r, c)


def layer_kernel(*refs):
    it = iter(refs)
    (len_ref, vec_ref, tok_ref, cot_ref, wq_ref, wk_ref, wv_ref, wo_ref, wu_ref, wd_ref) = (next(it) for _ in range(10))
    (mix_out, dtok_out, ga_out, gu_out, gd_out, gv_out) = (next(it) for _ in range(6))
    (x_s, cot_s, wa, wu, wd, q_s, k_s, v_s, p_s, att_s, linv_s, xh_s, rs_s, hl_s, act_s, gp_s, acc_s, dh_s, mix_s) = (
        next(it) for _ in range(19)
    )
    vs, vl = next(it), next(it)
    lands = [[next(it) for _ in ROUTES[path]] for path in PATH]
    finals = [next(it) if path != "B" else None for path in PATH]
    (wsem, lsem, asend, arecv, usend, urecv, vsend, vrecv) = (next(it) for _ in range(8))

    rows_loc, width = tok_ref.shape[1], tok_ref.shape[2]
    total = rows_loc * 4
    half = total // 2
    dp, sp = lax.axis_index("dp"), lax.axis_index("sp")
    bits = [lax.rem(lax.div(dp, 2**k), 2) for k in range(3)]
    core, ybit = lax.rem(sp, 2), lax.div(sp, 2)

    def sp_xor(k):
        low, high = core, ybit
        if k & 1:
            low = 1 - low
        if k & 2:
            high = 1 - high
        return high * 2 + low

    def peer(kind):
        if kind == "c":
            return (dp, sp_xor(1))
        if kind in "yY":
            return (dp, sp_xor(2))
        k = int(kind)
        return (dp + 2**k * (1 - 2 * bits[k]), sp)

    barrier = pltpu.get_barrier_semaphore()
    greet = [(dp, sp_xor(k)) for k in (1, 2, 3)] + [peer(k) for k in "012"]
    for other in greet:
        pl.semaphore_signal(barrier, inc=1, device_id=other, device_id_type=MESH_ID)

    loads = []

    def load(src, dst):
        copy = pltpu.make_async_copy(src, dst, wsem.at[len(loads)])
        copy.start()
        loads.append(copy)
        return copy

    own_tok = load(tok_ref.at[sp], x_s.at[pl.ds(aligned(sp * rows_loc), rows_loc)])
    attn_loads = [load(ref, wa.at[i]) for i, ref in enumerate((wq_ref, wk_ref, wv_ref, wo_ref))]
    pl.semaphore_wait(barrier, len(greet))

    def exchange(src, dst, base):
        copies = []
        for k in (2, 3, 1):
            other = sp_xor(k)
            copy = pltpu.make_async_remote_copy(
                src_ref=src.at[other],
                dst_ref=dst.at[pl.ds(aligned(sp * rows_loc), rows_loc)],
                send_sem=asend.at[base + k - 1],
                recv_sem=arecv.at[base + k - 1],
                device_id=(dp, other),
                device_id_type=MESH_ID,
            )
            copy.start()
            copies.append(copy)
        return copies

    tok_copies = exchange(tok_ref, x_s, 0)
    up_loads = [
        [load(wu_ref.at[:, :, :, :, pl.ds(384 * r + 128 * j, 128)], wu.at[j, :, :, :, :, pl.ds(128 * r, 128)]) for r in range(8)]
        for j in range(3)
    ]
    down_loads = [load(wd_ref.at[:, :, :, j], wd.at[j]) for j in range(3)]
    own_cot = load(cot_ref.at[sp], cot_s.at[pl.ds(aligned(sp * rows_loc), rows_loc)])

    state = [dict(stage=0, copies=[]) for _ in UNITS]

    def home(unit):
        kind, j = unit
        return {"d": wd, "u": wu, "a": wa}[kind], j

    def region(unit, kinds, last_other=False):
        ref, j = home(unit)
        rows, cols = ref.shape[4], ref.shape[5]
        lead = [slice(None)] * 3
        rsl, csl = slice(None), slice(None)
        for i, kind in enumerate(kinds):
            flip = last_other and i == len(kinds) - 1
            if kind == "c":
                at = 1 - core if flip else core
                csl = pl.ds(aligned(at * (cols // 2)), cols // 2)
            elif kind == "y":
                at = 1 - ybit if flip else ybit
                rsl = pl.ds(aligned(at * (rows // 2), 16), rows // 2)
            elif kind != "Y":
                b = bits[int(kind)]
                lead[2 - int(kind)] = 1 - b if flip else b
        return ref, (j, *lead, rsl, csl)

    def send(n, stage, src, dst, to):
        copy = pltpu.make_async_remote_copy(
            src_ref=src,
            dst_ref=dst,
            send_sem=usend.at[n, stage],
            recv_sem=urecv.at[n, stage],
            device_id=to,
            device_id_type=MESH_ID,
        )
        copy.start()
        state[n]["copies"].append(copy)

    def out_region(unit, at_core, at_y=None):
        kind, j = unit
        ref = {"d": gd_out, "u": gu_out, "a": ga_out}[kind]
        rows, cols = ref.shape[1], ref.shape[2]
        rsl = slice(None) if at_y is None else pl.ds(aligned(at_y * (rows // 2), 16), rows // 2)
        return ref.at[j, rsl, pl.ds(aligned(at_core * (cols // 2)), cols // 2)]

    def advance(n):
        unit, path = UNITS[n], PATH[n]
        route = ROUTES[path]
        stage = state[n]["stage"]
        state[n]["stage"] += 1
        if stage > 0:
            state[n]["copies"][stage - 1].wait_recv()
            kind = route[stage - 1]
            ref, at = region(unit, route[:stage])
            if kind == "Y":
                finals[n][...] = ref[at] + lands[n][stage - 1][...]
            else:
                ref[at] = ref[at] + lands[n][stage - 1][...]
        if stage < len(route):
            kind = route[stage]
            ref, at = region(unit, route[: stage + 1], last_other=True)
            send(n, stage, ref.at[at], lands[n][stage], peer(kind))
            return
        if path == "B":
            ref, at = region(unit, route)
            src, dst = ref.at[at], out_region(unit, core, ybit)
            for k in (1, 2, 3):
                send(n, stage + k - 1, src, dst, (dp, sp_xor(k)))
        else:
            src, dst = finals[n], out_region(unit, core)
            send(n, stage, src, dst, peer("c"))
        local = pltpu.make_async_copy(src, dst, lsem.at[n])
        local.start()
        state[n]["local"] = local

    def finish(n):
        while state[n]["stage"] <= len(ROUTES[PATH[n]]):
            advance(n)
        for copy in state[n]["copies"][len(ROUTES[PATH[n]]) :]:
            copy.wait_recv()
        for copy in state[n]["copies"]:
            copy.wait_send()
        state[n]["local"].wait()

    def vec(row, size=None):
        return vec_ref[pl.ds(row, 1), pl.ds(0, width if size is None else size)]

    def put_vec(row, value):
        vs[0, pl.ds(row, 1), pl.ds(0, value.shape[1])] = value

    vs[0] = jnp.zeros(vs.shape[1:], F32)

    def qkv(start):
        x = x_s[pl.ds(start, half), :]

        def tile(i, carry):
            cols = pl.ds(aligned(i * 256), 256)
            for w, (dst, row) in enumerate(((q_s, 0), (k_s, None), (v_s, 1))):
                r = nn(x, wa[w, :, :, :, :, cols].reshape(width, 256))
                if row is not None:
                    r = r + vec_ref[pl.ds(row, 1), cols]
                if w == 0:
                    r = r * HD ** (-0.5)
                dst[pl.ds(start, half), cols] = r.astype(BF)
            return carry

        lax.fori_loop(0, width // 256, tile, 0)

    for copy in attn_loads[:3]:
        copy.wait()
    own_tok.wait()
    tok_copies[2].wait_recv()
    qkv(aligned(ybit * half))
    tok_copies[0].wait_recv()
    tok_copies[1].wait_recv()
    cot_copies = exchange(cot_ref, cot_s, 3)
    qkv(aligned((1 - ybit) * half))

    length = len_ref[sp]
    lane = lax.broadcasted_iota(jnp.int32, (total, 128), 1)
    low = lane < HD
    groups = HEADS // 2

    def attend(g, carry):
        cols = pl.ds(aligned(g * 128), 128)
        q2, k2, v2 = q_s[:, cols], k_s[:, cols], v_s[:, cols]
        outs = []
        for h in range(2):
            mine = low if h == 0 else jnp.logical_not(low)
            qh = jnp.where(mine, q2, jnp.zeros_like(q2))
            vh = jnp.where(mine, v2, jnp.ones_like(v2))
            s = nt(qh, k2)
            s = jnp.where(lax.broadcasted_iota(jnp.int32, s.shape, 1) < length, s, -1e30)
            e = jnp.exp(s - jnp.max(s, axis=-1, keepdims=True)).astype(BF)
            p_s[g * 2 + h] = e
            outs.append(nn(e, vh))
        num = jnp.where(low, outs[0], outs[1])
        den = pltpu.roll(jnp.where(low, outs[1], outs[0]), HD, axis=1)
        inv = 1.0 / den
        linv_s[:, cols] = inv.astype(BF)
        att_s[:, cols] = (num * inv).astype(BF)
        return carry

    lax.fori_loop(0, groups, attend, 0)

    attn_loads[3].wait()
    wo = wa.at[3]

    def first_norm(i, carry):
        rows = pl.ds(aligned(i * 256, 256), 256)
        r = nn(att_s[rows, :], wo[...].reshape(width, width)) + vec(2) + x_s[rows, :].astype(F32)
        mean = jnp.mean(r, axis=-1, keepdims=True)
        center = r - mean
        rs = lax.rsqrt(jnp.mean(center * center, axis=-1, keepdims=True) + EPS)
        xh = center * rs
        hidden = xh * vec(3) + vec(4)
        rs_s[rows, :] = rs
        xh_s[rows, :] = xh
        acc_s[rows, :] = hidden
        hl_s[rows, :] = hidden.astype(BF)
        return carry

    lax.fori_loop(0, total // 256, first_norm, 0)

    for j in range(3):
        for copy in up_loads[j]:
            copy.wait()

        def up(t, carry, j=j):
            cols = pl.ds(aligned(t * 256), 256)
            inner = nn(hl_s[...], wu[j, :, :, :, :, cols].reshape(width, 256)) + vec_ref[pl.ds(10 + j, 1), cols]
            cdf = 0.5 + 0.5 * lax.erf(inner * (0.5**0.5))
            pdf = jnp.exp(-0.5 * inner * inner) * 0.3989422804014327
            act_s[j, :, cols] = (inner * cdf).astype(BF)
            gp_s[j, :, cols] = (cdf + inner * pdf).astype(BF)
            return carry

        lax.fori_loop(0, 4, up, 0)

    for copy in down_loads:
        copy.wait()

    def down(i, carry):
        cols = pl.ds(aligned(i * 256), 256)
        r = acc_s[:, cols] + vec_ref[pl.ds(5, 1), cols]
        for j in range(3):
            r = r + nn(act_s[j], wd[j, :, :, :, :, cols].reshape(1024, 256))
        acc_s[:, cols] = r
        return carry

    lax.fori_loop(0, width // 256, down, 0)

    own_cot.wait()
    for copy in cot_copies:
        copy.wait_recv()

    def second_norm(i, carry):
        rows = pl.ds(aligned(i * 128, 128), 128)
        r = acc_s[rows, :]
        mean = jnp.mean(r, axis=-1, keepdims=True)
        center = r - mean
        rs = lax.rsqrt(jnp.mean(center * center, axis=-1, keepdims=True) + EPS)
        xh = center * rs
        mix_s[rows, :] = (xh * vec(6) + vec(7)).astype(BF)
        dy = cot_s[rows, :].astype(F32)
        dxh = dy * vec(6)
        d2 = rs * (dxh - jnp.mean(dxh, axis=-1, keepdims=True) - xh * jnp.mean(dxh * xh, axis=-1, keepdims=True))
        acc_s[rows, :] = d2
        low2 = d2.astype(BF)
        cot_s[rows, :] = low2
        sums = (
            jnp.sum(dy * xh, axis=0, keepdims=True),
            jnp.sum(dy, axis=0, keepdims=True),
            jnp.sum(low2.astype(F32), axis=0, keepdims=True),
        )
        return tuple(c + s for c, s in zip(carry, sums))

    zero = jnp.zeros((1, width), F32)
    g_gain, g_shift, g_bdown = lax.fori_loop(0, total // 128, second_norm, (zero, zero, zero))
    put_vec(6, g_gain)
    put_vec(7, g_shift)
    put_vec(5, g_bdown)

    def give_back(src, dst, base):
        copies = []
        for k in (2, 3, 1):
            other = sp_xor(k)
            copy = pltpu.make_async_remote_copy(
                src_ref=src.at[pl.ds(aligned(other * rows_loc), rows_loc)],
                dst_ref=dst.at[sp],
                send_sem=asend.at[base + k - 1],
                recv_sem=arecv.at[base + k - 1],
                device_id=(dp, other),
                device_id_type=MESH_ID,
            )
            copy.start()
            copies.append(copy)
        own = pltpu.make_async_copy(src.at[pl.ds(aligned(sp * rows_loc), rows_loc)], dst.at[sp], lsem.at[10 + base // 3])
        own.start()
        return copies, own

    mix_copies, mix_own = give_back(mix_s, mix_out, 6)

    def inner_back(j):
        def tile(i, carry):
            a, b = lax.div(i, 2), lax.rem(i, 2)
            cols = pl.ds(aligned(i * 256), 256)
            d = nt(cot_s[...], wd[j, a, b].reshape(256, width)) * gp_s[j, :, cols].astype(F32)
            d = d.astype(BF)
            gp_s[j, :, cols] = d
            vs[0, pl.ds(10 + j, 1), cols] = jnp.sum(d.astype(F32), axis=0, keepdims=True)
            return carry

        lax.fori_loop(0, 4, tile, 0)

    def grad_down(j):
        def tile(i, carry):
            a, b = lax.div(i, 2), lax.rem(i, 2)
            cols = pl.ds(aligned(i * 256), 256)
            wd[j, a, b] = tn(act_s[j, :, cols], cot_s[...]).astype(BF).reshape(2, 128, width)
            return carry

        lax.fori_loop(0, 4, tile, 0)

    def hidden_back(j):
        def tile(a, carry):
            cols = pl.ds(aligned(a * 384), 384)
            acc_s[:, cols] += nt(gp_s[j], wu[j, a].reshape(384, 1024))
            return carry

        lax.fori_loop(0, 2, tile, 0)

    def grad_up(j):
        def tile(i, carry):
            a, b = lax.div(i, 4), lax.rem(i, 4)
            cols = pl.ds(aligned(b * 256), 256)
            r = tn(hl_s[:, pl.ds(aligned(a * 384), 384)], gp_s[j, :, cols])
            wu[j, a, :, :, :, cols] = r.astype(BF).reshape(2, 2, 96, 256)
            return carry

        lax.fori_loop(0, 8, tile, 0)

    inner_back(0)
    grad_down(0)
    advance(0)
    inner_back(1)
    grad_down(1)
    advance(1)
    advance(0)
    inner_back(2)
    grad_down(2)
    advance(2)
    advance(1)
    hidden_back(0)
    grad_up(0)
    advance(3)
    advance(2)
    hidden_back(1)
    advance(0)
    advance(3)
    grad_up(1)
    advance(4)
    hidden_back(2)
    advance(1)
    advance(4)
    grad_up(2)
    advance(5)

    def first_back(i, carry):
        rows = pl.ds(aligned(i * 128, 128), 128)
        dy = acc_s[rows, :]
        xh = xh_s[rows, :]
        dxh = dy * vec(3)
        d1 = rs_s[rows, :] * (
            dxh - jnp.mean(dxh, axis=-1, keepdims=True) - xh * jnp.mean(dxh * xh, axis=-1, keepdims=True)
        )
        acc_s[rows, :] = d1
        low1 = d1.astype(BF)
        dh_s[rows, :] = low1
        sums = (
            jnp.sum(dy * xh, axis=0, keepdims=True),
            jnp.sum(dy, axis=0, keepdims=True),
            jnp.sum(low1.astype(F32), axis=0, keepdims=True),
        )
        return tuple(c + s for c, s in zip(carry, sums))

    g_gain, g_shift, g_bout = lax.fori_loop(0, total // 128, first_back, (zero, zero, zero))
    put_vec(3, g_gain)
    put_vec(4, g_shift)
    put_vec(2, g_bout)
    advance(5)
    advance(0)
    advance(2)

    def attended_back(a, carry):
        cols = pl.ds(aligned(a * 384), 384)
        d = nt(dh_s[...], wo[a].reshape(384, width)) * linv_s[:, cols].astype(F32)
        mix2[:, cols] = d.astype(BF)
        return carry

    mix2 = hl_s
    lax.fori_loop(0, 2, attended_back, 0)

    def grad_out(i, carry):
        a, b = lax.div(i, 3), lax.rem(i, 3)
        cols = pl.ds(aligned(b * 256), 256)
        r = tn(att_s[:, pl.ds(aligned(a * 384), 384)], dh_s[:, cols])
        wa[3, a, :, :, :, cols] = r.astype(BF).reshape(2, 2, 96, 256)
        return carry

    lax.fori_loop(0, 6, grad_out, 0)
    advance(6)
    advance(3)
    advance(1)
    advance(0)

    def attend_back(g, carry):
        cols = pl.ds(aligned(g * 128), 128)
        q2, k2, v2, d2 = q_s[:, cols], k_s[:, cols], v_s[:, cols], mix2[:, cols]
        prod = d2.astype(F32) * att_s[:, cols].astype(F32)
        dqs, dks, dvs = [], [], []
        for h in range(2):
            mine = low if h == 0 else jnp.logical_not(low)
            dah = jnp.where(mine, d2, jnp.zeros_like(d2))
            delta = jnp.sum(jnp.where(mine, prod, 0.0), axis=-1, keepdims=True)
            e = p_s[g * 2 + h]
            ds = (e.astype(F32) * (nt(dah, v2) - delta)).astype(BF)
            dqs.append(nn(ds, k2))
            dks.append(tn(ds, q2))
            dvs.append(tn(e, d2))
        dq = (jnp.where(low, dqs[0], dqs[1]) * HD ** (-0.5)).astype(BF)
        dk = jnp.where(low, dks[0], dks[1]).astype(BF)
        dv = jnp.where(low, dvs[0], dvs[1]).astype(BF)
        q_s[:, cols] = dq
        k_s[:, cols] = dk
        v_s[:, cols] = dv
        vs[0, pl.ds(0, 1), cols] = jnp.sum(dq.astype(F32), axis=0, keepdims=True)
        vs[0, pl.ds(1, 1), cols] = jnp.sum(dv.astype(F32), axis=0, keepdims=True)
        return carry

    lax.fori_loop(0, 2, attend_back, 0)
    for n in (6, 5, 4, 2, 1, 3):
        advance(n)
    lax.fori_loop(2, 4, attend_back, 0)
    for n in (0, 4, 5, 6, 3, 2, 1):
        advance(n)
    lax.fori_loop(4, 6, attend_back, 0)

    vec_copies = []

    def vec_step(i):
        if i > 0:
            vec_copies[i - 1].wait_recv()
            vs[i] = vs[i - 1] + vl[i - 1]
        if i < 5:
            copy = pltpu.make_async_remote_copy(
                src_ref=vs.at[i],
                dst_ref=vl.at[i],
                send_sem=vsend.at[i],
                recv_sem=vrecv.at[i],
                device_id=peer("c012y"[i]),
                device_id_type=MESH_ID,
            )
            copy.start()
            vec_copies.append(copy)

    vec_step(0)

    def tokens_back(w, src):
        def tile(a, carry):
            cols = pl.ds(aligned(a * 384), 384)
            r = acc_s[:, cols] + nt(src[...], wa[w, a].reshape(384, width))
            if w == 2:
                dh_s[:, cols] = r.astype(BF)
            else:
                acc_s[:, cols] = r
            return carry

        lax.fori_loop(0, 2, tile, 0)

    def grad_proj(w, src):
        def tile(i, carry):
            a, b = lax.div(i, 3), lax.rem(i, 3)
            cols = pl.ds(aligned(b * 256), 256)
            r = tn(x_s[:, pl.ds(aligned(a * 384), 384)], src[:, cols])
            wa[w, a, :, :, :, cols] = r.astype(BF).reshape(2, 2, 96, 256)
            return carry

        lax.fori_loop(0, 6, tile, 0)

    tokens_back(0, q_s)
    grad_proj(0, q_s)
    advance(7)
    vec_step(1)
    tokens_back(1, k_s)
    grad_proj(1, k_s)
    advance(8)
    advance(7)
    vec_step(2)
    tokens_back(2, v_s)
    grad_proj(2, v_s)
    advance(9)
    tok_back, tok_own = give_back(dh_s, dtok_out, 9)
    advance(8)
    vec_step(3)
    advance(9)

    for _ in range(4):
        for n in range(len(UNITS)):
            if state[n]["stage"] <= len(ROUTES[PATH[n]]):
                advance(n)
        if len(vec_copies) < 5:
            vec_step(len(vec_copies))
    vec_step(5)
    gv_out[...] = vs[5]
    for n in range(len(UNITS)):
        finish(n)
    for copy in vec_copies:
        copy.wait_send()
    for copy in tok_copies + cot_copies:
        copy.wait_send()
    for copy in mix_copies + tok_back:
        copy.wait()
    mix_own.wait()
    tok_own.wait()


def fused(
    tokens, lengths, w_query, b_query, w_key, w_value, b_value, w_out, b_out, gain_attn, shift_attn,
    w_up, b_up, w_down, b_down, gain_ffn, shift_ffn, cotangent,
):
    rows_loc, pairs, width = tokens.shape
    total = rows_loc * 4
    rows = width // 8
    rows8 = [b_query, b_value, b_out, gain_attn, shift_attn, b_down, gain_ffn, shift_ffn]
    table = jnp.stack([jnp.pad(v.astype(F32), (0, 1024 - width)) for v in rows8] + [jnp.zeros((1024,), F32)] * 2)
    up_bias = b_up.astype(F32).reshape(8, 3, 128).transpose(1, 0, 2).reshape(3, 1024)
    table = jnp.concatenate([table, up_bias, jnp.zeros((3, 1024), F32)])
    square = lambda w: w.reshape(2, 2, 2, rows, w.shape[1])
    args = (
        lengths, table, tokens.transpose(1, 0, 2), cotangent.transpose(1, 0, 2),
        square(w_query), square(w_key), square(w_value), square(w_out), square(w_up),
        w_down.reshape(2, 2, 2, 3, 128, width),
    )
    shapes = {"d": (128, width), "u": (rows, 1024), "a": (rows, width)}
    vm = lambda shape, dtype=BF: pltpu.VMEM(shape, dtype)
    scratch = [
        vm((total, width)), vm((total, width)),
        vm((4, 2, 2, 2, rows, width)), vm((3, 2, 2, 2, rows, 1024)), vm((3, 2, 2, 2, 128, width)),
        vm((total, width)), vm((total, width)), vm((total, width)),
        vm((HEADS, total, total)), vm((total, width)), vm((total, width)),
        vm((total, width), F32), vm((total, 1), F32), vm((total, width)),
        vm((3, total, 1024)), vm((3, total, 1024)),
        vm((total, width), F32), vm((total, width)), vm((total, width)),
        vm((6, ROWS_VEC, 1024), F32), vm((5, ROWS_VEC, 1024), F32),
    ]
    for unit, path in zip(UNITS, PATH):
        scratch += [vm(land_shape(*shapes[unit[0]], path, s)) for s in range(5)]
    for unit, path in zip(UNITS, PATH):
        if path != "B":
            r, c = shapes[unit[0]]
            scratch.append(vm((r, c // 2)))
    dma = pltpu.SemaphoreType.DMA
    scratch += [dma((40,)), dma((14,)), dma((12,)), dma((12,)), dma((10, 8)), dma((10, 8)), dma((5,)), dma((5,))]
    anywhere = pl.BlockSpec(memory_space=pl.ANY)
    out = pl.pallas_call(
        layer_kernel,
        out_shape=(
            jax.ShapeDtypeStruct((4, rows_loc, width), BF),
            jax.ShapeDtypeStruct((4, rows_loc, width), BF),
            jax.ShapeDtypeStruct((4, rows, width), BF),
            jax.ShapeDtypeStruct((3, rows, 1024), BF),
            jax.ShapeDtypeStruct((3, 128, width), BF),
            jax.ShapeDtypeStruct((ROWS_VEC, 1024), F32),
        ),
        in_specs=[pl.BlockSpec(memory_space=pltpu.SMEM), pl.BlockSpec(memory_space=pltpu.VMEM)] + [anywhere] * 8,
        out_specs=(anywhere,) * 5 + (pl.BlockSpec(memory_space=pltpu.VMEM),),
        scratch_shapes=scratch,
        compiler_params=pltpu.CompilerParams(collective_id=0, has_side_effects=True, vmem_limit_bytes=63 * 2**20),
    )(*args)
    mixed, dtok, ga, gu, gd, gv = out
    at = lax.axis_index("dp")
    low = lax.dynamic_slice(gv[:8, :width].reshape(8, 8, rows), (0, at, 0), (8, 1, rows))[:, 0]
    bup = lax.dynamic_slice(gv[10:13].reshape(3, 8, 128), (0, at, 0), (3, 1, 128)).reshape(384)
    ga = ga.astype(F32)
    return (
        mixed.transpose(1, 0, 2),
        dtok.transpose(1, 0, 2),
        ga[0], low[0], ga[1], ga[2], low[1], ga[3], low[2], low[3], low[4],
        gu.astype(F32).reshape(3, rows, 8, 128).transpose(1, 2, 0, 3).reshape(rows, 3072),
        bup,
        gd.astype(F32).reshape(384, width),
        low[5], low[6], low[7],
    )


def norm_layer(resid, gain, shift):
    center = resid - jnp.mean(resid, axis=-1, keepdims=True)
    spread = jnp.mean(center * center, axis=-1, keepdims=True)
    return center * lax.rsqrt(spread + 1e-05) * gain + shift


def exact_gelu(value):
    return jax.nn.gelu(value, approximate=False)


def project(left, weight):
    return jnp.einsum("spd,de->spe", left, weight, preferred_element_type=jnp.float32)


def back_project(grad_in, weight):
    return jnp.einsum("spe,de->spd", grad_in, weight, preferred_element_type=jnp.float32)


def weight_grad(left, right):
    return jnp.einsum("spd,spe->de", left, right, preferred_element_type=jnp.float32)


def column_sum(grad_in):
    return jnp.sum(grad_in.astype(jnp.float32), axis=(0, 1))


def shards(
    tokens,
    lengths,
    w_query,
    b_query,
    w_key,
    w_value,
    b_value,
    w_out,
    b_out,
    gain_attn,
    shift_attn,
    w_up,
    b_up,
    w_down,
    b_down,
    gain_ffn,
    shift_ffn,
    cotangent,
):
    local_rows, pair_count, model_width = tokens.shape
    score_scale = HD ** (-0.5)
    total_len = local_rows * lax.axis_size("sp")
    queries = (project(tokens, w_query) + b_query.astype(jnp.float32)).astype(jnp.bfloat16)
    keys_local = project(tokens, w_key).astype(jnp.bfloat16)
    values_local = (project(tokens, w_value) + b_value.astype(jnp.float32)).astype(jnp.bfloat16)
    keys_all, values_all = (
        lax.all_gather(keys_local, "sp", axis=0, tiled=True),
        lax.all_gather(values_local, "sp", axis=0, tiled=True),
    )
    query_heads = queries.reshape(local_rows, pair_count, HEADS, HD)
    key_heads = keys_all.reshape(total_len, pair_count, HEADS, HD)
    value_heads = values_all.reshape(total_len, pair_count, HEADS, HD)
    scores = (
        jnp.einsum("iphe,jphe->phij", query_heads, key_heads, preferred_element_type=jnp.float32)
        * score_scale
    )
    key_valid = jnp.arange(total_len)[None, :] < lengths[:, None]
    scores = jnp.where(key_valid[:, None, None, :], scores, -1e30)
    top_score = jnp.max(scores, axis=-1, keepdims=True)
    expo = jnp.exp(scores - top_score)
    row_total = jnp.sum(expo, axis=-1, keepdims=True)
    weights_full = expo / row_total
    probs = weights_full.astype(jnp.bfloat16)
    attended = jnp.einsum("phij,jphe->iphe", probs, value_heads, preferred_element_type=jnp.float32)
    attended_low = attended.reshape(local_rows, pair_count, model_width).astype(jnp.bfloat16)
    branch = project(attended_low, w_out) + b_out.astype(jnp.float32)
    first_sum = tokens.astype(jnp.float32) + branch
    hidden, first_back = jax.vjp(
        norm_layer, first_sum, gain_attn.astype(jnp.float32), shift_attn.astype(jnp.float32)
    )
    hidden_low = hidden.astype(jnp.bfloat16)
    inner = project(hidden_low, w_up) + b_up.astype(jnp.float32)
    activated, gelu_back = jax.vjp(exact_gelu, inner)
    activated_low = activated.astype(jnp.bfloat16)
    second_sum = hidden + project(activated_low, w_down) + b_down.astype(jnp.float32)
    mixed, second_back = jax.vjp(
        norm_layer, second_sum, gain_ffn.astype(jnp.float32), shift_ffn.astype(jnp.float32)
    )
    d_second, grad_gain_ffn, grad_shift_ffn = second_back(cotangent.astype(jnp.float32))
    d_ffn = d_second.astype(jnp.bfloat16)
    grad_down = weight_grad(activated_low, d_ffn)
    grad_bdown = column_sum(d_ffn)
    d_inner = gelu_back(back_project(d_ffn, w_down))[0].astype(jnp.bfloat16)
    grad_up = weight_grad(hidden_low, d_inner)
    grad_bup = column_sum(d_inner)
    d_hidden = d_second + back_project(d_inner, w_up)
    d_first, grad_gain_attn, grad_shift_attn = first_back(d_hidden)
    d_branch = d_first.astype(jnp.bfloat16)
    grad_out = weight_grad(attended_low, d_branch)
    grad_bout = column_sum(d_branch)
    d_attended = back_project(d_branch, w_out).astype(jnp.bfloat16)
    d_att_heads = d_attended.reshape(local_rows, pair_count, HEADS, HD)
    d_probs = jnp.einsum(
        "iphe,jphe->phij", d_att_heads, value_heads, preferred_element_type=jnp.float32
    )
    row_delta = jnp.sum(weights_full * d_probs, axis=-1, keepdims=True)
    d_scores = weights_full * (d_probs - row_delta)
    d_scores_low = d_scores.astype(jnp.bfloat16)
    d_query_heads = (
        jnp.einsum("phij,jphe->iphe", d_scores_low, key_heads, preferred_element_type=jnp.float32)
        * score_scale
    )
    d_queries = d_query_heads.reshape(local_rows, pair_count, model_width).astype(jnp.bfloat16)
    row_count = local_rows * lax.axis_size("sp")
    key_part = (
        jnp.einsum("phij,iphe->jphe", d_scores_low, query_heads, preferred_element_type=jnp.float32)
        * score_scale
    )
    value_part = jnp.einsum(
        "phij,iphe->jphe", probs, d_att_heads, preferred_element_type=jnp.float32
    )
    key_grads = lax.psum_scatter(
        jnp.concatenate(
            (
                key_part.reshape(row_count, pair_count, model_width),
                value_part.reshape(row_count, pair_count, model_width),
            ),
            axis=2,
        ).astype(jnp.bfloat16),
        "sp",
        scatter_dimension=0,
        tiled=True,
    ).astype(jnp.float32)
    d_keys = key_grads[:, :, :model_width].astype(jnp.bfloat16)
    d_values = key_grads[:, :, model_width:].astype(jnp.bfloat16)
    grad_query = weight_grad(tokens, d_queries)
    grad_bquery = column_sum(d_queries)
    grad_key = weight_grad(tokens, d_keys)
    grad_value = weight_grad(tokens, d_values)
    grad_bvalue = column_sum(d_values)
    d_tokens = (
        d_first
        + back_project(d_queries, w_query)
        + back_project(d_keys, w_key)
        + back_project(d_values, w_value)
    )
    summed = (
        lax.psum_scatter(grad_query, "dp", scatter_dimension=0, tiled=True),
        lax.psum_scatter(grad_bquery, "dp", scatter_dimension=0, tiled=True),
        lax.psum_scatter(grad_key, "dp", scatter_dimension=0, tiled=True),
        lax.psum_scatter(grad_value, "dp", scatter_dimension=0, tiled=True),
        lax.psum_scatter(grad_bvalue, "dp", scatter_dimension=0, tiled=True),
        lax.psum_scatter(grad_out, "dp", scatter_dimension=0, tiled=True),
        lax.psum_scatter(grad_bout, "dp", scatter_dimension=0, tiled=True),
        lax.psum_scatter(grad_gain_attn, "dp", scatter_dimension=0, tiled=True),
        lax.psum_scatter(grad_shift_attn, "dp", scatter_dimension=0, tiled=True),
        lax.psum_scatter(grad_up, "dp", scatter_dimension=0, tiled=True),
        lax.psum_scatter(grad_bup, "dp", scatter_dimension=0, tiled=True),
        lax.psum_scatter(grad_down, "dp", scatter_dimension=0, tiled=True),
        lax.psum_scatter(grad_bdown, "dp", scatter_dimension=0, tiled=True),
        lax.psum_scatter(grad_gain_ffn, "dp", scatter_dimension=0, tiled=True),
        lax.psum_scatter(grad_shift_ffn, "dp", scatter_dimension=0, tiled=True),
    )
    summed = tuple(
        (
            lax.psum(summed[0].astype(jnp.bfloat16), "sp").astype(jnp.float32),
            lax.psum(summed[1].astype(jnp.bfloat16), "sp").astype(jnp.float32),
            lax.psum(summed[2].astype(jnp.bfloat16), "sp").astype(jnp.float32),
            lax.psum(summed[3].astype(jnp.bfloat16), "sp").astype(jnp.float32),
            lax.psum(summed[4].astype(jnp.bfloat16), "sp").astype(jnp.float32),
            lax.psum(summed[5].astype(jnp.bfloat16), "sp").astype(jnp.float32),
            lax.psum(summed[6].astype(jnp.bfloat16), "sp").astype(jnp.float32),
            lax.psum(summed[7].astype(jnp.bfloat16), "sp").astype(jnp.float32),
            lax.psum(summed[8].astype(jnp.bfloat16), "sp").astype(jnp.float32),
            lax.psum(summed[9].astype(jnp.bfloat16), "sp").astype(jnp.float32),
            lax.psum(summed[10].astype(jnp.bfloat16), "sp").astype(jnp.float32),
            lax.psum(summed[11].astype(jnp.bfloat16), "sp").astype(jnp.float32),
            lax.psum(summed[12].astype(jnp.bfloat16), "sp").astype(jnp.float32),
            lax.psum(summed[13].astype(jnp.bfloat16), "sp").astype(jnp.float32),
            lax.psum(summed[14].astype(jnp.bfloat16), "sp").astype(jnp.float32),
        )
    )
    return (
        mixed.astype(jnp.bfloat16),
        d_tokens.astype(jnp.bfloat16),
        summed[0],
        summed[1],
        summed[2],
        summed[3],
        summed[4],
        summed[5],
        summed[6],
        summed[7],
        summed[8],
        summed[9],
        summed[10],
        summed[11],
        summed[12],
        summed[13],
        summed[14],
    )


def solution(mesh):
    placed = (
        P("sp", "dp", None),
        P("dp"),
        P(),
        P(),
        P(),
        P(),
        P(),
        P(),
        P(),
        P(),
        P(),
        P(),
        P(),
        P(),
        P(),
        P(),
        P(),
        P("sp", "dp", None),
    )
    fits = mesh.shape["dp"] == 8 and mesh.shape["sp"] == 4
    return jax.shard_map(
        fused if fits else shards,
        mesh=mesh,
        in_specs=placed,
        out_specs=(
            P("sp", "dp", None),
            P("sp", "dp", None),
            P("dp", None),
            P("dp"),
            P("dp", None),
            P("dp", None),
            P("dp"),
            P("dp", None),
            P("dp"),
            P("dp"),
            P("dp"),
            P("dp", None),
            P("dp"),
            P("dp", None),
            P("dp"),
            P("dp"),
            P("dp"),
        ),
        check_vma=False,
    )
```

```python
import functools

import jax
import jax.numpy as jnp
from jax import lax
from jax.experimental import pallas as pl
from jax.experimental.pallas import tpu as pltpu
from jax.sharding import PartitionSpec as P

HEADS = 12
HD = 64
EPS = 1e-05
MESH_ID = pl.DeviceIdType.MESH
BF = jnp.bfloat16
F32 = jnp.float32


def nn(left, right):
    return jnp.dot(left, right, preferred_element_type=F32)


def nt(left, right):
    return lax.dot_general(left, right, (((1,), (1,)), ((), ())), preferred_element_type=F32)


def tn(left, right):
    return lax.dot_general(left, right, (((0,), (0,)), ((), ())), preferred_element_type=F32)


def aligned(start, step=128):
    return pl.multiple_of(start, step)


UNITS = (
    ("d", 0, 0, 256), ("d", 0, 256, 256), ("d", 0, 512, 256), ("d", 1, 0, 256), ("d", 1, 256, 256),
    ("d", 1, 512, 256), ("d", 2, 0, 256), ("d", 2, 256, 256), ("d", 2, 512, 256), ("u", 0, 0, 1024),
    ("u", 1, 0, 1024), ("u", 2, 0, 1024), ("o",), ("p", 0, 3, 0), ("p", 0, 3, 1), ("p", 0, 1, 2), ("p", 1, 1, 2),
    ("p", 2, 1, 2),
)
PATH = (
    "c0y12", "c1y02", "c120Y", "c1y02", "c120Y", "c012Y", "c0y12", "c012Y", "cy120", "c012Y", "cy120", "cy012",
    "c012Y", "c012Y", "c012Y", "cy012", "c0y12", "c012Y",
)
ORDER = (
    "M", 0, 1, 2, 3, 0, 1, 4, 5, 2, "X", 3, "I0", 4, 5, 6, 7, 8, "I1", 0, 1, 6, "I2", 7, 8, "H0", 5, 2, 9, "H1", 0,
    10, 6, 3, 1, 9, "H2", 11, 7, 10, 4, 8, 1, 5, 6, "F", 11, 3, 2, 0, "A", 12, 7, "B0", 4, "B1", 8, 12, 1, 9, 5, 6, 3,
    0, 13, 2, 7, 4, "B2", 10, 8, 13, "B3", 14, "B4", 9, 6, 3, 12, 14, 8, "B5", 11, "T", "K", 10, 5, 2, 15, 16, 7, 17,
    "V0", 4, 9, 13, 15, 16, 17, "V1", 12, 10, 14, 13, 12, 11, 14, 9, 16, 13, 15, 17, "V2", 11, 12, 10, 16, 14, 15, 17,
    13, "V3", 11, 16, 15, 17, 14, "V4", 16, 15, 17, "V5",
)
VEC_PATH = "c012y"
ROWS_VEC = 16
CHUNK = 1024
ATTEND = 3


def unit_dims(unit, rows, width):
    kind = unit[0]
    if kind == "d":
        return None, unit[3], 128
    if kind == "u":
        return None, rows, unit[3]
    if kind == "o":
        return None, rows, width
    return unit[2], rows, 256


def land_shape(unit, path, stage, rows, width):
    many, r, c = unit_dims(unit, rows, width)
    lead = [2, 2, 2]
    for kind in path[: stage + 1]:
        if kind == "c" and unit[0] != "d":
            c //= 2
        elif kind in "cy":
            r //= 2
        elif kind != "Y":
            lead[2 - int(kind)] = 0
    return (() if many is None else (many,)) + tuple(n for n in lead if n) + (r, c)


def gelu_parts(x):
    cdf = 0.5 + 0.5 * lax.erf(x * (0.5**0.5))
    pdf = jnp.exp(-0.5 * x * x) * 0.3989422804014327
    return x * cdf, cdf + x * pdf


def layer_kernel(*refs):
    it = iter(refs)
    len_ref = next(it)
    bias_refs = [next(it) for _ in range(9)]
    (tok_ref, cot_ref, wq_ref, wk_ref, wv_ref, wo_ref, wu_ref, wd_ref) = (next(it) for _ in range(8))
    (mix_out, dtok_out, go_out, gp_out, gu_out, gd_out, gv_out) = (next(it) for _ in range(7))
    (raw_s, tokp, cotp, x_s, cot_s, x_t, hl_t, df_t) = (next(it) for _ in range(8))
    (wa, wu, wd, gd_s, q_s, k_s, v_s, p_s, att_s, linv_s, xh_s, rs_s, hl_s, act_s, gp_s, acc_s, km_s, vec_s) = (
        next(it) for _ in range(18)
    )
    vs, vl = next(it), next(it)
    lands = [[next(it) for _ in path] for path in PATH]
    (wsem, lsem, asend, arecv, usend, urecv, vsend, vrecv) = (next(it) for _ in range(8))

    rows_loc, width = tok_ref.shape[0], tok_ref.shape[2]
    total = rows_loc * 4
    half = total // 2
    rows = width // 8
    dp, sp = lax.axis_index("dp"), lax.axis_index("sp")
    bits = [lax.rem(lax.div(dp, 2**k), 2) for k in range(3)]
    core, ybit = lax.rem(sp, 2), lax.div(sp, 2)

    def sp_xor(k):
        low, high = core, ybit
        if k & 1:
            low = 1 - low
        if k & 2:
            high = 1 - high
        return high * 2 + low

    def peer(kind):
        if kind == "c":
            return (dp, sp_xor(1))
        if kind in "yY":
            return (dp, sp_xor(2))
        k = int(kind)
        return (dp + 2**k * (1 - 2 * bits[k]), sp)

    barrier = pltpu.get_barrier_semaphore()
    greet = [(dp, sp_xor(k)) for k in (1, 2, 3)] + [peer(k) for k in "012"]
    for other in greet:
        pl.semaphore_signal(barrier, inc=1, device_id=other, device_id_type=MESH_ID)

    loads = []

    def load(src, dst):
        copy = pltpu.make_async_copy(src, dst, wsem.at[len(loads)])
        copy.start()
        loads.append(copy)
        return copy

    tok_load = load(tok_ref, raw_s)
    attn_loads = [load(ref, wa.at[i]) for i, ref in enumerate((wq_ref, wk_ref, wv_ref, wo_ref))]

    def exchange(src, dst, base):
        copies = []
        for k in (2, 3, 1):
            other = sp_xor(k)
            copy = pltpu.make_async_remote_copy(
                src_ref=src.at[other],
                dst_ref=dst.at[pl.ds(aligned(sp * rows_loc), rows_loc)],
                send_sem=asend.at[base + k - 1],
                recv_sem=arecv.at[base + k - 1],
                device_id=(dp, other),
                device_id_type=MESH_ID,
            )
            copy.start()
            copies.append(copy)
        dst[pl.ds(aligned(sp * rows_loc), rows_loc), :] = src[sp]
        return copies

    tok_load.wait()
    tokp[...] = jnp.swapaxes(raw_s[...], 0, 1)
    cot_load = load(cot_ref, raw_s)
    pl.semaphore_wait(barrier, len(greet))
    tok_copies = exchange(tokp, x_s, 0)
    up_loads = [
        [load(wu_ref.at[:, :, :, :, pl.ds(384 * r + 128 * j, 128)], wu.at[j, :, :, :, :, pl.ds(128 * r, 128)]) for r in range(8)]
        for j in range(3)
    ]
    down_loads = [load(wd_ref.at[:, :, :, j], wd.at[j]) for j in range(3)]

    for i in range(8):
        vec_s[pl.ds(i, 1), pl.ds(0, width)] = bias_refs[i][...].astype(F32).reshape(1, width)
    for j in range(3):
        for r in range(8):
            part = bias_refs[8][pl.ds(384 * r + 128 * j, 128)]
            vec_s[pl.ds(10 + j, 1), pl.ds(128 * r, 128)] = part.astype(F32).reshape(1, 128)

    state = [dict(stage=0, copies=[]) for _ in UNITS]

    def region(unit, kinds, last_other=False):
        kind = unit[0]
        many, r, c = unit_dims(unit, rows, width)
        r0, c0 = (unit[2] if kind == "d" else 0), (256 * unit[3] if kind == "p" else unit[2] if kind == "u" else 0)
        lead = [slice(None)] * 3
        for i, step in enumerate(kinds):
            flip = last_other and i == len(kinds) - 1
            if step == "c":
                at = 1 - core if flip else core
                if kind == "d":
                    r //= 2
                    r0 = r0 + at * r
                else:
                    c //= 2
                    c0 = c0 + at * c
            elif step == "y":
                r //= 2
                r0 = r0 + (1 - ybit if flip else ybit) * r
            elif step != "Y":
                b = bits[int(step)]
                lead[2 - int(step)] = 1 - b if flip else b
        span = (pl.ds(r0 if isinstance(r0, int) else aligned(r0, 16), r), pl.ds(c0 if isinstance(c0, int) else aligned(c0), c))
        if kind == "d":
            return gd_s, (unit[1], *lead, *span)
        if kind == "u":
            return wu, (unit[1], *lead, *span)
        if kind == "o":
            return wa, (3, *lead, *span)
        return wd, (pl.ds(unit[1], many), *lead, *span)

    def out_region(unit, path):
        ref, at = region(unit, path)
        kind = unit[0]
        if kind == "d":
            return gd_out.at[unit[1], at[4], at[5]]
        if kind == "u":
            return gu_out.at[unit[1], at[4], at[5]]
        if kind == "o":
            return go_out.at[at[4], at[5]]
        return gp_out.at[at[0], at[4], at[5]]

    def send(n, stage, src, dst, to):
        copy = pltpu.make_async_remote_copy(
            src_ref=src,
            dst_ref=dst,
            send_sem=usend.at[n, stage],
            recv_sem=urecv.at[n, stage],
            device_id=to,
            device_id_type=MESH_ID,
        )
        copy.start()
        state[n]["copies"].append(copy)

    def advance(n):
        unit, path = UNITS[n], PATH[n]
        stage = state[n]["stage"]
        state[n]["stage"] += 1
        if stage > 0:
            state[n]["copies"][stage - 1].wait_recv()
            ref, at = region(unit, path[:stage])
            if path[stage - 1] == "Y":
                lands[n][stage - 1][...] = ref[at] + lands[n][stage - 1][...]
            else:
                ref[at] = ref[at] + lands[n][stage - 1][...]
        if stage < len(path):
            ref, at = region(unit, path[: stage + 1], last_other=True)
            send(n, stage, ref.at[at], lands[n][stage], peer(path[stage]))
            return
        dst = out_region(unit, path)
        if "Y" in path:
            src = lands[n][-1]
            send(n, stage, src, dst, peer("c"))
        else:
            ref, at = region(unit, path)
            src = ref.at[at]
            for k in (1, 2, 3):
                send(n, stage + k - 1, src, dst, (dp, sp_xor(k)))
        local = pltpu.make_async_copy(src, dst, lsem.at[n])
        local.start()
        state[n]["local"] = local

    def finish(n):
        for copy in state[n]["copies"][len(PATH[n]) :]:
            copy.wait_recv()
        for copy in state[n]["copies"]:
            copy.wait_send()
        state[n]["local"].wait()

    def vec(row):
        return vec_s[pl.ds(row, 1), pl.ds(0, width)]

    def put_vec(row, value):
        vs[0, pl.ds(row, 1), pl.ds(0, value.shape[1])] = value

    vs[0] = jnp.zeros(vs.shape[1:], F32)
    length = len_ref[sp]
    dead = lax.broadcasted_iota(jnp.int32, (total, 128), 0) >= length
    km_s[...] = jnp.where(dead, -1e30, 0.0).astype(BF)
    ones = jnp.ones((16, total), BF)
    for ref in (x_t, hl_t, df_t):
        ref[pl.ds(width, 16), :] = ones

    def qkv(start):
        x = x_s[pl.ds(start, half), :]
        for w, (dst, row) in enumerate(((q_s, 0), (k_s, None), (v_s, 1))):
            r = nn(x, wa[w].reshape(width, width))
            if row is not None:
                r = r + vec(row)
            if w == 0:
                r = r * HD ** (-0.5)
            dst[pl.ds(start, half), :] = r.astype(BF)

    for copy in attn_loads[:3]:
        copy.wait()
    tok_copies[2].wait_recv()
    qkv(aligned(ybit * half))
    cot_load.wait()
    cotp[...] = jnp.swapaxes(raw_s[...], 0, 1)
    tok_copies[0].wait_recv()
    tok_copies[1].wait_recv()
    cot_copies = exchange(cotp, cot_s, 3)
    qkv(aligned((1 - ybit) * half))

    lane = lax.broadcasted_iota(jnp.int32, (total, 128), 1)
    low = lane < HD
    zeros = jnp.zeros((total, 128), BF)
    ones2 = jnp.ones((total, 128), BF)

    def attend(g):
        cols = pl.ds(aligned(g * 128), 128)
        q2, k2, v2 = q_s[:, cols], k_s[:, cols], v_s[:, cols]
        outs = []
        for h in range(2):
            mine = low if h == 0 else jnp.logical_not(low)
            qh = jnp.where(mine, q2, jnp.where(lane == HD * (1 - h), ones2, zeros))
            kh = jnp.where(mine, k2, km_s[...])
            vh = jnp.where(mine, v2, ones2)
            s = nt(qh, kh)
            e = jnp.exp(s - jnp.max(s, axis=-1, keepdims=True)).astype(BF)
            p_s[g * 2 + h] = e
            outs.append(nn(e, vh))
        num = jnp.where(low, outs[0], outs[1])
        den = pltpu.roll(jnp.where(low, outs[1], outs[0]), HD, axis=1)
        inv = 1.0 / den
        linv_s[:, cols] = inv.astype(BF)
        att_s[:, cols] = (num * inv).astype(BF)

    def attend_some(i, carry):
        for g in range(ATTEND):
            attend(i * ATTEND + g)
        return carry

    lax.fori_loop(0, HEADS // 2 // ATTEND, attend_some, 0)

    attn_loads[3].wait()

    for i in range(total // 256):
        at = slice(256 * i, 256 * i + 256)
        r = nn(att_s[at, :], wa[3].reshape(width, width)) + vec(2) + x_s[at, :].astype(F32)
        mean = jnp.mean(r, axis=-1, keepdims=True)
        center = r - mean
        rs = lax.rsqrt(jnp.mean(center * center, axis=-1, keepdims=True) + EPS)
        xh = center * rs
        hidden = xh * vec(3) + vec(4)
        rs_s[at, :] = rs
        xh_s[at, :] = xh.astype(BF)
        acc_s[at, :] = hidden
        hl_s[at, :] = hidden.astype(BF)

    for j in range(3):
        for copy in up_loads[j]:
            copy.wait()

    def up(j, carry):
        inner = nn(hl_s[...], wu[j].reshape(width, CHUNK)) + vec_s[pl.ds(10 + j, 1), :]
        value, slope = gelu_parts(inner)
        act_s[j] = value.astype(BF)
        gp_s[j] = slope.astype(BF)
        return carry

    lax.fori_loop(0, 3, up, 0)

    for copy in down_loads:
        copy.wait()

    r = acc_s[...] + vec(5)
    for j in range(3):
        r = r + nn(act_s[j], wd[j].reshape(CHUNK, width))
    acc_s[...] = r

    for copy in cot_copies:
        copy.wait_recv()
    for copy in tok_copies + cot_copies:
        copy.wait_send()

    sums = [jnp.zeros((1, width), F32)] * 3
    for i in range(total // 128):
        at = slice(128 * i, 128 * i + 128)
        r = acc_s[at, :]
        mean = jnp.mean(r, axis=-1, keepdims=True)
        center = r - mean
        rs = lax.rsqrt(jnp.mean(center * center, axis=-1, keepdims=True) + EPS)
        xh = center * rs
        tokp[i] = (xh * vec(6) + vec(7)).astype(BF)
        dy = cot_s[at, :].astype(F32)
        dxh = dy * vec(6)
        d2 = rs * (dxh - jnp.mean(dxh, axis=-1, keepdims=True) - xh * jnp.mean(dxh * xh, axis=-1, keepdims=True))
        acc_s[at, :] = d2
        low2 = d2.astype(BF)
        cot_s[at, :] = low2
        df_t[:width, at] = low2.T
        adds = (
            jnp.sum(dy * xh, axis=0, keepdims=True),
            jnp.sum(dy, axis=0, keepdims=True),
            jnp.sum(low2.astype(F32), axis=0, keepdims=True),
        )
        sums = [c + a for c, a in zip(sums, adds)]
    g_gain, g_shift, g_bdown = sums
    put_vec(6, g_gain)
    put_vec(7, g_shift)
    put_vec(5, g_bdown)

    given = []

    def give_back(src, dst, base):
        for k in (2, 3, 1):
            other = sp_xor(k)
            copy = pltpu.make_async_remote_copy(
                src_ref=src.at[other],
                dst_ref=dst.at[sp],
                send_sem=asend.at[base + k - 1],
                recv_sem=arecv.at[base + k - 1],
                device_id=(dp, other),
                device_id_type=MESH_ID,
            )
            copy.start()
            given.append(copy)
        own = pltpu.make_async_copy(src.at[sp], dst.at[sp], lsem.at[len(UNITS) + base // 3 - 2])
        own.start()
        given.append(own)

    def grad_down(j, first, size):
        r = nn(df_t[first : first + size, :], act_s[j]).astype(BF)
        for i in range(8):
            gd_s[j, i // 4, i // 2 % 2, i % 2, first : first + size, :] = r[:, 128 * i : 128 * i + 128]

    def inner_back(j):
        gp_s[j] = nt(cot_s[...], wd[j].reshape(CHUNK, width)).astype(BF) * gp_s[j]

    def hidden_back(j):
        acc_s[...] += nt(gp_s[j], wu[j].reshape(width, CHUNK))

    def grad_up(j):
        r = nn(hl_t[...], gp_s[j])
        wu[j] = r[:width].astype(BF).reshape(2, 2, 2, rows, CHUNK)
        vs[0, 10 + j : 11 + j, :] = r[width : width + 1]

    def first_back():
        sums = [jnp.zeros((1, width), F32)] * 2
        for i in range(total // 128):
            at = slice(128 * i, 128 * i + 128)
            dy = acc_s[at, :]
            xh = xh_s[at, :].astype(F32)
            dxh = dy * vec(3)
            d1 = rs_s[at, :] * (
                dxh - jnp.mean(dxh, axis=-1, keepdims=True) - xh * jnp.mean(dxh * xh, axis=-1, keepdims=True)
            )
            acc_s[at, :] = d1
            dh_s[at, :] = d1.astype(BF)
            adds = (jnp.sum(dy * xh, axis=0, keepdims=True), jnp.sum(dy, axis=0, keepdims=True))
            sums = [c + a for c, a in zip(sums, adds)]
        put_vec(3, sums[0])
        put_vec(4, sums[1])

    def attended_back():
        d = nt(dh_s[...], wa[3].reshape(width, width))
        da_s[...] = (d * linv_s[...].astype(F32)).astype(BF)

    da_s = linv_s

    def grad_out():
        df_t[:width, :] = att_s[...].T
        r = nn(df_t[...], dh_s[...])
        wa[3] = r[:width].astype(BF).reshape(2, 2, 2, rows, width)
        vs[0, 2:3, :width] = r[width : width + 1]

    def attend_back(g):
        cols = slice(g * 128, g * 128 + 128)
        q2, k2, v2, d2 = q_s[:, cols], k_s[:, cols], v_s[:, cols], da_s[:, cols]
        prod = d2.astype(F32) * att_s[:, cols].astype(F32)
        dqs, dks, dvs = [], [], []
        for h in range(2):
            mine = low if h == 0 else jnp.logical_not(low)
            delta = -jnp.sum(jnp.where(mine, prod, 0.0), axis=-1, keepdims=True)
            upper = delta.astype(BF)
            lower = (delta - upper.astype(F32)).astype(BF)
            other = HD * (1 - h)
            fill = jnp.where(lane == other, upper, jnp.where(lane == other + 1, lower, zeros))
            e = p_s[g * 2 + h]
            ds = e * nt(jnp.where(mine, d2, fill), jnp.where(mine, v2, ones2)).astype(BF)
            dqs.append(nn(ds, k2))
            dks.append(tn(ds, q2))
            dvs.append(tn(e, d2))
        q_s[:, cols] = (jnp.where(low, dqs[0], dqs[1]) * HD ** (-0.5)).astype(BF)
        k_s[:, cols] = jnp.where(low, dks[0], dks[1]).astype(BF)
        v_s[:, cols] = jnp.where(low, dvs[0], dvs[1]).astype(BF)

    def grad_proj(n, first, count):
        cols = slice(256 * n, 256 * n + 256)
        for w, src, row in ((0, q_s, 0), (1, k_s, None), (2, v_s, 1)):
            if first <= w < first + count:
                r = nn(x_t[...], src[:, cols])
                wd[w, :, :, :, :rows, cols] = r[:width].astype(BF).reshape(2, 2, 2, rows, 256)
                if row is not None:
                    vs[0, row : row + 1, cols] = r[width : width + 1]

    def tokens_back():
        r = acc_s[...]
        for w, src in enumerate((q_s, k_s, v_s)):
            r = r + nt(src[...], wa[w].reshape(width, width))
        cotp[...] = r.astype(BF).reshape(4, rows_loc, width)

    vec_copies = []

    def vec_step(i):
        if i == 0:
            vl[0] = vs[0].astype(BF)
        else:
            vec_copies[i - 1].wait_recv()
            vl[i] = vl[i - 1] + vl[i]
        if i < 5:
            copy = pltpu.make_async_remote_copy(
                src_ref=vl.at[i],
                dst_ref=vl.at[i + 1],
                send_sem=vsend.at[i],
                recv_sem=vrecv.at[i],
                device_id=peer(VEC_PATH[i]),
                device_id_type=MESH_ID,
            )
            copy.start()
            vec_copies.append(copy)

    def transpose_tokens():
        x_t[:width, :] = x_s[...].T
        hl_t[:width, :] = hl_s[...].T

    dh_s = hl_s

    made = set()

    def produce(n):
        unit = UNITS[n]
        if unit[0] == "d":
            if unit[1] == 0:
                grad_down(0, unit[2], unit[3])
            elif ("d", unit[1]) not in made:
                grad_down(unit[1], 0, width)
                made.add(("d", unit[1]))
        elif unit[0] == "u":
            if ("u", unit[1]) not in made:
                grad_up(unit[1])
                made.add(("u", unit[1]))
        elif unit[0] == "o":
            grad_out()
        else:
            grad_proj(unit[3], unit[1], unit[2])

    for step in ORDER:
        if isinstance(step, int):
            if state[step]["stage"] == 0:
                produce(step)
            advance(step)
            continue
        name, at = step[0], int(step[1:] or 0)
        if name == "I":
            inner_back(at)
        elif name == "H":
            hidden_back(at)
        elif name == "F":
            first_back()
        elif name == "A":
            attended_back()
        elif name == "B":
            attend_back(at)
        elif name == "T":
            tokens_back()
        elif name == "X":
            transpose_tokens()
        elif name == "M":
            give_back(tokp, mix_out, 6)
        elif name == "K":
            give_back(cotp, dtok_out, 9)
        elif name == "V":
            vec_step(at)
    gv_out[...] = vl[5].astype(F32)
    for n in range(len(UNITS)):
        finish(n)
    for copy in vec_copies:
        copy.wait_send()
    for copy in given:
        copy.wait()


def finish_kernel(*refs):
    it = iter(refs)
    sources = [next(it) for _ in range(7)]
    (o_mix, o_dtok, o_wq, o_bq, o_wk, o_wv, o_bv, o_wo, o_bo, o_ga, o_sa, o_up, o_bup, o_down, o_bdown, o_gf, o_sf) = (
        next(it) for _ in range(17)
    )
    held = [next(it) for _ in range(7)]
    staged = [next(it) for _ in range(5)]
    isem, osem = next(it), next(it)
    loads = [pltpu.make_async_copy(src, dst, isem.at[i]) for i, (src, dst) in enumerate(zip(sources, held))]
    for copy in loads:
        copy.start()
    mix, dtok, go, gp, gu, gd, gv = held
    s_mix, s_dtok, s_sq, s_up, s_down = staged
    width = mix.shape[2]
    rows = width // 8
    dp = lax.axis_index("dp")
    stores = []

    def store(src, dst):
        copy = pltpu.make_async_copy(src, dst, osem.at[len(stores)])
        copy.start()
        stores.append(copy)

    loads[4].wait()
    for j in range(3):
        for r in range(8):
            s_up[:, 384 * r + 128 * j : 384 * r + 128 * j + 128] = gu[j, :, 128 * r : 128 * r + 128].astype(F32)
    store(s_up, o_up)
    loads[5].wait()
    for j in range(3):
        s_down[128 * j : 128 * j + 128, :] = gd[j].astype(F32).T
    store(s_down, o_down)
    loads[3].wait()
    loads[2].wait()
    for w in range(4):
        s_sq[w] = (go[...] if w == 3 else gp[w]).astype(F32)
        store(s_sq.at[w], (o_wq, o_wk, o_wv, o_wo)[w])
    loads[0].wait()
    s_mix[...] = jnp.swapaxes(mix[...], 0, 1)
    store(s_mix, o_mix)
    loads[1].wait()
    s_dtok[...] = jnp.swapaxes(dtok[...], 0, 1)
    store(s_dtok, o_dtok)
    loads[6].wait()
    for j in range(3):
        o_bup[pl.ds(128 * j, 128)] = gv[pl.ds(10 + j, 1), pl.ds(aligned(dp * 128), 128)].reshape(128)
    turned = pltpu.roll(gv[pl.ds(0, 8), pl.ds(0, width)], lax.rem(width - rows * dp, width), axis=1)
    for i, ref in enumerate((o_bq, o_bv, o_bo, o_ga, o_sa, o_bdown, o_gf, o_sf)):
        ref[...] = turned[i : i + 1, :rows].reshape(rows)
    for copy in stores:
        copy.wait()


def fused(
    tokens, lengths, w_query, b_query, w_key, w_value, b_value, w_out, b_out, gain_attn, shift_attn,
    w_up, b_up, w_down, b_down, gain_ffn, shift_ffn, cotangent,
):
    rows_loc, pairs, width = tokens.shape
    total = rows_loc * 4
    rows = width // 8
    square = lambda w: w.reshape(2, 2, 2, rows, w.shape[1])
    args = (
        lengths, b_query, b_value, b_out, gain_attn, shift_attn, b_down, gain_ffn, shift_ffn, b_up, tokens, cotangent,
        square(w_query), square(w_key), square(w_value), square(w_out), square(w_up),
        w_down.reshape(2, 2, 2, 3, 128, width),
    )
    vm = lambda shape, dtype=BF: pltpu.VMEM(shape, dtype)
    full = (total, width)
    swapped = (4, rows_loc, width)
    turned = (width + 16, total)
    scratch = [
        vm((rows_loc, 4, width)), vm(swapped), vm(swapped), vm(full), vm(full), vm(turned), vm(turned), vm(turned),
        vm((4, 2, 2, 2, rows, width)), vm((3, 2, 2, 2, rows, CHUNK)), vm((3, 2, 2, 2, 128, width)),
        vm((3, 2, 2, 2, width, 128)),
        vm(full), vm(full), vm(full), vm((HEADS, total, total)), vm(full), vm(full),
        vm(full), vm((total, 1), F32), vm(full), vm((3, total, CHUNK)), vm((3, total, CHUNK)),
        vm(full, F32), vm((total, 128)), vm((ROWS_VEC, CHUNK), F32),
        vm((1, ROWS_VEC, CHUNK), F32), vm((6, ROWS_VEC, CHUNK)),
    ]
    for unit, path in zip(UNITS, PATH):
        scratch += [vm(land_shape(unit, path, s, rows, width)) for s in range(len(path))]
    dma = pltpu.SemaphoreType.DMA
    count = len(UNITS)
    scratch += [dma((40,)), dma((count + 2,)), dma((12,)), dma((12,)), dma((count, 8)), dma((count, 8)), dma((5,)), dma((5,))]
    anywhere = pl.BlockSpec(memory_space=pl.ANY)
    vmem = pl.BlockSpec(memory_space=pltpu.VMEM)
    got = pl.pallas_call(
        layer_kernel,
        out_shape=(
            jax.ShapeDtypeStruct(swapped, BF),
            jax.ShapeDtypeStruct(swapped, BF),
            jax.ShapeDtypeStruct((rows, width), BF),
            jax.ShapeDtypeStruct((3, rows, width), BF),
            jax.ShapeDtypeStruct((3, rows, CHUNK), BF),
            jax.ShapeDtypeStruct((3, width, 128), BF),
            jax.ShapeDtypeStruct((ROWS_VEC, CHUNK), F32),
        ),
        in_specs=[pl.BlockSpec(memory_space=pltpu.SMEM)] + [vmem] * 9 + [anywhere] * 8,
        out_specs=(anywhere,) * 6 + (vmem,),
        scratch_shapes=scratch,
        compiler_params=pltpu.CompilerParams(collective_id=0, has_side_effects=True, vmem_limit_bytes=63 * 2**20),
    )(*args)
    small = jax.ShapeDtypeStruct((rows,), F32)
    flat = jax.ShapeDtypeStruct((rows, width), F32)
    whole = jax.ShapeDtypeStruct((rows_loc, 4, width), BF)
    return pl.pallas_call(
        finish_kernel,
        out_shape=(
            whole, whole, flat, small, flat, flat, small, flat, small, small, small,
            jax.ShapeDtypeStruct((rows, 3 * CHUNK), F32),
            jax.ShapeDtypeStruct((384,), F32),
            jax.ShapeDtypeStruct((384, width), F32),
            small, small, small,
        ),
        in_specs=[anywhere] * 7,
        out_specs=tuple(anywhere if big else vmem for big in (1, 1, 1, 0, 1, 1, 0, 1, 0, 0, 0, 1, 0, 1, 0, 0, 0)),
        scratch_shapes=[vm(value.shape, value.dtype) for value in got]
        + [
            vm((rows_loc, 4, width)), vm((rows_loc, 4, width)), vm((4, rows, width), F32),
            vm((rows, 3 * CHUNK), F32), vm((384, width), F32), dma((7,)), dma((8,)),
        ],
        compiler_params=pltpu.CompilerParams(vmem_limit_bytes=63 * 2**20),
    )(*got)


def norm_layer(resid, gain, shift):
    center = resid - jnp.mean(resid, axis=-1, keepdims=True)
    spread = jnp.mean(center * center, axis=-1, keepdims=True)
    return center * lax.rsqrt(spread + 1e-05) * gain + shift


def exact_gelu(value):
    return jax.nn.gelu(value, approximate=False)


def project(left, weight):
    return jnp.einsum("spd,de->spe", left, weight, preferred_element_type=jnp.float32)


def back_project(grad_in, weight):
    return jnp.einsum("spe,de->spd", grad_in, weight, preferred_element_type=jnp.float32)


def weight_grad(left, right):
    return jnp.einsum("spd,spe->de", left, right, preferred_element_type=jnp.float32)


def column_sum(grad_in):
    return jnp.sum(grad_in.astype(jnp.float32), axis=(0, 1))


def shards(
    tokens,
    lengths,
    w_query,
    b_query,
    w_key,
    w_value,
    b_value,
    w_out,
    b_out,
    gain_attn,
    shift_attn,
    w_up,
    b_up,
    w_down,
    b_down,
    gain_ffn,
    shift_ffn,
    cotangent,
):
    local_rows, pair_count, model_width = tokens.shape
    score_scale = HD ** (-0.5)
    total_len = local_rows * lax.axis_size("sp")
    queries = (project(tokens, w_query) + b_query.astype(jnp.float32)).astype(jnp.bfloat16)
    keys_local = project(tokens, w_key).astype(jnp.bfloat16)
    values_local = (project(tokens, w_value) + b_value.astype(jnp.float32)).astype(jnp.bfloat16)
    keys_all, values_all = (
        lax.all_gather(keys_local, "sp", axis=0, tiled=True),
        lax.all_gather(values_local, "sp", axis=0, tiled=True),
    )
    query_heads = queries.reshape(local_rows, pair_count, HEADS, HD)
    key_heads = keys_all.reshape(total_len, pair_count, HEADS, HD)
    value_heads = values_all.reshape(total_len, pair_count, HEADS, HD)
    scores = (
        jnp.einsum("iphe,jphe->phij", query_heads, key_heads, preferred_element_type=jnp.float32)
        * score_scale
    )
    key_valid = jnp.arange(total_len)[None, :] < lengths[:, None]
    scores = jnp.where(key_valid[:, None, None, :], scores, -1e30)
    top_score = jnp.max(scores, axis=-1, keepdims=True)
    expo = jnp.exp(scores - top_score)
    row_total = jnp.sum(expo, axis=-1, keepdims=True)
    weights_full = expo / row_total
    probs = weights_full.astype(jnp.bfloat16)
    attended = jnp.einsum("phij,jphe->iphe", probs, value_heads, preferred_element_type=jnp.float32)
    attended_low = attended.reshape(local_rows, pair_count, model_width).astype(jnp.bfloat16)
    branch = project(attended_low, w_out) + b_out.astype(jnp.float32)
    first_sum = tokens.astype(jnp.float32) + branch
    hidden, first_back = jax.vjp(
        norm_layer, first_sum, gain_attn.astype(jnp.float32), shift_attn.astype(jnp.float32)
    )
    hidden_low = hidden.astype(jnp.bfloat16)
    inner = project(hidden_low, w_up) + b_up.astype(jnp.float32)
    activated, gelu_back = jax.vjp(exact_gelu, inner)
    activated_low = activated.astype(jnp.bfloat16)
    second_sum = hidden + project(activated_low, w_down) + b_down.astype(jnp.float32)
    mixed, second_back = jax.vjp(
        norm_layer, second_sum, gain_ffn.astype(jnp.float32), shift_ffn.astype(jnp.float32)
    )
    d_second, grad_gain_ffn, grad_shift_ffn = second_back(cotangent.astype(jnp.float32))
    d_ffn = d_second.astype(jnp.bfloat16)
    grad_down = weight_grad(activated_low, d_ffn)
    grad_bdown = column_sum(d_ffn)
    d_inner = gelu_back(back_project(d_ffn, w_down))[0].astype(jnp.bfloat16)
    grad_up = weight_grad(hidden_low, d_inner)
    grad_bup = column_sum(d_inner)
    d_hidden = d_second + back_project(d_inner, w_up)
    d_first, grad_gain_attn, grad_shift_attn = first_back(d_hidden)
    d_branch = d_first.astype(jnp.bfloat16)
    grad_out = weight_grad(attended_low, d_branch)
    grad_bout = column_sum(d_branch)
    d_attended = back_project(d_branch, w_out).astype(jnp.bfloat16)
    d_att_heads = d_attended.reshape(local_rows, pair_count, HEADS, HD)
    d_probs = jnp.einsum(
        "iphe,jphe->phij", d_att_heads, value_heads, preferred_element_type=jnp.float32
    )
    row_delta = jnp.sum(weights_full * d_probs, axis=-1, keepdims=True)
    d_scores = weights_full * (d_probs - row_delta)
    d_scores_low = d_scores.astype(jnp.bfloat16)
    d_query_heads = (
        jnp.einsum("phij,jphe->iphe", d_scores_low, key_heads, preferred_element_type=jnp.float32)
        * score_scale
    )
    d_queries = d_query_heads.reshape(local_rows, pair_count, model_width).astype(jnp.bfloat16)
    row_count = local_rows * lax.axis_size("sp")
    key_part = (
        jnp.einsum("phij,iphe->jphe", d_scores_low, query_heads, preferred_element_type=jnp.float32)
        * score_scale
    )
    value_part = jnp.einsum(
        "phij,iphe->jphe", probs, d_att_heads, preferred_element_type=jnp.float32
    )
    key_grads = lax.psum_scatter(
        jnp.concatenate(
            (
                key_part.reshape(row_count, pair_count, model_width),
                value_part.reshape(row_count, pair_count, model_width),
            ),
            axis=2,
        ).astype(jnp.bfloat16),
        "sp",
        scatter_dimension=0,
        tiled=True,
    ).astype(jnp.float32)
    d_keys = key_grads[:, :, :model_width].astype(jnp.bfloat16)
    d_values = key_grads[:, :, model_width:].astype(jnp.bfloat16)
    grad_query = weight_grad(tokens, d_queries)
    grad_bquery = column_sum(d_queries)
    grad_key = weight_grad(tokens, d_keys)
    grad_value = weight_grad(tokens, d_values)
    grad_bvalue = column_sum(d_values)
    d_tokens = (
        d_first
        + back_project(d_queries, w_query)
        + back_project(d_keys, w_key)
        + back_project(d_values, w_value)
    )
    summed = (
        lax.psum_scatter(grad_query, "dp", scatter_dimension=0, tiled=True),
        lax.psum_scatter(grad_bquery, "dp", scatter_dimension=0, tiled=True),
        lax.psum_scatter(grad_key, "dp", scatter_dimension=0, tiled=True),
        lax.psum_scatter(grad_value, "dp", scatter_dimension=0, tiled=True),
        lax.psum_scatter(grad_bvalue, "dp", scatter_dimension=0, tiled=True),
        lax.psum_scatter(grad_out, "dp", scatter_dimension=0, tiled=True),
        lax.psum_scatter(grad_bout, "dp", scatter_dimension=0, tiled=True),
        lax.psum_scatter(grad_gain_attn, "dp", scatter_dimension=0, tiled=True),
        lax.psum_scatter(grad_shift_attn, "dp", scatter_dimension=0, tiled=True),
        lax.psum_scatter(grad_up, "dp", scatter_dimension=0, tiled=True),
        lax.psum_scatter(grad_bup, "dp", scatter_dimension=0, tiled=True),
        lax.psum_scatter(grad_down, "dp", scatter_dimension=0, tiled=True),
        lax.psum_scatter(grad_bdown, "dp", scatter_dimension=0, tiled=True),
        lax.psum_scatter(grad_gain_ffn, "dp", scatter_dimension=0, tiled=True),
        lax.psum_scatter(grad_shift_ffn, "dp", scatter_dimension=0, tiled=True),
    )
    summed = tuple(
        (
            lax.psum(summed[0].astype(jnp.bfloat16), "sp").astype(jnp.float32),
            lax.psum(summed[1].astype(jnp.bfloat16), "sp").astype(jnp.float32),
            lax.psum(summed[2].astype(jnp.bfloat16), "sp").astype(jnp.float32),
            lax.psum(summed[3].astype(jnp.bfloat16), "sp").astype(jnp.float32),
            lax.psum(summed[4].astype(jnp.bfloat16), "sp").astype(jnp.float32),
            lax.psum(summed[5].astype(jnp.bfloat16), "sp").astype(jnp.float32),
            lax.psum(summed[6].astype(jnp.bfloat16), "sp").astype(jnp.float32),
            lax.psum(summed[7].astype(jnp.bfloat16), "sp").astype(jnp.float32),
            lax.psum(summed[8].astype(jnp.bfloat16), "sp").astype(jnp.float32),
            lax.psum(summed[9].astype(jnp.bfloat16), "sp").astype(jnp.float32),
            lax.psum(summed[10].astype(jnp.bfloat16), "sp").astype(jnp.float32),
            lax.psum(summed[11].astype(jnp.bfloat16), "sp").astype(jnp.float32),
            lax.psum(summed[12].astype(jnp.bfloat16), "sp").astype(jnp.float32),
            lax.psum(summed[13].astype(jnp.bfloat16), "sp").astype(jnp.float32),
            lax.psum(summed[14].astype(jnp.bfloat16), "sp").astype(jnp.float32),
        )
    )
    return (
        mixed.astype(jnp.bfloat16),
        d_tokens.astype(jnp.bfloat16),
        summed[0],
        summed[1],
        summed[2],
        summed[3],
        summed[4],
        summed[5],
        summed[6],
        summed[7],
        summed[8],
        summed[9],
        summed[10],
        summed[11],
        summed[12],
        summed[13],
        summed[14],
    )


def solution(mesh):
    placed = (
        P("sp", "dp", None),
        P("dp"),
        P(),
        P(),
        P(),
        P(),
        P(),
        P(),
        P(),
        P(),
        P(),
        P(),
        P(),
        P(),
        P(),
        P(),
        P(),
        P("sp", "dp", None),
    )
    fits = mesh.shape["dp"] == 8 and mesh.shape["sp"] == 4
    return jax.shard_map(
        fused if fits else shards,
        mesh=mesh,
        in_specs=placed,
        out_specs=(
            P("sp", "dp", None),
            P("sp", "dp", None),
            P("dp", None),
            P("dp"),
            P("dp", None),
            P("dp", None),
            P("dp"),
            P("dp", None),
            P("dp"),
            P("dp"),
            P("dp"),
            P("dp", None),
            P("dp"),
            P("dp", None),
            P("dp"),
            P("dp"),
            P("dp"),
        ),
        check_vma=False,
    )
```

```python
import functools

import jax
import jax.numpy as jnp
from jax import lax
from jax.experimental import pallas as pl
from jax.experimental.pallas import tpu as pltpu
from jax.sharding import PartitionSpec as P

HEADS = 12
HD = 64
EPS = 1e-05
MESH_ID = pl.DeviceIdType.MESH
BF = jnp.bfloat16
F32 = jnp.float32


def nn(left, right):
    return jnp.dot(left, right, preferred_element_type=F32)


def nt(left, right):
    return lax.dot_general(left, right, (((1,), (1,)), ((), ())), preferred_element_type=F32)


def tn(left, right):
    return lax.dot_general(left, right, (((0,), (0,)), ((), ())), preferred_element_type=F32)


def aligned(start, step=128):
    return pl.multiple_of(start, step)


UNITS = (
    ("d", 0, 0, 256), ("d", 0, 256, 256), ("d", 0, 512, 256), ("d", 1, 0, 384), ("d", 1, 384, 384), ("d", 2, 0, 384),
    ("d", 2, 384, 384), ("u", 0, 0, 1024), ("u", 1, 0, 1024), ("u", 2, 0, 1024), ("o",), ("p", 0, 3, 0),
    ("p", 0, 1, 1), ("p", 1, 2, 1), ("p", 0, 1, 2), ("p", 1, 1, 2), ("p", 2, 1, 2),
)
PATH = (
    "c102y", "c120Y", "c0y12", "c102y", "c0y12", "cy120", "c01y2", "cy120", "cy012", "c0y12", "c120Y", "c012y",
    "c012y", "c0y12", "c012Y", "c0y12", "c0y12",
)
ORDER = (
    "M", 0, 1, 2, 3, 0, 1, 2, 4, 5, 6, "X", "I0", 3, 4, "I1", 5, 6, 0, 2, "H0", 1, 7, 4, 8, 5, 3, 7, 2, 9, "F", 6, 1,
    8, 4, 0, "A", 9, 5, 2, 10, 3, 1, "B0", 6, 4, 10, 0, 11, 5, 2, "B2", 7, 3, 11, 4, 12, 9, 5, 13, "B4", 12, 13, 10,
    8, "T", "K", 1, 6, 0, 2, 7, 3, 11, 4, 14, 15, 16, "V0", 12, 14, 15, 16, "V1", 9, 5, 10, 13, 6, 11, 12, 8, 7, 9,
    14, 0, 11, 3, 15, 12, 8, 13, 6, 16, 9, "V2", 11, 14, 15, 12, 10, 13, 16, 7, 8, "V3", 9, 14, 15, 11, 12, 16, 13,
    10, 7, "V4", 15, 8, 16, 14, 13, "V5", 15, 16,
)
VEC_PATH = "c012y"
ROWS_VEC = 16
CHUNK = 1024
ATTEND = 6


def unit_dims(unit, rows, width):
    kind = unit[0]
    if kind == "d":
        return None, unit[3], 128
    if kind == "u":
        return None, rows, unit[3]
    if kind == "o":
        return None, rows, width
    return unit[2], rows, 256


def land_shape(unit, path, stage, rows, width):
    many, r, c = unit_dims(unit, rows, width)
    lead = [2, 2, 2]
    for kind in path[: stage + 1]:
        if kind == "c" and unit[0] != "d":
            c //= 2
        elif kind in "cy":
            r //= 2
        elif kind != "Y":
            lead[2 - int(kind)] = 0
    return (() if many is None else (many,)) + tuple(n for n in lead if n) + (r, c)


def gelu_parts(x):
    cdf = 0.5 + 0.5 * lax.erf(x * (0.5**0.5))
    pdf = jnp.exp(-0.5 * x * x) * 0.3989422804014327
    return x * cdf, cdf + x * pdf


def layer_kernel(*refs):
    it = iter(refs)
    len_ref = next(it)
    bias_refs = [next(it) for _ in range(9)]
    (tok_ref, cot_ref, wq_ref, wk_ref, wv_ref, wo_ref, wu_ref, wd_ref) = (next(it) for _ in range(8))
    (mix_out, dtok_out, go_out, gp_out, gu_out, gd_out, gv_out) = (next(it) for _ in range(7))
    (raw_s, tokp, cotp, x_s, cot_s, x_t, hl_t, df_t) = (next(it) for _ in range(8))
    (wa, wu, wd, gd_s, qkv_s, p_s, att_s, linv_s, xh_s, rs_s, hl_s, act_s, gp_s, acc_s, km_s, vec_s) = (
        next(it) for _ in range(16)
    )
    vs, vl = next(it), next(it)
    lands = [[next(it) for _ in path] for path in PATH]
    tails = [next(it) if "y" in path else None for path in PATH]
    (wsem, lsem, asend, arecv, usend, urecv, vsend, vrecv) = (next(it) for _ in range(8))

    rows_loc, width = tok_ref.shape[0], tok_ref.shape[2]
    total = rows_loc * 4
    half = total // 2
    rows = width // 8
    dp, sp = lax.axis_index("dp"), lax.axis_index("sp")
    bits = [lax.rem(lax.div(dp, 2**k), 2) for k in range(3)]
    core, ybit = lax.rem(sp, 2), lax.div(sp, 2)

    def sp_xor(k):
        low, high = core, ybit
        if k & 1:
            low = 1 - low
        if k & 2:
            high = 1 - high
        return high * 2 + low

    def peer(kind):
        if kind == "c":
            return (dp, sp_xor(1))
        if kind in "yY":
            return (dp, sp_xor(2))
        k = int(kind)
        return (dp + 2**k * (1 - 2 * bits[k]), sp)

    barrier = pltpu.get_barrier_semaphore()
    greet = [(dp, sp_xor(k)) for k in (1, 2, 3)] + [peer(k) for k in "012"]
    for other in greet:
        pl.semaphore_signal(barrier, inc=1, device_id=other, device_id_type=MESH_ID)

    loads = []

    def load(src, dst):
        copy = pltpu.make_async_copy(src, dst, wsem.at[len(loads)])
        copy.start()
        loads.append(copy)
        return copy

    quick = rows_loc // 2
    tok_loads = [load(tok_ref.at[pl.ds(i * quick, quick)], raw_s.at[pl.ds(i * quick, quick)]) for i in range(2)]
    attn_loads = [load(ref, wa.at[i]) for i, ref in enumerate((wq_ref, wk_ref, wv_ref, wo_ref))]

    def exchange(src, dst, base, first=0, size=rows_loc):
        copies = []
        for k in (2, 3, 1):
            other = sp_xor(k)
            copy = pltpu.make_async_remote_copy(
                src_ref=src.at[other, pl.ds(first, size)],
                dst_ref=dst.at[pl.ds(aligned(sp * rows_loc + first, size), size)],
                send_sem=asend.at[base + k - 1],
                recv_sem=arecv.at[base + k - 1],
                device_id=(dp, other),
                device_id_type=MESH_ID,
            )
            copy.start()
            copies.append(copy)
        dst[pl.ds(aligned(sp * rows_loc + first, size), size), :] = src[sp, pl.ds(first, size)]
        return copies

    tok_copies = []
    for i in range(2):
        tok_loads[i].wait()
        tokp[:, pl.ds(i * quick, quick)] = jnp.swapaxes(raw_s[pl.ds(i * quick, quick)], 0, 1)
        if i == 0:
            pl.semaphore_wait(barrier, len(greet))
        tok_copies += exchange(tokp, x_s, 12 * i, i * quick, quick)
    cot_load = load(cot_ref, raw_s)
    up_loads = [
        [load(wu_ref.at[:, :, :, :, pl.ds(384 * r + 128 * j, 128)], wu.at[j, :, :, :, :, pl.ds(128 * r, 128)]) for r in range(8)]
        for j in range(3)
    ]
    down_loads = [load(wd_ref.at[:, :, :, j], wd.at[j]) for j in range(3)]

    vec_s[1:2, :] = jnp.zeros((1, CHUNK), F32)
    for i, row in enumerate((0, 2, 3, 4, 5, 6, 7, 8)):
        vec_s[pl.ds(row, 1), pl.ds(0, width)] = bias_refs[i][...].astype(F32).reshape(1, width)
    for j in range(3):
        for r in range(8):
            part = bias_refs[8][pl.ds(384 * r + 128 * j, 128)]
            vec_s[pl.ds(10 + j, 1), pl.ds(128 * r, 128)] = part.astype(F32).reshape(1, 128)

    state = [dict(stage=0, copies=[]) for _ in UNITS]

    def region(unit, kinds, last_other=False, at_y=None):
        kind = unit[0]
        many, r, c = unit_dims(unit, rows, width)
        r0, c0 = (unit[2] if kind == "d" else 0), (256 * unit[3] if kind == "p" else unit[2] if kind == "u" else 0)
        lead = [slice(None)] * 3
        for i, step in enumerate(kinds):
            flip = last_other and i == len(kinds) - 1
            if step == "c":
                at = 1 - core if flip else core
                if kind == "d":
                    r //= 2
                    r0 = r0 + at * r
                else:
                    c //= 2
                    c0 = c0 + at * c
            elif step == "y":
                r //= 2
                r0 = r0 + (1 - ybit if flip else ybit if at_y is None else at_y) * r
            elif step != "Y":
                b = bits[int(step)]
                lead[2 - int(step)] = 1 - b if flip else b
        span = (pl.ds(r0 if isinstance(r0, int) else aligned(r0, 16), r), pl.ds(c0 if isinstance(c0, int) else aligned(c0), c))
        if kind == "d":
            return gd_s, (unit[1], *lead, *span)
        if kind == "u":
            return wu, (unit[1], *lead, *span)
        if kind == "o":
            return wa, (3, *lead, *span)
        return wd, (pl.ds(unit[1], many), *lead, *span)

    def out_region(unit, path, at_y=None):
        ref, at = region(unit, path, at_y=at_y)
        kind = unit[0]
        if kind == "d":
            return gd_out.at[unit[1], at[4], at[5]]
        if kind == "u":
            return gu_out.at[unit[1], at[4], at[5]]
        if kind == "o":
            return go_out.at[at[4], at[5]]
        return gp_out.at[at[0], at[4], at[5]]

    def send(n, stage, src, dst, to):
        copy = pltpu.make_async_remote_copy(
            src_ref=src,
            dst_ref=dst,
            send_sem=usend.at[n, stage],
            recv_sem=urecv.at[n, stage],
            device_id=to,
            device_id_type=MESH_ID,
        )
        copy.start()
        state[n]["copies"].append(copy)

    def advance(n):
        unit, path = UNITS[n], PATH[n]
        stage = state[n]["stage"]
        state[n]["stage"] += 1
        if stage > len(path):
            state[n]["copies"][stage - 1].wait_recv()
            dst = out_region(unit, path, 1 - ybit)
            send(n, stage + 1, tails[n], dst, peer("c"))
            local = pltpu.make_async_copy(tails[n], dst, lsem.at[n, 1])
            local.start()
            state[n]["local"].append(local)
            return
        if stage > 0:
            state[n]["copies"][stage - 1].wait_recv()
            ref, at = region(unit, path[:stage])
            if path[stage - 1] == "Y":
                lands[n][stage - 1][...] = ref[at] + lands[n][stage - 1][...]
            else:
                ref[at] = ref[at] + lands[n][stage - 1][...]
        if stage < len(path):
            ref, at = region(unit, path[: stage + 1], last_other=True)
            send(n, stage, ref.at[at], lands[n][stage], peer(path[stage]))
            return
        dst = out_region(unit, path)
        if "Y" in path:
            src = lands[n][-1]
            send(n, stage, src, dst, peer("c"))
        else:
            ref, at = region(unit, path)
            src = ref.at[at]
            send(n, stage, src, tails[n], peer("y"))
            send(n, stage + 1, src, dst, peer("c"))
        local = pltpu.make_async_copy(src, dst, lsem.at[n, 0])
        local.start()
        state[n]["local"] = [local]

    def finish(n):
        for copy in state[n]["copies"][len(PATH[n]) + ("y" in PATH[n]) :]:
            copy.wait_recv()
        for copy in state[n]["copies"]:
            copy.wait_send()
        for copy in state[n]["local"]:
            copy.wait()

    def vec(row):
        return vec_s[pl.ds(row, 1), pl.ds(0, width)]

    def put_vec(row, value):
        vs[0, pl.ds(row, 1), pl.ds(0, value.shape[1])] = value

    vs[0] = jnp.zeros(vs.shape[1:], F32)
    length = len_ref[sp]
    dead = lax.broadcasted_iota(jnp.int32, (total, 128), 0) >= length
    km_s[...] = jnp.where(dead, -1e30, 0.0).astype(BF)
    ones = jnp.ones((16, total), BF)
    for ref in (x_t, hl_t, df_t):
        ref[pl.ds(width, 16), :] = ones

    def qkv(start):
        def one(w, carry):
            r = nn(x_s[pl.ds(start, half), :], wa[w].reshape(width, width)) + vec_s[pl.ds(w, 1), pl.ds(0, width)]
            r = r * jnp.where(w == 0, HD ** (-0.5), 1.0)
            qkv_s[w, pl.ds(start, half), :] = r.astype(BF)
            return carry

        lax.fori_loop(0, 3, one, 0)

    for copy in attn_loads[:3]:
        copy.wait()
    for i in (2, 5):
        tok_copies[i].wait_recv()
    qkv(aligned(ybit * half))
    cot_load.wait()
    cotp[...] = jnp.swapaxes(raw_s[...], 0, 1)
    for i in (0, 1, 3, 4):
        tok_copies[i].wait_recv()
    cot_copies = exchange(cotp, cot_s, 3)
    qkv(aligned((1 - ybit) * half))

    lane = lax.broadcasted_iota(jnp.int32, (total, 128), 1)
    low = lane < HD
    zeros = jnp.zeros((total, 128), BF)
    ones2 = jnp.ones((total, 128), BF)

    def attend(g):
        cols = pl.ds(aligned(g * 128), 128)
        q2, k2, v2 = qkv_s[0, :, cols], qkv_s[1, :, cols], qkv_s[2, :, cols]
        outs = []
        for h in range(2):
            mine = low if h == 0 else jnp.logical_not(low)
            qh = jnp.where(mine, q2, jnp.where(lane == HD * (1 - h), ones2, zeros))
            kh = jnp.where(mine, k2, km_s[...])
            vh = jnp.where(mine, v2, ones2)
            s = nt(qh, kh)
            e = jnp.exp(s - jnp.max(s, axis=-1, keepdims=True)).astype(BF)
            p_s[g * 2 + h] = e
            outs.append(nn(e, vh))
        num = jnp.where(low, outs[0], outs[1])
        den = pltpu.roll(jnp.where(low, outs[1], outs[0]), HD, axis=1)
        inv = 1.0 / den
        linv_s[:, cols] = inv.astype(BF)
        att_s[:, cols] = (num * inv).astype(BF)

    def attend_some(i, carry):
        for g in range(ATTEND):
            attend(i * ATTEND + g)
        return carry

    lax.fori_loop(0, HEADS // 2 // ATTEND, attend_some, 0)

    attn_loads[3].wait()

    def first_norm(i, carry):
        at = pl.ds(aligned(256 * i, 256), 256)
        r = nn(att_s[at, :], wa[3].reshape(width, width)) + vec(3) + x_s[at, :].astype(F32)
        mean = jnp.mean(r, axis=-1, keepdims=True)
        center = r - mean
        rs = lax.rsqrt(jnp.mean(center * center, axis=-1, keepdims=True) + EPS)
        xh = center * rs
        hidden = xh * vec(4) + vec(5)
        rs_s[at, :] = rs
        xh_s[at, :] = xh.astype(BF)
        acc_s[at, :] = hidden
        hl_s[at, :] = hidden.astype(BF)
        return carry

    lax.fori_loop(0, total // 256, first_norm, 0)

    for j in range(3):
        for copy in up_loads[j]:
            copy.wait()

    def up(j, carry):
        inner = nn(hl_s[...], wu[j].reshape(width, CHUNK)) + vec_s[pl.ds(10 + j, 1), :]
        value, slope = gelu_parts(inner)
        act_s[j] = value.astype(BF)
        gp_s[j] = slope.astype(BF)
        return carry

    lax.fori_loop(0, 3, up, 0)

    for copy in down_loads:
        copy.wait()

    def down(i, carry):
        cols = pl.ds(aligned(i * 256), 256)
        r = acc_s[:, cols] + vec_s[pl.ds(6, 1), cols]
        for j in range(3):
            r = r + nn(act_s[j], wd[j, :, :, :, :, cols].reshape(CHUNK, 256))
        acc_s[:, cols] = r
        return carry

    lax.fori_loop(0, width // 256, down, 0)

    for copy in cot_copies:
        copy.wait_recv()
    for copy in tok_copies + cot_copies:
        copy.wait_send()

    def second_norm(i, carry):
        at = pl.ds(aligned(128 * i, 128), 128)
        r = acc_s[at, :]
        mean = jnp.mean(r, axis=-1, keepdims=True)
        center = r - mean
        rs = lax.rsqrt(jnp.mean(center * center, axis=-1, keepdims=True) + EPS)
        xh = center * rs
        tokp[i] = (xh * vec(7) + vec(8)).astype(BF)
        dy = cot_s[at, :].astype(F32)
        dxh = dy * vec(7)
        d2 = rs * (dxh - jnp.mean(dxh, axis=-1, keepdims=True) - xh * jnp.mean(dxh * xh, axis=-1, keepdims=True))
        acc_s[at, :] = d2
        low2 = d2.astype(BF)
        cot_s[at, :] = low2
        df_t[:width, at] = low2.T
        adds = (
            jnp.sum(dy * xh, axis=0, keepdims=True),
            jnp.sum(dy, axis=0, keepdims=True),
            jnp.sum(low2.astype(F32), axis=0, keepdims=True),
        )
        return tuple(c + a for c, a in zip(carry, adds))

    zero = jnp.zeros((1, width), F32)
    g_gain, g_shift, g_bdown = lax.fori_loop(0, total // 128, second_norm, (zero, zero, zero))
    put_vec(6, g_gain)
    put_vec(7, g_shift)
    put_vec(5, g_bdown)

    given = []

    def give_back(src, dst, base):
        for k in (2, 3, 1):
            other = sp_xor(k)
            copy = pltpu.make_async_remote_copy(
                src_ref=src.at[other],
                dst_ref=dst.at[sp],
                send_sem=asend.at[base + k - 1],
                recv_sem=arecv.at[base + k - 1],
                device_id=(dp, other),
                device_id_type=MESH_ID,
            )
            copy.start()
            given.append(copy)
        own = pltpu.make_async_copy(src.at[sp], dst.at[sp], lsem.at[len(UNITS) + base // 3 - 2, 0])
        own.start()
        given.append(own)

    def grad_down(j, first, size):
        r = nn(df_t[pl.ds(first, size), :], act_s[j]).astype(BF)
        for k in range(8):
            gd_s[j, k // 4, k // 2 % 2, k % 2, pl.ds(first, size), :] = r[:, 128 * k : 128 * k + 128]

    def inner_back(first, count):
        def body(j, carry):
            gp_s[j] = nt(cot_s[...], wd[j].reshape(CHUNK, width)).astype(BF) * gp_s[j]
            return carry

        lax.fori_loop(first, first + count, body, 0)

    def hidden_back(first, count):
        def body(j, carry):
            acc_s[...] += nt(gp_s[j], wu[j].reshape(width, CHUNK))
            return carry

        lax.fori_loop(first, first + count, body, 0)

    def grad_up(first, count):
        def body(j, carry):
            r = nn(hl_t[...], gp_s[j])
            wu[j] = r[:width].astype(BF).reshape(2, 2, 2, rows, CHUNK)
            vs[0, pl.ds(10 + j, 1), :] = r[width : width + 1]
            return carry

        lax.fori_loop(first, first + count, body, 0)

    def first_back():
        def body(i, carry):
            at = pl.ds(aligned(128 * i, 128), 128)
            dy = acc_s[at, :]
            xh = xh_s[at, :].astype(F32)
            dxh = dy * vec(4)
            d1 = rs_s[at, :] * (
                dxh - jnp.mean(dxh, axis=-1, keepdims=True) - xh * jnp.mean(dxh * xh, axis=-1, keepdims=True)
            )
            acc_s[at, :] = d1
            dh_s[at, :] = d1.astype(BF)
            adds = (jnp.sum(dy * xh, axis=0, keepdims=True), jnp.sum(dy, axis=0, keepdims=True))
            return tuple(c + a for c, a in zip(carry, adds))

        g_gain, g_shift = lax.fori_loop(0, total // 128, body, (zero, zero))
        put_vec(3, g_gain)
        put_vec(4, g_shift)

    def attended_back():
        d = nt(dh_s[...], wa[3].reshape(width, width))
        da_s[...] = (d * linv_s[...].astype(F32)).astype(BF)

    da_s = linv_s

    def grad_out():
        df_t[:width, :] = att_s[...].T
        r = nn(df_t[...], dh_s[...])
        wa[3] = r[:width].astype(BF).reshape(2, 2, 2, rows, width)
        vs[0, 2:3, :width] = r[width : width + 1]

    def attend_back(g):
        cols = slice(g * 128, g * 128 + 128)
        q2, k2, v2, d2 = qkv_s[0, :, cols], qkv_s[1, :, cols], qkv_s[2, :, cols], da_s[:, cols]
        prod = d2.astype(F32) * att_s[:, cols].astype(F32)
        dqs, dks, dvs = [], [], []
        for h in range(2):
            mine = low if h == 0 else jnp.logical_not(low)
            delta = -jnp.sum(jnp.where(mine, prod, 0.0), axis=-1, keepdims=True)
            upper = delta.astype(BF)
            lower = (delta - upper.astype(F32)).astype(BF)
            other = HD * (1 - h)
            fill = jnp.where(lane == other, upper, jnp.where(lane == other + 1, lower, zeros))
            e = p_s[g * 2 + h]
            ds = e * nt(jnp.where(mine, d2, fill), jnp.where(mine, v2, ones2)).astype(BF)
            dqs.append(nn(ds, k2))
            dks.append(tn(ds, q2))
            dvs.append(tn(e, d2))
        qkv_s[0, :, cols] = (jnp.where(low, dqs[0], dqs[1]) * HD ** (-0.5)).astype(BF)
        qkv_s[1, :, cols] = jnp.where(low, dks[0], dks[1]).astype(BF)
        qkv_s[2, :, cols] = jnp.where(low, dvs[0], dvs[1]).astype(BF)

    def grad_proj(n):
        cols = slice(256 * n, 256 * n + 256)

        def body(w, carry):
            r = nn(x_t[...], qkv_s[w, :, cols])
            wd[w, :, :, :, :rows, cols] = r[:width].astype(BF).reshape(2, 2, 2, rows, 256)
            vs[0, pl.ds(lax.rem(w * 14, 27), 1), cols] = r[width : width + 1]
            return carry

        lax.fori_loop(0, 3, body, 0)

    def tokens_back():
        def body(w, carry):
            acc_s[...] += nt(qkv_s[w], wa[w].reshape(width, width))
            return carry

        lax.fori_loop(0, 3, body, 0)
        cotp[...] = acc_s[...].astype(BF).reshape(4, rows_loc, width)

    vec_copies = []

    def vec_step(i):
        if i == 0:
            vl[0] = vs[0].astype(BF)
        else:
            vec_copies[i - 1].wait_recv()
            vl[i] = vl[i - 1] + vl[i]
        if i < 5:
            copy = pltpu.make_async_remote_copy(
                src_ref=vl.at[i],
                dst_ref=vl.at[i + 1],
                send_sem=vsend.at[i],
                recv_sem=vrecv.at[i],
                device_id=peer(VEC_PATH[i]),
                device_id_type=MESH_ID,
            )
            copy.start()
            vec_copies.append(copy)

    def transpose_tokens():
        x_t[:width, :] = x_s[...].T
        hl_t[:width, :] = hl_s[...].T

    dh_s = hl_s

    made = set()

    def produce(n):
        unit = UNITS[n]
        if unit[0] == "d" and unit[1] == 0:
            grad_down(0, unit[2], unit[3])
            return
        key = (unit[0], unit[3]) if unit[0] == "p" else (unit[0], min(unit[1], 1)) if unit[0] in "du" else unit
        if key in made:
            return
        made.add(key)
        if key == ("d", 1):

            def both(j, carry):
                grad_down(j, 0, width)
                return carry

            lax.fori_loop(1, 3, both, 0)
        elif key[0] == "u":
            grad_up(key[1], 1 + key[1])
        elif key[0] == "o":
            grad_out()
        else:
            grad_proj(unit[3])

    for step in ORDER:
        if isinstance(step, int):
            if state[step]["stage"] == 0:
                produce(step)
            advance(step)
            continue
        name, at = step[0], int(step[1:] or 0)
        if name == "I":
            inner_back(at, 1 + at)
        elif name == "H":
            hidden_back(at, 3)
        elif name == "F":
            first_back()
        elif name == "A":
            attended_back()
        elif name == "B":
            attend_back(at)
            attend_back(at + 1)
        elif name == "T":
            tokens_back()
        elif name == "X":
            transpose_tokens()
        elif name == "M":
            give_back(tokp, mix_out, 6)
        elif name == "K":
            give_back(cotp, dtok_out, 9)
        elif name == "V":
            vec_step(at)
    gv_out[...] = vl[5].astype(F32)
    for n in range(len(UNITS)):
        finish(n)
    for copy in vec_copies:
        copy.wait_send()
    for copy in given:
        copy.wait()


def finish_kernel(*refs):
    it = iter(refs)
    sources = [next(it) for _ in range(7)]
    (o_mix, o_dtok, o_wq, o_bq, o_wk, o_wv, o_bv, o_wo, o_bo, o_ga, o_sa, o_up, o_bup, o_down, o_bdown, o_gf, o_sf) = (
        next(it) for _ in range(17)
    )
    held = [next(it) for _ in range(7)]
    staged = [next(it) for _ in range(5)]
    isem, osem = next(it), next(it)
    loads = [pltpu.make_async_copy(src, dst, isem.at[i]) for i, (src, dst) in enumerate(zip(sources, held))]
    for copy in loads:
        copy.start()
    mix, dtok, go, gp, gu, gd, gv = held
    s_mix, s_dtok, s_sq, s_up, s_down = staged
    width = mix.shape[2]
    rows = width // 8
    dp = lax.axis_index("dp")
    stores = []

    def store(src, dst):
        copy = pltpu.make_async_copy(src, dst, osem.at[len(stores)])
        copy.start()
        stores.append(copy)

    loads[4].wait()
    for j in range(3):
        for r in range(8):
            s_up[:, 384 * r + 128 * j : 384 * r + 128 * j + 128] = gu[j, :, 128 * r : 128 * r + 128].astype(F32)
    store(s_up, o_up)
    loads[5].wait()
    for j in range(3):
        s_down[128 * j : 128 * j + 128, :] = gd[j].astype(F32).T
    store(s_down, o_down)
    loads[3].wait()
    loads[2].wait()
    for w in range(4):
        s_sq[w] = (go[...] if w == 3 else gp[w]).astype(F32)
        store(s_sq.at[w], (o_wq, o_wk, o_wv, o_wo)[w])
    loads[0].wait()
    s_mix[...] = jnp.swapaxes(mix[...], 0, 1)
    store(s_mix, o_mix)
    loads[1].wait()
    s_dtok[...] = jnp.swapaxes(dtok[...], 0, 1)
    store(s_dtok, o_dtok)
    loads[6].wait()
    for j in range(3):
        o_bup[pl.ds(128 * j, 128)] = gv[pl.ds(10 + j, 1), pl.ds(aligned(dp * 128), 128)].reshape(128)
    turned = pltpu.roll(gv[pl.ds(0, 8), pl.ds(0, width)], lax.rem(width - rows * dp, width), axis=1)
    for i, ref in enumerate((o_bq, o_bv, o_bo, o_ga, o_sa, o_bdown, o_gf, o_sf)):
        ref[...] = turned[i : i + 1, :rows].reshape(rows)
    for copy in stores:
        copy.wait()


def fused(
    tokens, lengths, w_query, b_query, w_key, w_value, b_value, w_out, b_out, gain_attn, shift_attn,
    w_up, b_up, w_down, b_down, gain_ffn, shift_ffn, cotangent,
):
    rows_loc, pairs, width = tokens.shape
    total = rows_loc * 4
    rows = width // 8
    square = lambda w: w.reshape(2, 2, 2, rows, w.shape[1])
    args = (
        lengths, b_query, b_value, b_out, gain_attn, shift_attn, b_down, gain_ffn, shift_ffn, b_up, tokens, cotangent,
        square(w_query), square(w_key), square(w_value), square(w_out), square(w_up),
        w_down.reshape(2, 2, 2, 3, 128, width),
    )
    vm = lambda shape, dtype=BF: pltpu.VMEM(shape, dtype)
    full = (total, width)
    swapped = (4, rows_loc, width)
    turned = (width + 16, total)
    scratch = [
        vm((rows_loc, 4, width)), vm(swapped), vm(swapped), vm(full), vm(full), vm(turned), vm(turned), vm(turned),
        vm((4, 2, 2, 2, rows, width)), vm((3, 2, 2, 2, rows, CHUNK)), vm((3, 2, 2, 2, 128, width)),
        vm((3, 2, 2, 2, width, 128)),
        vm((3, total, width)), vm((HEADS, total, total)), vm(full), vm(full),
        vm(full), vm((total, 1), F32), vm(full), vm((3, total, CHUNK)), vm((3, total, CHUNK)),
        vm(full, F32), vm((total, 128)), vm((ROWS_VEC, CHUNK), F32),
        vm((1, ROWS_VEC, CHUNK), F32), vm((6, ROWS_VEC, CHUNK)),
    ]
    for unit, path in zip(UNITS, PATH):
        scratch += [vm(land_shape(unit, path, s, rows, width)) for s in range(len(path))]
    for unit, path in zip(UNITS, PATH):
        if "y" in path:
            scratch.append(vm(land_shape(unit, path, 4, rows, width)))
    dma = pltpu.SemaphoreType.DMA
    count = len(UNITS)
    scratch += [dma((40,)), dma((count + 2, 2)), dma((15,)), dma((15,)), dma((count, 8)), dma((count, 8)), dma((5,)), dma((5,))]
    anywhere = pl.BlockSpec(memory_space=pl.ANY)
    vmem = pl.BlockSpec(memory_space=pltpu.VMEM)
    got = pl.pallas_call(
        layer_kernel,
        out_shape=(
            jax.ShapeDtypeStruct(swapped, BF),
            jax.ShapeDtypeStruct(swapped, BF),
            jax.ShapeDtypeStruct((rows, width), BF),
            jax.ShapeDtypeStruct((3, rows, width), BF),
            jax.ShapeDtypeStruct((3, rows, CHUNK), BF),
            jax.ShapeDtypeStruct((3, width, 128), BF),
            jax.ShapeDtypeStruct((ROWS_VEC, CHUNK), F32),
        ),
        in_specs=[pl.BlockSpec(memory_space=pltpu.SMEM)] + [vmem] * 9 + [anywhere] * 8,
        out_specs=(anywhere,) * 6 + (vmem,),
        scratch_shapes=scratch,
        compiler_params=pltpu.CompilerParams(collective_id=0, has_side_effects=True, vmem_limit_bytes=63 * 2**20),
    )(*args)
    small = jax.ShapeDtypeStruct((rows,), F32)
    flat = jax.ShapeDtypeStruct((rows, width), F32)
    whole = jax.ShapeDtypeStruct((rows_loc, 4, width), BF)
    return pl.pallas_call(
        finish_kernel,
        out_shape=(
            whole, whole, flat, small, flat, flat, small, flat, small, small, small,
            jax.ShapeDtypeStruct((rows, 3 * CHUNK), F32),
            jax.ShapeDtypeStruct((384,), F32),
            jax.ShapeDtypeStruct((384, width), F32),
            small, small, small,
        ),
        in_specs=[anywhere] * 7,
        out_specs=tuple(anywhere if big else vmem for big in (1, 1, 1, 0, 1, 1, 0, 1, 0, 0, 0, 1, 0, 1, 0, 0, 0)),
        scratch_shapes=[vm(value.shape, value.dtype) for value in got]
        + [
            vm((rows_loc, 4, width)), vm((rows_loc, 4, width)), vm((4, rows, width), F32),
            vm((rows, 3 * CHUNK), F32), vm((384, width), F32), dma((7,)), dma((8,)),
        ],
        compiler_params=pltpu.CompilerParams(vmem_limit_bytes=63 * 2**20),
    )(*got)


def norm_layer(resid, gain, shift):
    center = resid - jnp.mean(resid, axis=-1, keepdims=True)
    spread = jnp.mean(center * center, axis=-1, keepdims=True)
    return center * lax.rsqrt(spread + 1e-05) * gain + shift


def exact_gelu(value):
    return jax.nn.gelu(value, approximate=False)


def project(left, weight):
    return jnp.einsum("spd,de->spe", left, weight, preferred_element_type=jnp.float32)


def back_project(grad_in, weight):
    return jnp.einsum("spe,de->spd", grad_in, weight, preferred_element_type=jnp.float32)


def weight_grad(left, right):
    return jnp.einsum("spd,spe->de", left, right, preferred_element_type=jnp.float32)


def column_sum(grad_in):
    return jnp.sum(grad_in.astype(jnp.float32), axis=(0, 1))


def shards(
    tokens,
    lengths,
    w_query,
    b_query,
    w_key,
    w_value,
    b_value,
    w_out,
    b_out,
    gain_attn,
    shift_attn,
    w_up,
    b_up,
    w_down,
    b_down,
    gain_ffn,
    shift_ffn,
    cotangent,
):
    local_rows, pair_count, model_width = tokens.shape
    score_scale = HD ** (-0.5)
    total_len = local_rows * lax.axis_size("sp")
    queries = (project(tokens, w_query) + b_query.astype(jnp.float32)).astype(jnp.bfloat16)
    keys_local = project(tokens, w_key).astype(jnp.bfloat16)
    values_local = (project(tokens, w_value) + b_value.astype(jnp.float32)).astype(jnp.bfloat16)
    keys_all, values_all = (
        lax.all_gather(keys_local, "sp", axis=0, tiled=True),
        lax.all_gather(values_local, "sp", axis=0, tiled=True),
    )
    query_heads = queries.reshape(local_rows, pair_count, HEADS, HD)
    key_heads = keys_all.reshape(total_len, pair_count, HEADS, HD)
    value_heads = values_all.reshape(total_len, pair_count, HEADS, HD)
    scores = (
        jnp.einsum("iphe,jphe->phij", query_heads, key_heads, preferred_element_type=jnp.float32)
        * score_scale
    )
    key_valid = jnp.arange(total_len)[None, :] < lengths[:, None]
    scores = jnp.where(key_valid[:, None, None, :], scores, -1e30)
    top_score = jnp.max(scores, axis=-1, keepdims=True)
    expo = jnp.exp(scores - top_score)
    row_total = jnp.sum(expo, axis=-1, keepdims=True)
    weights_full = expo / row_total
    probs = weights_full.astype(jnp.bfloat16)
    attended = jnp.einsum("phij,jphe->iphe", probs, value_heads, preferred_element_type=jnp.float32)
    attended_low = attended.reshape(local_rows, pair_count, model_width).astype(jnp.bfloat16)
    branch = project(attended_low, w_out) + b_out.astype(jnp.float32)
    first_sum = tokens.astype(jnp.float32) + branch
    hidden, first_back = jax.vjp(
        norm_layer, first_sum, gain_attn.astype(jnp.float32), shift_attn.astype(jnp.float32)
    )
    hidden_low = hidden.astype(jnp.bfloat16)
    inner = project(hidden_low, w_up) + b_up.astype(jnp.float32)
    activated, gelu_back = jax.vjp(exact_gelu, inner)
    activated_low = activated.astype(jnp.bfloat16)
    second_sum = hidden + project(activated_low, w_down) + b_down.astype(jnp.float32)
    mixed, second_back = jax.vjp(
        norm_layer, second_sum, gain_ffn.astype(jnp.float32), shift_ffn.astype(jnp.float32)
    )
    d_second, grad_gain_ffn, grad_shift_ffn = second_back(cotangent.astype(jnp.float32))
    d_ffn = d_second.astype(jnp.bfloat16)
    grad_down = weight_grad(activated_low, d_ffn)
    grad_bdown = column_sum(d_ffn)
    d_inner = gelu_back(back_project(d_ffn, w_down))[0].astype(jnp.bfloat16)
    grad_up = weight_grad(hidden_low, d_inner)
    grad_bup = column_sum(d_inner)
    d_hidden = d_second + back_project(d_inner, w_up)
    d_first, grad_gain_attn, grad_shift_attn = first_back(d_hidden)
    d_branch = d_first.astype(jnp.bfloat16)
    grad_out = weight_grad(attended_low, d_branch)
    grad_bout = column_sum(d_branch)
    d_attended = back_project(d_branch, w_out).astype(jnp.bfloat16)
    d_att_heads = d_attended.reshape(local_rows, pair_count, HEADS, HD)
    d_probs = jnp.einsum(
        "iphe,jphe->phij", d_att_heads, value_heads, preferred_element_type=jnp.float32
    )
    row_delta = jnp.sum(weights_full * d_probs, axis=-1, keepdims=True)
    d_scores = weights_full * (d_probs - row_delta)
    d_scores_low = d_scores.astype(jnp.bfloat16)
    d_query_heads = (
        jnp.einsum("phij,jphe->iphe", d_scores_low, key_heads, preferred_element_type=jnp.float32)
        * score_scale
    )
    d_queries = d_query_heads.reshape(local_rows, pair_count, model_width).astype(jnp.bfloat16)
    row_count = local_rows * lax.axis_size("sp")
    key_part = (
        jnp.einsum("phij,iphe->jphe", d_scores_low, query_heads, preferred_element_type=jnp.float32)
        * score_scale
    )
    value_part = jnp.einsum(
        "phij,iphe->jphe", probs, d_att_heads, preferred_element_type=jnp.float32
    )
    key_grads = lax.psum_scatter(
        jnp.concatenate(
            (
                key_part.reshape(row_count, pair_count, model_width),
                value_part.reshape(row_count, pair_count, model_width),
            ),
            axis=2,
        ).astype(jnp.bfloat16),
        "sp",
        scatter_dimension=0,
        tiled=True,
    ).astype(jnp.float32)
    d_keys = key_grads[:, :, :model_width].astype(jnp.bfloat16)
    d_values = key_grads[:, :, model_width:].astype(jnp.bfloat16)
    grad_query = weight_grad(tokens, d_queries)
    grad_bquery = column_sum(d_queries)
    grad_key = weight_grad(tokens, d_keys)
    grad_value = weight_grad(tokens, d_values)
    grad_bvalue = column_sum(d_values)
    d_tokens = (
        d_first
        + back_project(d_queries, w_query)
        + back_project(d_keys, w_key)
        + back_project(d_values, w_value)
    )
    summed = (
        lax.psum_scatter(grad_query, "dp", scatter_dimension=0, tiled=True),
        lax.psum_scatter(grad_bquery, "dp", scatter_dimension=0, tiled=True),
        lax.psum_scatter(grad_key, "dp", scatter_dimension=0, tiled=True),
        lax.psum_scatter(grad_value, "dp", scatter_dimension=0, tiled=True),
        lax.psum_scatter(grad_bvalue, "dp", scatter_dimension=0, tiled=True),
        lax.psum_scatter(grad_out, "dp", scatter_dimension=0, tiled=True),
        lax.psum_scatter(grad_bout, "dp", scatter_dimension=0, tiled=True),
        lax.psum_scatter(grad_gain_attn, "dp", scatter_dimension=0, tiled=True),
        lax.psum_scatter(grad_shift_attn, "dp", scatter_dimension=0, tiled=True),
        lax.psum_scatter(grad_up, "dp", scatter_dimension=0, tiled=True),
        lax.psum_scatter(grad_bup, "dp", scatter_dimension=0, tiled=True),
        lax.psum_scatter(grad_down, "dp", scatter_dimension=0, tiled=True),
        lax.psum_scatter(grad_bdown, "dp", scatter_dimension=0, tiled=True),
        lax.psum_scatter(grad_gain_ffn, "dp", scatter_dimension=0, tiled=True),
        lax.psum_scatter(grad_shift_ffn, "dp", scatter_dimension=0, tiled=True),
    )
    summed = tuple(
        (
            lax.psum(summed[0].astype(jnp.bfloat16), "sp").astype(jnp.float32),
            lax.psum(summed[1].astype(jnp.bfloat16), "sp").astype(jnp.float32),
            lax.psum(summed[2].astype(jnp.bfloat16), "sp").astype(jnp.float32),
            lax.psum(summed[3].astype(jnp.bfloat16), "sp").astype(jnp.float32),
            lax.psum(summed[4].astype(jnp.bfloat16), "sp").astype(jnp.float32),
            lax.psum(summed[5].astype(jnp.bfloat16), "sp").astype(jnp.float32),
            lax.psum(summed[6].astype(jnp.bfloat16), "sp").astype(jnp.float32),
            lax.psum(summed[7].astype(jnp.bfloat16), "sp").astype(jnp.float32),
            lax.psum(summed[8].astype(jnp.bfloat16), "sp").astype(jnp.float32),
            lax.psum(summed[9].astype(jnp.bfloat16), "sp").astype(jnp.float32),
            lax.psum(summed[10].astype(jnp.bfloat16), "sp").astype(jnp.float32),
            lax.psum(summed[11].astype(jnp.bfloat16), "sp").astype(jnp.float32),
            lax.psum(summed[12].astype(jnp.bfloat16), "sp").astype(jnp.float32),
            lax.psum(summed[13].astype(jnp.bfloat16), "sp").astype(jnp.float32),
            lax.psum(summed[14].astype(jnp.bfloat16), "sp").astype(jnp.float32),
        )
    )
    return (
        mixed.astype(jnp.bfloat16),
        d_tokens.astype(jnp.bfloat16),
        summed[0],
        summed[1],
        summed[2],
        summed[3],
        summed[4],
        summed[5],
        summed[6],
        summed[7],
        summed[8],
        summed[9],
        summed[10],
        summed[11],
        summed[12],
        summed[13],
        summed[14],
    )


def solution(mesh):
    placed = (
        P("sp", "dp", None),
        P("dp"),
        P(),
        P(),
        P(),
        P(),
        P(),
        P(),
        P(),
        P(),
        P(),
        P(),
        P(),
        P(),
        P(),
        P(),
        P(),
        P("sp", "dp", None),
    )
    fits = mesh.shape["dp"] == 8 and mesh.shape["sp"] == 4
    return jax.shard_map(
        fused if fits else shards,
        mesh=mesh,
        in_specs=placed,
        out_specs=(
            P("sp", "dp", None),
            P("sp", "dp", None),
            P("dp", None),
            P("dp"),
            P("dp", None),
            P("dp", None),
            P("dp"),
            P("dp", None),
            P("dp"),
            P("dp"),
            P("dp"),
            P("dp", None),
            P("dp"),
            P("dp", None),
            P("dp"),
            P("dp"),
            P("dp"),
        ),
        check_vma=False,
    )
```

```python
import functools

import jax
import jax.numpy as jnp
from jax import lax
from jax.experimental import pallas as pl
from jax.experimental.pallas import tpu as pltpu
from jax.sharding import PartitionSpec as P

HEADS = 12
HD = 64
EPS = 1e-05
MESH_ID = pl.DeviceIdType.MESH
BF = jnp.bfloat16
F32 = jnp.float32


def nn(left, right):
    return jnp.dot(left, right, preferred_element_type=F32)


def nt(left, right):
    return lax.dot_general(left, right, (((1,), (1,)), ((), ())), preferred_element_type=F32)


def tn(left, right):
    return lax.dot_general(left, right, (((0,), (0,)), ((), ())), preferred_element_type=F32)


def aligned(start, step=128):
    return pl.multiple_of(start, step)


UNITS = (
    ("d", 0, 0, 256), ("d", 0, 256, 256), ("d", 0, 512, 256), ("d", 1, 0, 384), ("d", 1, 384, 384), ("d", 2, 0, 384),
    ("d", 2, 384, 384), ("u", 0, 0, 1024), ("u", 1, 0, 1024), ("u", 2, 0, 1024), ("o",), ("p", 0, 3, 0),
    ("p", 0, 1, 1), ("p", 1, 2, 1), ("p", 0, 1, 2), ("p", 1, 1, 2), ("p", 2, 1, 2),
)
PATH = (
    "c102y", "c120Y", "c0y12", "c102y", "c0y12", "cy120", "c01y2", "cy120", "cy012", "c0y12", "c120Y", "c012y",
    "c012y", "c0y12", "c012Y", "c0y12", "c0y12",
)
ORDER = (
    "M", 0, 1, 2, 3, 0, 1, 2, 4, 5, 6, "X", "I0", 3, 4, "I1", 5, 6, 0, 2, "H0", 1, 7, 4, 8, 5, 3, 7, 2, 9, "F", 6, 1,
    8, 4, 0, "A", 9, 5, 2, 10, 3, 1, "B0", 6, 4, 10, 0, 11, 5, 2, "B2", 7, 3, 11, 4, 12, 9, 5, 13, "B4", 12, 13, 10,
    8, "T", "K", 1, 6, 0, 2, 7, 3, 11, 4, 14, 15, 16, "V0", 12, 14, 15, 16, "V1", 9, 5, 10, 13, 6, 11, 12, 8, 7, 9,
    14, 0, 11, 3, 15, 12, 8, 13, 6, 16, 9, "V2", 11, 14, 15, 12, 10, 13, 16, 7, 8, "V3", 9, 14, 15, 11, 12, 16, 13,
    10, 7, "V4", 15, 8, 16, 14, 13, "V5", 15, 16,
)
VEC_PATH = "c012y"
ROWS_VEC = 16
CHUNK = 1024
ATTEND = 6


def unit_dims(unit, rows, width):
    kind = unit[0]
    if kind == "d":
        return None, unit[3], 128
    if kind == "u":
        return None, rows, unit[3]
    if kind == "o":
        return None, rows, width
    return unit[2], rows, 256


def land_shape(unit, path, stage, rows, width):
    many, r, c = unit_dims(unit, rows, width)
    lead = [2, 2, 2]
    for kind in path[: stage + 1]:
        if kind == "c" and unit[0] != "d":
            c //= 2
        elif kind in "cy":
            r //= 2
        elif kind != "Y":
            lead[2 - int(kind)] = 0
    return (() if many is None else (many,)) + tuple(n for n in lead if n) + (r, c)


def gelu_parts(x):
    cdf = 0.5 + 0.5 * lax.erf(x * (0.5**0.5))
    pdf = jnp.exp(-0.5 * x * x) * 0.3989422804014327
    return x * cdf, cdf + x * pdf


def layer_kernel(*refs):
    it = iter(refs)
    len_ref = next(it)
    bias_refs = [next(it) for _ in range(9)]
    (tok_ref, cot_ref, wq_ref, wk_ref, wv_ref, wo_ref, wu_ref, wd_ref) = (next(it) for _ in range(8))
    (mix_out, dtok_out, go_out, gp_out, gu_out, gd_out, gv_out) = (next(it) for _ in range(7))
    (raw_s, tokp, cotp, x_s, cot_s, x_t, hl_t, df_t) = (next(it) for _ in range(8))
    (wa, wu, wd, gd_s, qkv_s, p_s, att_s, linv_s, xh_s, rs_s, hl_s, act_s, gp_s, acc_s, km_s, vec_s) = (
        next(it) for _ in range(16)
    )
    vs, vl = next(it), next(it)
    lands = [[next(it) for _ in path] for path in PATH]
    tails = [next(it) if "y" in path else None for path in PATH]
    (wsem, lsem, asend, arecv, usend, urecv, ufin, vsend, vrecv) = (next(it) for _ in range(9))

    rows_loc, width = tok_ref.shape[0], tok_ref.shape[2]
    total = rows_loc * 4
    half = total // 2
    rows = width // 8
    dp, sp = lax.axis_index("dp"), lax.axis_index("sp")
    bits = [lax.rem(lax.div(dp, 2**k), 2) for k in range(3)]
    core, ybit = lax.rem(sp, 2), lax.div(sp, 2)

    def sp_xor(k):
        low, high = core, ybit
        if k & 1:
            low = 1 - low
        if k & 2:
            high = 1 - high
        return high * 2 + low

    def peer(kind):
        if kind == "c":
            return (dp, sp_xor(1))
        if kind in "yY":
            return (dp, sp_xor(2))
        k = int(kind)
        return (dp + 2**k * (1 - 2 * bits[k]), sp)

    barrier = pltpu.get_barrier_semaphore()
    greet = [(dp, sp_xor(k)) for k in (1, 2, 3)] + [peer(k) for k in "012"]
    for other in greet:
        pl.semaphore_signal(barrier, inc=1, device_id=other, device_id_type=MESH_ID)

    def load(src, dst, at):
        copy = pltpu.make_async_copy(src, dst, wsem.at[at])
        copy.start()
        return copy

    def landed(ref, sem):
        pltpu.make_async_copy(ref, ref, sem).wait()

    quick = rows_loc // 2
    tok_loads = [load(tok_ref.at[pl.ds(i * quick, quick)], raw_s.at[pl.ds(i * quick, quick)], i) for i in range(2)]
    attn_loads = [load(ref, wa.at[i], 2 + i) for i, ref in enumerate((wq_ref, wk_ref, wv_ref, wo_ref))]

    def exchange(src, dst, group, first=0, size=rows_loc):
        for k in (2, 3, 1):
            other = sp_xor(k)
            pltpu.make_async_remote_copy(
                src_ref=src.at[other, pl.ds(first, size)],
                dst_ref=dst.at[pl.ds(aligned(sp * rows_loc + first, size), size)],
                send_sem=asend.at[group],
                recv_sem=arecv.at[2 if group else 0 if k == 1 else 1],
                device_id=(dp, other),
                device_id_type=MESH_ID,
            ).start()
        dst[pl.ds(aligned(sp * rows_loc + first, size), size), :] = src[sp, pl.ds(first, size)]

    for i in range(2):
        tok_loads[i].wait()
        tokp[:, pl.ds(i * quick, quick)] = jnp.swapaxes(raw_s[pl.ds(i * quick, quick)], 0, 1)
        if i == 0:
            pl.semaphore_wait(barrier, len(greet))
        exchange(tokp, x_s, 0, i * quick, quick)
    cot_load = load(cot_ref, raw_s, 6)
    for j in range(3):
        for r in range(8):
            load(wu_ref.at[:, :, :, :, pl.ds(384 * r + 128 * j, 128)], wu.at[j, :, :, :, :, pl.ds(128 * r, 128)], 7 + j)
    for j in range(3):
        load(wd_ref.at[:, :, :, j], wd.at[j], 10)

    vec_s[1:2, :] = jnp.zeros((1, CHUNK), F32)
    for i, row in enumerate((0, 2, 3, 4, 5, 6, 7, 8)):
        vec_s[pl.ds(row, 1), pl.ds(0, width)] = bias_refs[i][...].astype(F32).reshape(1, width)
    for j in range(3):
        for r in range(8):
            part = bias_refs[8][pl.ds(384 * r + 128 * j, 128)]
            vec_s[pl.ds(10 + j, 1), pl.ds(128 * r, 128)] = part.astype(F32).reshape(1, 128)

    state = [dict(stage=0, copies=[]) for _ in UNITS]

    def region(unit, kinds, last_other=False, at_y=None):
        kind = unit[0]
        many, r, c = unit_dims(unit, rows, width)
        r0, c0 = (unit[2] if kind == "d" else 0), (256 * unit[3] if kind == "p" else unit[2] if kind == "u" else 0)
        lead = [slice(None)] * 3
        for i, step in enumerate(kinds):
            flip = last_other and i == len(kinds) - 1
            if step == "c":
                at = 1 - core if flip else core
                if kind == "d":
                    r //= 2
                    r0 = r0 + at * r
                else:
                    c //= 2
                    c0 = c0 + at * c
            elif step == "y":
                r //= 2
                r0 = r0 + (1 - ybit if flip else ybit if at_y is None else at_y) * r
            elif step != "Y":
                b = bits[int(step)]
                lead[2 - int(step)] = 1 - b if flip else b
        span = (pl.ds(r0 if isinstance(r0, int) else aligned(r0, 16), r), pl.ds(c0 if isinstance(c0, int) else aligned(c0), c))
        if kind == "d":
            return gd_s, (unit[1], *lead, *span)
        if kind == "u":
            return wu, (unit[1], *lead, *span)
        if kind == "o":
            return wa, (3, *lead, *span)
        return wd, (pl.ds(unit[1], many), *lead, *span)

    def out_region(unit, path, at_y=None):
        ref, at = region(unit, path, at_y=at_y)
        kind = unit[0]
        if kind == "d":
            return gd_out.at[unit[1], at[4], at[5]]
        if kind == "u":
            return gu_out.at[unit[1], at[4], at[5]]
        if kind == "o":
            return go_out.at[at[4], at[5]]
        return gp_out.at[at[0], at[4], at[5]]

    def send(n, stage, src, dst, to, last=False):
        copy = pltpu.make_async_remote_copy(
            src_ref=src,
            dst_ref=dst,
            send_sem=usend.at[n],
            recv_sem=ufin.at[0] if last else urecv.at[n, stage],
            device_id=to,
            device_id_type=MESH_ID,
        )
        copy.start()
        state[n]["copies"].append(copy)

    def advance(n):
        unit, path = UNITS[n], PATH[n]
        stage = state[n]["stage"]
        state[n]["stage"] += 1
        if stage > len(path):
            state[n]["copies"][stage - 1].wait_recv()
            dst = out_region(unit, path, 1 - ybit)
            send(n, stage, tails[n], dst, peer("c"), last=True)
            pltpu.make_async_copy(tails[n], dst, lsem.at[0]).start()
            return
        if stage > 0:
            state[n]["copies"][stage - 1].wait_recv()
            ref, at = region(unit, path[:stage])
            if path[stage - 1] == "Y":
                lands[n][stage - 1][...] = ref[at] + lands[n][stage - 1][...]
            else:
                ref[at] = ref[at] + lands[n][stage - 1][...]
        if stage < len(path):
            ref, at = region(unit, path[: stage + 1], last_other=True)
            send(n, stage, ref.at[at], lands[n][stage], peer(path[stage]))
            return
        dst = out_region(unit, path)
        if "Y" in path:
            src = lands[n][-1]
            send(n, stage, src, dst, peer("c"), last=True)
        else:
            ref, at = region(unit, path)
            src = ref.at[at]
            send(n, stage, src, tails[n], peer("y"))
            send(n, stage, src, dst, peer("c"), last=True)
        pltpu.make_async_copy(src, dst, lsem.at[0]).start()

    def finish(n):
        many, r, c = unit_dims(UNITS[n], rows, width)
        wide = (many or 1) * 8 * r * c // 256
        cols = next(b for b in (512, 384, 256, 128) if wide % b == 0 and wide // b <= HEADS)
        landed(p_s.at[pl.ds(0, wide // cols), pl.ds(0, 272), pl.ds(0, cols)], usend.at[n])

    def vec(row):
        return vec_s[pl.ds(row, 1), pl.ds(0, width)]

    def put_vec(row, value):
        vs[0, pl.ds(row, 1), pl.ds(0, value.shape[1])] = value

    vs[0] = jnp.zeros(vs.shape[1:], F32)
    length = len_ref[sp]
    dead = lax.broadcasted_iota(jnp.int32, (total, 128), 0) >= length
    km_s[...] = jnp.where(dead, -1e30, 0.0).astype(BF)
    ones = jnp.ones((16, total), BF)
    for ref in (x_t, hl_t, df_t):
        ref[pl.ds(width, 16), :] = ones

    def qkv(start):
        def one(w, carry):
            r = nn(x_s[pl.ds(start, half), :], wa[w].reshape(width, width)) + vec_s[pl.ds(w, 1), pl.ds(0, width)]
            r = r * jnp.where(w == 0, HD ** (-0.5), 1.0)
            qkv_s[w, pl.ds(start, half), :] = r.astype(BF)
            return carry

        lax.fori_loop(0, 3, one, 0)

    for copy in attn_loads[:3]:
        copy.wait()
    landed(x_s.at[pl.ds(0, rows_loc)], arecv.at[0])
    qkv(aligned(ybit * half))
    cot_load.wait()
    cotp[...] = jnp.swapaxes(raw_s[...], 0, 1)
    landed(x_s.at[pl.ds(0, half)], arecv.at[1])
    exchange(cotp, cot_s, 1)
    qkv(aligned((1 - ybit) * half))

    lane = lax.broadcasted_iota(jnp.int32, (total, 128), 1)
    low = lane < HD
    zeros = jnp.zeros((total, 128), BF)
    ones2 = jnp.ones((total, 128), BF)

    def attend(g):
        cols = pl.ds(aligned(g * 128), 128)
        q2, k2, v2 = qkv_s[0, :, cols], qkv_s[1, :, cols], qkv_s[2, :, cols]
        outs = []
        for h in range(2):
            mine = low if h == 0 else jnp.logical_not(low)
            qh = jnp.where(mine, q2, jnp.where(lane == HD * (1 - h), ones2, zeros))
            kh = jnp.where(mine, k2, km_s[...])
            vh = jnp.where(mine, v2, ones2)
            s = nt(qh, kh)
            e = jnp.exp(s - jnp.max(s, axis=-1, keepdims=True)).astype(BF)
            p_s[g * 2 + h] = e
            outs.append(nn(e, vh))
        num = jnp.where(low, outs[0], outs[1])
        den = pltpu.roll(jnp.where(low, outs[1], outs[0]), HD, axis=1)
        inv = 1.0 / den
        linv_s[:, cols] = inv.astype(BF)
        att_s[:, cols] = (num * inv).astype(BF)

    def attend_some(i, carry):
        for g in range(ATTEND):
            attend(i * ATTEND + g)
        return carry

    lax.fori_loop(0, HEADS // 2 // ATTEND, attend_some, 0)

    attn_loads[3].wait()

    def first_norm(i, carry):
        at = pl.ds(aligned(256 * i, 256), 256)
        r = nn(att_s[at, :], wa[3].reshape(width, width)) + vec(3) + x_s[at, :].astype(F32)
        mean = jnp.mean(r, axis=-1, keepdims=True)
        center = r - mean
        rs = lax.rsqrt(jnp.mean(center * center, axis=-1, keepdims=True) + EPS)
        xh = center * rs
        hidden = xh * vec(4) + vec(5)
        rs_s[at, :] = rs
        xh_s[at, :] = xh.astype(BF)
        acc_s[at, :] = hidden
        hl_s[at, :] = hidden.astype(BF)
        return carry

    lax.fori_loop(0, total // 256, first_norm, 0)

    for j in range(3):
        landed(wu.at[j], wsem.at[7 + j])

    def up(j, carry):
        inner = nn(hl_s[...], wu[j].reshape(width, CHUNK)) + vec_s[pl.ds(10 + j, 1), :]
        value, slope = gelu_parts(inner)
        act_s[j] = value.astype(BF)
        gp_s[j] = slope.astype(BF)
        return carry

    lax.fori_loop(0, 3, up, 0)

    landed(wd, wsem.at[10])

    def down(i, carry):
        cols = pl.ds(aligned(i * 256), 256)
        r = acc_s[:, cols] + vec_s[pl.ds(6, 1), cols]
        for j in range(3):
            r = r + nn(act_s[j], wd[j, :, :, :, :, cols].reshape(CHUNK, 256))
        acc_s[:, cols] = r
        return carry

    lax.fori_loop(0, width // 256, down, 0)

    away = cot_s.at[pl.ds(0, 3 * rows_loc)]
    landed(away, arecv.at[2])
    landed(away, asend.at[0])
    landed(away, asend.at[1])

    def second_norm(i, carry):
        at = pl.ds(aligned(128 * i, 128), 128)
        r = acc_s[at, :]
        mean = jnp.mean(r, axis=-1, keepdims=True)
        center = r - mean
        rs = lax.rsqrt(jnp.mean(center * center, axis=-1, keepdims=True) + EPS)
        xh = center * rs
        tokp[i] = (xh * vec(7) + vec(8)).astype(BF)
        dy = cot_s[at, :].astype(F32)
        dxh = dy * vec(7)
        d2 = rs * (dxh - jnp.mean(dxh, axis=-1, keepdims=True) - xh * jnp.mean(dxh * xh, axis=-1, keepdims=True))
        acc_s[at, :] = d2
        low2 = d2.astype(BF)
        cot_s[at, :] = low2
        df_t[:width, at] = low2.T
        adds = (
            jnp.sum(dy * xh, axis=0, keepdims=True),
            jnp.sum(dy, axis=0, keepdims=True),
            jnp.sum(low2.astype(F32), axis=0, keepdims=True),
        )
        return tuple(c + a for c, a in zip(carry, adds))

    zero = jnp.zeros((1, width), F32)
    g_gain, g_shift, g_bdown = lax.fori_loop(0, total // 128, second_norm, (zero, zero, zero))
    put_vec(6, g_gain)
    put_vec(7, g_shift)
    put_vec(5, g_bdown)

    given = []

    def give_back(src, dst, group):
        for k in (2, 3, 1):
            other = sp_xor(k)
            pltpu.make_async_remote_copy(
                src_ref=src.at[other],
                dst_ref=dst.at[sp],
                send_sem=asend.at[group],
                recv_sem=arecv.at[group + 1],
                device_id=(dp, other),
                device_id_type=MESH_ID,
            ).start()
        own = pltpu.make_async_copy(src.at[sp], dst.at[sp], lsem.at[group - 1])
        own.start()
        given.append((group, dst, own))

    def grad_down(j, first, size):
        r = nn(df_t[pl.ds(first, size), :], act_s[j]).astype(BF)
        for k in range(8):
            gd_s[j, k // 4, k // 2 % 2, k % 2, pl.ds(first, size), :] = r[:, 128 * k : 128 * k + 128]

    def inner_back(first, count):
        def body(j, carry):
            gp_s[j] = nt(cot_s[...], wd[j].reshape(CHUNK, width)).astype(BF) * gp_s[j]
            return carry

        lax.fori_loop(first, first + count, body, 0)

    def hidden_back(first, count):
        def body(j, carry):
            acc_s[...] += nt(gp_s[j], wu[j].reshape(width, CHUNK))
            return carry

        lax.fori_loop(first, first + count, body, 0)

    def grad_up(first, count):
        def body(j, carry):
            r = nn(hl_t[...], gp_s[j])
            wu[j] = r[:width].astype(BF).reshape(2, 2, 2, rows, CHUNK)
            vs[0, pl.ds(10 + j, 1), :] = r[width : width + 1]
            return carry

        lax.fori_loop(first, first + count, body, 0)

    def first_back():
        def body(i, carry):
            at = pl.ds(aligned(128 * i, 128), 128)
            dy = acc_s[at, :]
            xh = xh_s[at, :].astype(F32)
            dxh = dy * vec(4)
            d1 = rs_s[at, :] * (
                dxh - jnp.mean(dxh, axis=-1, keepdims=True) - xh * jnp.mean(dxh * xh, axis=-1, keepdims=True)
            )
            acc_s[at, :] = d1
            dh_s[at, :] = d1.astype(BF)
            adds = (jnp.sum(dy * xh, axis=0, keepdims=True), jnp.sum(dy, axis=0, keepdims=True))
            return tuple(c + a for c, a in zip(carry, adds))

        g_gain, g_shift = lax.fori_loop(0, total // 128, body, (zero, zero))
        put_vec(3, g_gain)
        put_vec(4, g_shift)

    def attended_back():
        d = nt(dh_s[...], wa[3].reshape(width, width))
        da_s[...] = (d * linv_s[...].astype(F32)).astype(BF)

    da_s = linv_s

    def grad_out():
        df_t[:width, :] = att_s[...].T
        r = nn(df_t[...], dh_s[...])
        wa[3] = r[:width].astype(BF).reshape(2, 2, 2, rows, width)
        vs[0, 2:3, :width] = r[width : width + 1]

    def attend_back(g):
        cols = slice(g * 128, g * 128 + 128)
        q2, k2, v2, d2 = qkv_s[0, :, cols], qkv_s[1, :, cols], qkv_s[2, :, cols], da_s[:, cols]
        prod = d2.astype(F32) * att_s[:, cols].astype(F32)
        dqs, dks, dvs = [], [], []
        for h in range(2):
            mine = low if h == 0 else jnp.logical_not(low)
            delta = -jnp.sum(jnp.where(mine, prod, 0.0), axis=-1, keepdims=True)
            upper = delta.astype(BF)
            lower = (delta - upper.astype(F32)).astype(BF)
            other = HD * (1 - h)
            fill = jnp.where(lane == other, upper, jnp.where(lane == other + 1, lower, zeros))
            e = p_s[g * 2 + h]
            ds = e * nt(jnp.where(mine, d2, fill), jnp.where(mine, v2, ones2)).astype(BF)
            dqs.append(nn(ds, k2))
            dks.append(tn(ds, q2))
            dvs.append(tn(e, d2))
        qkv_s[0, :, cols] = (jnp.where(low, dqs[0], dqs[1]) * HD ** (-0.5)).astype(BF)
        qkv_s[1, :, cols] = jnp.where(low, dks[0], dks[1]).astype(BF)
        qkv_s[2, :, cols] = jnp.where(low, dvs[0], dvs[1]).astype(BF)

    def grad_proj(n):
        cols = slice(256 * n, 256 * n + 256)

        def body(w, carry):
            r = nn(x_t[...], qkv_s[w, :, cols])
            wd[w, :, :, :, :rows, cols] = r[:width].astype(BF).reshape(2, 2, 2, rows, 256)
            vs[0, pl.ds(lax.rem(w * 14, 27), 1), cols] = r[width : width + 1]
            return carry

        lax.fori_loop(0, 3, body, 0)

    def tokens_back():
        def body(w, carry):
            acc_s[...] += nt(qkv_s[w], wa[w].reshape(width, width))
            return carry

        lax.fori_loop(0, 3, body, 0)
        cotp[...] = acc_s[...].astype(BF).reshape(4, rows_loc, width)

    vec_copies = []

    def vec_step(i):
        if i == 0:
            vl[0] = vs[0].astype(BF)
        else:
            vec_copies[i - 1].wait_recv()
            vl[i] = vl[i - 1] + vl[i]
        if i == 5:
            load(vl.at[5], gv_out, 11)
        if i < 5:
            copy = pltpu.make_async_remote_copy(
                src_ref=vl.at[i],
                dst_ref=vl.at[i + 1],
                send_sem=vsend.at[0],
                recv_sem=vrecv.at[i],
                device_id=peer(VEC_PATH[i]),
                device_id_type=MESH_ID,
            )
            copy.start()
            vec_copies.append(copy)

    def transpose_tokens():
        x_t[:width, :] = x_s[...].T
        hl_t[:width, :] = hl_s[...].T

    dh_s = hl_s

    made = set()

    def produce(n):
        unit = UNITS[n]
        if unit[0] == "d" and unit[1] == 0:
            grad_down(0, unit[2], unit[3])
            return
        key = (unit[0], unit[3]) if unit[0] == "p" else (unit[0], min(unit[1], 1)) if unit[0] in "du" else unit
        if key in made:
            return
        made.add(key)
        if key == ("d", 1):

            def both(j, carry):
                grad_down(j, 0, width)
                return carry

            lax.fori_loop(1, 3, both, 0)
        elif key[0] == "u":
            grad_up(key[1], 1 + key[1])
        elif key[0] == "o":
            grad_out()
        else:
            grad_proj(unit[3])

    for step in ORDER:
        if isinstance(step, int):
            if state[step]["stage"] == 0:
                produce(step)
            advance(step)
            continue
        name, at = step[0], int(step[1:] or 0)
        if name == "I":
            inner_back(at, 1 + at)
        elif name == "H":
            hidden_back(at, 3)
        elif name == "F":
            first_back()
        elif name == "A":
            attended_back()
        elif name == "B":
            attend_back(at)
            attend_back(at + 1)
        elif name == "T":
            tokens_back()
        elif name == "X":
            transpose_tokens()
        elif name == "M":
            give_back(tokp, mix_out, 2)
        elif name == "K":
            give_back(cotp, dtok_out, 3)
        elif name == "V":
            vec_step(at)
    landed(gv_out, wsem.at[11])
    final = p_s.at[pl.ds(0, 2), pl.ds(0, width * 9 // 16)]
    landed(final, ufin.at[0])
    landed(final, lsem.at[0])
    for n in range(len(UNITS)):
        finish(n)
    landed(vl.at[pl.ds(0, 5)], vsend.at[0])
    for group, dst, own in given:
        landed(tokp.at[pl.ds(0, 3)], asend.at[group])
        landed(dst.at[pl.ds(0, 3)], arecv.at[group + 1])
        own.wait()


def finish_kernel(*refs):
    it = iter(refs)
    sources = [next(it) for _ in range(7)]
    (o_mix, o_dtok, o_wq, o_bq, o_wk, o_wv, o_bv, o_wo, o_bo, o_ga, o_sa, o_up, o_bup, o_down, o_bdown, o_gf, o_sf) = (
        next(it) for _ in range(17)
    )
    held = [next(it) for _ in range(7)]
    staged = [next(it) for _ in range(5)]
    isem, osem = next(it), next(it)
    mix, dtok, go, gp, gu, gd, gv = held
    s_mix, s_dtok, s_sq, s_up, s_down = staged
    part = gu.shape[1] // 2
    pieces = [(4, (slice(None), pl.ds(i * part, part))) for i in range(2)] + [(5, (j,)) for j in range(3)]
    pieces += [(3, (w,)) for w in range(3)] + [(i, ()) for i in (2, 0, 1, 6)]
    loads = []
    for i, at in pieces:
        src, dst = (sources[i].at[at], held[i].at[at]) if at else (sources[i], held[i])
        copy = pltpu.make_async_copy(src, dst, isem.at[len(loads)])
        copy.start()
        loads.append(copy)
    width = mix.shape[2]
    rows = width // 8
    dp = lax.axis_index("dp")
    stores = []

    def store(src, dst):
        copy = pltpu.make_async_copy(src, dst, osem.at[len(stores)])
        copy.start()
        stores.append(copy)

    for i in range(2):
        loads[i].wait()
        at = slice(part * i, part * i + part)
        for j in range(3):
            for r in range(8):
                s_up[at, 384 * r + 128 * j : 384 * r + 128 * j + 128] = gu[j, at, 128 * r : 128 * r + 128].astype(F32)
        store(s_up.at[pl.ds(part * i, part)], o_up.at[pl.ds(part * i, part)])
    for j in range(3):
        loads[2 + j].wait()
        s_down[128 * j : 128 * j + 128, :] = gd[j].astype(F32).T
        store(s_down.at[pl.ds(128 * j, 128)], o_down.at[pl.ds(128 * j, 128)])
    for w in range(4):
        loads[5 + w].wait()
        s_sq[w] = (go[...] if w == 3 else gp[w]).astype(F32)
        store(s_sq.at[w], (o_wq, o_wk, o_wv, o_wo)[w])
    loads[9].wait()
    s_mix[...] = jnp.swapaxes(mix[...], 0, 1)
    store(s_mix, o_mix)
    loads[10].wait()
    s_dtok[...] = jnp.swapaxes(dtok[...], 0, 1)
    store(s_dtok, o_dtok)
    loads[11].wait()
    for j in range(3):
        o_bup[pl.ds(128 * j, 128)] = gv[pl.ds(10 + j, 1), pl.ds(aligned(dp * 128), 128)].astype(F32).reshape(128)
    turned = pltpu.roll(gv[pl.ds(0, 8), pl.ds(0, width)].astype(F32), lax.rem(width - rows * dp, width), axis=1)
    for i, ref in enumerate((o_bq, o_bv, o_bo, o_ga, o_sa, o_bdown, o_gf, o_sf)):
        ref[...] = turned[i : i + 1, :rows].reshape(rows)
    for copy in stores:
        copy.wait()


def fused(
    tokens, lengths, w_query, b_query, w_key, w_value, b_value, w_out, b_out, gain_attn, shift_attn,
    w_up, b_up, w_down, b_down, gain_ffn, shift_ffn, cotangent,
):
    rows_loc, pairs, width = tokens.shape
    total = rows_loc * 4
    rows = width // 8
    square = lambda w: w.reshape(2, 2, 2, rows, w.shape[1])
    args = (
        lengths, b_query, b_value, b_out, gain_attn, shift_attn, b_down, gain_ffn, shift_ffn, b_up, tokens, cotangent,
        square(w_query), square(w_key), square(w_value), square(w_out), square(w_up),
        w_down.reshape(2, 2, 2, 3, 128, width),
    )
    vm = lambda shape, dtype=BF: pltpu.VMEM(shape, dtype)
    full = (total, width)
    swapped = (4, rows_loc, width)
    turned = (width + 16, total)
    scratch = [
        vm((rows_loc, 4, width)), vm(swapped), vm(swapped), vm(full), vm(full), vm(turned), vm(turned), vm(turned),
        vm((4, 2, 2, 2, rows, width)), vm((3, 2, 2, 2, rows, CHUNK)), vm((3, 2, 2, 2, 128, width)),
        vm((3, 2, 2, 2, width, 128)),
        vm((3, total, width)), vm((HEADS, total, total)), vm(full), vm(full),
        vm(full), vm((total, 1), F32), vm(full), vm((3, total, CHUNK)), vm((3, total, CHUNK)),
        vm(full, F32), vm((total, 128)), vm((ROWS_VEC, CHUNK), F32),
        vm((1, ROWS_VEC, CHUNK), F32), vm((6, ROWS_VEC, CHUNK)),
    ]
    for unit, path in zip(UNITS, PATH):
        scratch += [vm(land_shape(unit, path, s, rows, width)) for s in range(len(path))]
    for unit, path in zip(UNITS, PATH):
        if "y" in path:
            scratch.append(vm(land_shape(unit, path, 4, rows, width)))
    dma = pltpu.SemaphoreType.DMA
    count = len(UNITS)
    scratch += [dma((12,)), dma((3,)), dma((4,)), dma((5,)), dma((count,)), dma((count, 6)), dma((1,)), dma((1,)), dma((5,))]
    anywhere = pl.BlockSpec(memory_space=pl.ANY)
    vmem = pl.BlockSpec(memory_space=pltpu.VMEM)
    got = pl.pallas_call(
        layer_kernel,
        out_shape=(
            jax.ShapeDtypeStruct(swapped, BF),
            jax.ShapeDtypeStruct(swapped, BF),
            jax.ShapeDtypeStruct((rows, width), BF),
            jax.ShapeDtypeStruct((3, rows, width), BF),
            jax.ShapeDtypeStruct((3, rows, CHUNK), BF),
            jax.ShapeDtypeStruct((3, width, 128), BF),
            jax.ShapeDtypeStruct((ROWS_VEC, CHUNK), BF),
        ),
        in_specs=[pl.BlockSpec(memory_space=pltpu.SMEM)] + [vmem] * 9 + [anywhere] * 8,
        out_specs=(anywhere,) * 7,
        scratch_shapes=scratch,
        compiler_params=pltpu.CompilerParams(collective_id=0, has_side_effects=True, vmem_limit_bytes=63 * 2**20),
    )(*args)
    small = jax.ShapeDtypeStruct((rows,), F32)
    flat = jax.ShapeDtypeStruct((rows, width), F32)
    whole = jax.ShapeDtypeStruct((rows_loc, 4, width), BF)
    return pl.pallas_call(
        finish_kernel,
        out_shape=(
            whole, whole, flat, small, flat, flat, small, flat, small, small, small,
            jax.ShapeDtypeStruct((rows, 3 * CHUNK), F32),
            jax.ShapeDtypeStruct((384,), F32),
            jax.ShapeDtypeStruct((384, width), F32),
            small, small, small,
        ),
        in_specs=[anywhere] * 7,
        out_specs=tuple(anywhere if big else vmem for big in (1, 1, 1, 0, 1, 1, 0, 1, 0, 0, 0, 1, 0, 1, 0, 0, 0)),
        scratch_shapes=[vm(value.shape, value.dtype) for value in got]
        + [
            vm((rows_loc, 4, width)), vm((rows_loc, 4, width)), vm((4, rows, width), F32),
            vm((rows, 3 * CHUNK), F32), vm((384, width), F32), dma((12,)), dma((11,)),
        ],
        compiler_params=pltpu.CompilerParams(vmem_limit_bytes=63 * 2**20),
    )(*got)


def norm_layer(resid, gain, shift):
    center = resid - jnp.mean(resid, axis=-1, keepdims=True)
    spread = jnp.mean(center * center, axis=-1, keepdims=True)
    return center * lax.rsqrt(spread + 1e-05) * gain + shift


def exact_gelu(value):
    return jax.nn.gelu(value, approximate=False)


def project(left, weight):
    return jnp.einsum("spd,de->spe", left, weight, preferred_element_type=jnp.float32)


def back_project(grad_in, weight):
    return jnp.einsum("spe,de->spd", grad_in, weight, preferred_element_type=jnp.float32)


def weight_grad(left, right):
    return jnp.einsum("spd,spe->de", left, right, preferred_element_type=jnp.float32)


def column_sum(grad_in):
    return jnp.sum(grad_in.astype(jnp.float32), axis=(0, 1))


def shards(
    tokens,
    lengths,
    w_query,
    b_query,
    w_key,
    w_value,
    b_value,
    w_out,
    b_out,
    gain_attn,
    shift_attn,
    w_up,
    b_up,
    w_down,
    b_down,
    gain_ffn,
    shift_ffn,
    cotangent,
):
    local_rows, pair_count, model_width = tokens.shape
    score_scale = HD ** (-0.5)
    total_len = local_rows * lax.axis_size("sp")
    queries = (project(tokens, w_query) + b_query.astype(jnp.float32)).astype(jnp.bfloat16)
    keys_local = project(tokens, w_key).astype(jnp.bfloat16)
    values_local = (project(tokens, w_value) + b_value.astype(jnp.float32)).astype(jnp.bfloat16)
    keys_all, values_all = (
        lax.all_gather(keys_local, "sp", axis=0, tiled=True),
        lax.all_gather(values_local, "sp", axis=0, tiled=True),
    )
    query_heads = queries.reshape(local_rows, pair_count, HEADS, HD)
    key_heads = keys_all.reshape(total_len, pair_count, HEADS, HD)
    value_heads = values_all.reshape(total_len, pair_count, HEADS, HD)
    scores = (
        jnp.einsum("iphe,jphe->phij", query_heads, key_heads, preferred_element_type=jnp.float32)
        * score_scale
    )
    key_valid = jnp.arange(total_len)[None, :] < lengths[:, None]
    scores = jnp.where(key_valid[:, None, None, :], scores, -1e30)
    top_score = jnp.max(scores, axis=-1, keepdims=True)
    expo = jnp.exp(scores - top_score)
    row_total = jnp.sum(expo, axis=-1, keepdims=True)
    weights_full = expo / row_total
    probs = weights_full.astype(jnp.bfloat16)
    attended = jnp.einsum("phij,jphe->iphe", probs, value_heads, preferred_element_type=jnp.float32)
    attended_low = attended.reshape(local_rows, pair_count, model_width).astype(jnp.bfloat16)
    branch = project(attended_low, w_out) + b_out.astype(jnp.float32)
    first_sum = tokens.astype(jnp.float32) + branch
    hidden, first_back = jax.vjp(
        norm_layer, first_sum, gain_attn.astype(jnp.float32), shift_attn.astype(jnp.float32)
    )
    hidden_low = hidden.astype(jnp.bfloat16)
    inner = project(hidden_low, w_up) + b_up.astype(jnp.float32)
    activated, gelu_back = jax.vjp(exact_gelu, inner)
    activated_low = activated.astype(jnp.bfloat16)
    second_sum = hidden + project(activated_low, w_down) + b_down.astype(jnp.float32)
    mixed, second_back = jax.vjp(
        norm_layer, second_sum, gain_ffn.astype(jnp.float32), shift_ffn.astype(jnp.float32)
    )
    d_second, grad_gain_ffn, grad_shift_ffn = second_back(cotangent.astype(jnp.float32))
    d_ffn = d_second.astype(jnp.bfloat16)
    grad_down = weight_grad(activated_low, d_ffn)
    grad_bdown = column_sum(d_ffn)
    d_inner = gelu_back(back_project(d_ffn, w_down))[0].astype(jnp.bfloat16)
    grad_up = weight_grad(hidden_low, d_inner)
    grad_bup = column_sum(d_inner)
    d_hidden = d_second + back_project(d_inner, w_up)
    d_first, grad_gain_attn, grad_shift_attn = first_back(d_hidden)
    d_branch = d_first.astype(jnp.bfloat16)
    grad_out = weight_grad(attended_low, d_branch)
    grad_bout = column_sum(d_branch)
    d_attended = back_project(d_branch, w_out).astype(jnp.bfloat16)
    d_att_heads = d_attended.reshape(local_rows, pair_count, HEADS, HD)
    d_probs = jnp.einsum(
        "iphe,jphe->phij", d_att_heads, value_heads, preferred_element_type=jnp.float32
    )
    row_delta = jnp.sum(weights_full * d_probs, axis=-1, keepdims=True)
    d_scores = weights_full * (d_probs - row_delta)
    d_scores_low = d_scores.astype(jnp.bfloat16)
    d_query_heads = (
        jnp.einsum("phij,jphe->iphe", d_scores_low, key_heads, preferred_element_type=jnp.float32)
        * score_scale
    )
    d_queries = d_query_heads.reshape(local_rows, pair_count, model_width).astype(jnp.bfloat16)
    row_count = local_rows * lax.axis_size("sp")
    key_part = (
        jnp.einsum("phij,iphe->jphe", d_scores_low, query_heads, preferred_element_type=jnp.float32)
        * score_scale
    )
    value_part = jnp.einsum(
        "phij,iphe->jphe", probs, d_att_heads, preferred_element_type=jnp.float32
    )
    key_grads = lax.psum_scatter(
        jnp.concatenate(
            (
                key_part.reshape(row_count, pair_count, model_width),
                value_part.reshape(row_count, pair_count, model_width),
            ),
            axis=2,
        ).astype(jnp.bfloat16),
        "sp",
        scatter_dimension=0,
        tiled=True,
    ).astype(jnp.float32)
    d_keys = key_grads[:, :, :model_width].astype(jnp.bfloat16)
    d_values = key_grads[:, :, model_width:].astype(jnp.bfloat16)
    grad_query = weight_grad(tokens, d_queries)
    grad_bquery = column_sum(d_queries)
    grad_key = weight_grad(tokens, d_keys)
    grad_value = weight_grad(tokens, d_values)
    grad_bvalue = column_sum(d_values)
    d_tokens = (
        d_first
        + back_project(d_queries, w_query)
        + back_project(d_keys, w_key)
        + back_project(d_values, w_value)
    )
    summed = (
        lax.psum_scatter(grad_query, "dp", scatter_dimension=0, tiled=True),
        lax.psum_scatter(grad_bquery, "dp", scatter_dimension=0, tiled=True),
        lax.psum_scatter(grad_key, "dp", scatter_dimension=0, tiled=True),
        lax.psum_scatter(grad_value, "dp", scatter_dimension=0, tiled=True),
        lax.psum_scatter(grad_bvalue, "dp", scatter_dimension=0, tiled=True),
        lax.psum_scatter(grad_out, "dp", scatter_dimension=0, tiled=True),
        lax.psum_scatter(grad_bout, "dp", scatter_dimension=0, tiled=True),
        lax.psum_scatter(grad_gain_attn, "dp", scatter_dimension=0, tiled=True),
        lax.psum_scatter(grad_shift_attn, "dp", scatter_dimension=0, tiled=True),
        lax.psum_scatter(grad_up, "dp", scatter_dimension=0, tiled=True),
        lax.psum_scatter(grad_bup, "dp", scatter_dimension=0, tiled=True),
        lax.psum_scatter(grad_down, "dp", scatter_dimension=0, tiled=True),
        lax.psum_scatter(grad_bdown, "dp", scatter_dimension=0, tiled=True),
        lax.psum_scatter(grad_gain_ffn, "dp", scatter_dimension=0, tiled=True),
        lax.psum_scatter(grad_shift_ffn, "dp", scatter_dimension=0, tiled=True),
    )
    summed = tuple(
        (
            lax.psum(summed[0].astype(jnp.bfloat16), "sp").astype(jnp.float32),
            lax.psum(summed[1].astype(jnp.bfloat16), "sp").astype(jnp.float32),
            lax.psum(summed[2].astype(jnp.bfloat16), "sp").astype(jnp.float32),
            lax.psum(summed[3].astype(jnp.bfloat16), "sp").astype(jnp.float32),
            lax.psum(summed[4].astype(jnp.bfloat16), "sp").astype(jnp.float32),
            lax.psum(summed[5].astype(jnp.bfloat16), "sp").astype(jnp.float32),
            lax.psum(summed[6].astype(jnp.bfloat16), "sp").astype(jnp.float32),
            lax.psum(summed[7].astype(jnp.bfloat16), "sp").astype(jnp.float32),
            lax.psum(summed[8].astype(jnp.bfloat16), "sp").astype(jnp.float32),
            lax.psum(summed[9].astype(jnp.bfloat16), "sp").astype(jnp.float32),
            lax.psum(summed[10].astype(jnp.bfloat16), "sp").astype(jnp.float32),
            lax.psum(summed[11].astype(jnp.bfloat16), "sp").astype(jnp.float32),
            lax.psum(summed[12].astype(jnp.bfloat16), "sp").astype(jnp.float32),
            lax.psum(summed[13].astype(jnp.bfloat16), "sp").astype(jnp.float32),
            lax.psum(summed[14].astype(jnp.bfloat16), "sp").astype(jnp.float32),
        )
    )
    return (
        mixed.astype(jnp.bfloat16),
        d_tokens.astype(jnp.bfloat16),
        summed[0],
        summed[1],
        summed[2],
        summed[3],
        summed[4],
        summed[5],
        summed[6],
        summed[7],
        summed[8],
        summed[9],
        summed[10],
        summed[11],
        summed[12],
        summed[13],
        summed[14],
    )


def solution(mesh):
    placed = (
        P("sp", "dp", None),
        P("dp"),
        P(),
        P(),
        P(),
        P(),
        P(),
        P(),
        P(),
        P(),
        P(),
        P(),
        P(),
        P(),
        P(),
        P(),
        P(),
        P("sp", "dp", None),
    )
    fits = mesh.shape["dp"] == 8 and mesh.shape["sp"] == 4
    return jax.shard_map(
        fused if fits else shards,
        mesh=mesh,
        in_specs=placed,
        out_specs=(
            P("sp", "dp", None),
            P("sp", "dp", None),
            P("dp", None),
            P("dp"),
            P("dp", None),
            P("dp", None),
            P("dp"),
            P("dp", None),
            P("dp"),
            P("dp"),
            P("dp"),
            P("dp", None),
            P("dp"),
            P("dp", None),
            P("dp"),
            P("dp"),
            P("dp"),
        ),
        check_vma=False,
    )
```

```python
import functools

import jax
import jax.numpy as jnp
from jax import lax
from jax.experimental import pallas as pl
from jax.experimental.pallas import tpu as pltpu
from jax.sharding import PartitionSpec as P

HEADS = 12
HD = 64
EPS = 1e-05
MESH_ID = pl.DeviceIdType.MESH
BF = jnp.bfloat16
F32 = jnp.float32


def nn(left, right):
    return jnp.dot(left, right, preferred_element_type=F32)


def nt(left, right):
    return lax.dot_general(left, right, (((1,), (1,)), ((), ())), preferred_element_type=F32)


def tn(left, right):
    return lax.dot_general(left, right, (((0,), (0,)), ((), ())), preferred_element_type=F32)


def aligned(start, step=128):
    return pl.multiple_of(start, step)


UNITS = (
    ("d", 0, 0, 256), ("d", 0, 256, 256), ("d", 0, 512, 256), ("d", 1, 0, 256), ("d", 1, 256, 256),
    ("d", 1, 512, 256), ("d", 2, 0, 256), ("d", 2, 256, 256), ("d", 2, 512, 256), ("u", 0, 0, 1024),
    ("u", 1, 0, 1024), ("u", 2, 0, 1024), ("o",), ("p", 0, 3, 0), ("p", 0, 1, 1), ("p", 1, 2, 1), ("p", 0, 1, 2),
    ("p", 1, 1, 2), ("p", 2, 1, 2),
)
PATH = (
    "c102Y", "c10y2", "c01y2", "c102y", "cy012", "cy120", "c01y2", "cy102", "c120Y", "c01y2", "c012y", "cy012",
    "c102y", "cy012", "c120Y", "cy012", "c01y2", "c01y2", "c0y12",
)
ORDER = (
    "M", 0, 1, 2, "X", 0, "I0", 1, 2, 3, 4, 5, 6, 7, 8, "I1", 3, 0, 4, 5, 6, 2, 7, "H0", 8, 1, 0, 9, 3, 4, 10, 2, 6,
    1, 9, 5, 11, "F", 8, 3, 10, 0, 4, 7, 6, "A", 11, 2, 1, 5, 12, 0, "B0", 6, 4, 8, 12, 7, 3, 2, 13, 1, "B2", 9, 5, 6,
    13, 4, 14, 11, 3, 2, 15, "B4", 1, 6, 14, 15, 12, 10, "T", "K", 8, 7, 5, 9, 16, 13, 4, 3, 17, 18, "V0", 14, 16, 17,
    11, 18, "V1", 15, 10, 12, 7, 14, 13, 11, 16, 10, 17, 8, 5, 13, 18, 12, "V2", 9, 16, 7, 17, 11, 10, 15, 14, 18,
    "V3", 13, 12, 16, 17, 15, 9, 18, 11, 10, "V4", 14, 16, 17, 13, 12, 15, 18, 9, "V5", 16, 17, 15, 18,
)
VEC_PATH = "c120y"
ROWS_VEC = 16
CHUNK = 1024
ATTEND = 6


def unit_dims(unit, rows, width):
    kind = unit[0]
    if kind == "d":
        return None, unit[3], 128
    if kind == "u":
        return None, rows, unit[3]
    if kind == "o":
        return None, rows, width
    return unit[2], rows, 256


def land_shape(unit, path, stage, rows, width):
    many, r, c = unit_dims(unit, rows, width)
    lead = [2, 2, 2]
    for kind in path[: stage + 1]:
        if kind == "c" and unit[0] != "d":
            c //= 2
        elif kind in "cy":
            r //= 2
        elif kind != "Y":
            lead[2 - int(kind)] = 0
    return (() if many is None else (many,)) + tuple(n for n in lead if n) + (r, c)


def gelu_parts(x):
    cdf = 0.5 + 0.5 * lax.erf(x * (0.5**0.5))
    pdf = jnp.exp(-0.5 * x * x) * 0.3989422804014327
    return x * cdf, cdf + x * pdf


def layer_kernel(*refs):
    it = iter(refs)
    len_ref = next(it)
    bias_refs = [next(it) for _ in range(9)]
    (tok_ref, cot_ref, wq_ref, wk_ref, wv_ref, wo_ref, wu_ref, wd_ref) = (next(it) for _ in range(8))
    (mix_out, dtok_out, go_out, gp_out, gu_out, gd_out, gv_out) = (next(it) for _ in range(7))
    (raw_s, tokp, cotp, x_s, cot_s, x_t, hl_t, df_t) = (next(it) for _ in range(8))
    (wa, wu, wd, gd_s, qkv_s, p_s, att_s, linv_s, xh_s, rs_s, hl_s, act_s, gp_s, acc_s, km_s, vec_s) = (
        next(it) for _ in range(16)
    )
    vs, vl = next(it), next(it)
    lands = [[next(it) for _ in path] for path in PATH]
    tails = [next(it) if "y" in path else None for path in PATH]
    (wsem, lsem, asend, arecv, usend, urecv, ufin, vsend, vrecv) = (next(it) for _ in range(9))

    rows_loc, width = tok_ref.shape[0], tok_ref.shape[2]
    total = rows_loc * 4
    half = total // 2
    rows = width // 8
    dp, sp = lax.axis_index("dp"), lax.axis_index("sp")
    bits = [lax.rem(lax.div(dp, 2**k), 2) for k in range(3)]
    core, ybit = lax.rem(sp, 2), lax.div(sp, 2)

    def sp_xor(k):
        low, high = core, ybit
        if k & 1:
            low = 1 - low
        if k & 2:
            high = 1 - high
        return high * 2 + low

    def peer(kind):
        if kind == "c":
            return (dp, sp_xor(1))
        if kind in "yY":
            return (dp, sp_xor(2))
        k = int(kind)
        return (dp + 2**k * (1 - 2 * bits[k]), sp)

    barrier = pltpu.get_barrier_semaphore()
    greet = [(dp, sp_xor(k)) for k in (1, 2, 3)] + [peer(k) for k in "012"]
    for other in greet:
        pl.semaphore_signal(barrier, inc=1, device_id=other, device_id_type=MESH_ID)

    def load(src, dst, at):
        copy = pltpu.make_async_copy(src, dst, wsem.at[at])
        copy.start()
        return copy

    def landed(ref, sem):
        pltpu.make_async_copy(ref, ref, sem).wait()

    quick = rows_loc // 2
    tok_loads = [load(tok_ref.at[pl.ds(i * quick, quick)], raw_s.at[pl.ds(i * quick, quick)], i) for i in range(2)]
    attn_loads = [load(ref, wa.at[i], 2 + i) for i, ref in enumerate((wq_ref, wk_ref, wv_ref, wo_ref))]

    def exchange(src, dst, group, first=0, size=rows_loc):
        for k in (2, 3, 1):
            other = sp_xor(k)
            pltpu.make_async_remote_copy(
                src_ref=src.at[other, pl.ds(first, size)],
                dst_ref=dst.at[pl.ds(aligned(sp * rows_loc + first, size), size)],
                send_sem=asend.at[group],
                recv_sem=arecv.at[2 if group else 0 if k == 1 else 1],
                device_id=(dp, other),
                device_id_type=MESH_ID,
            ).start()
        dst[pl.ds(aligned(sp * rows_loc + first, size), size), :] = src[sp, pl.ds(first, size)]

    for i in range(2):
        tok_loads[i].wait()
        tokp[:, pl.ds(i * quick, quick)] = jnp.swapaxes(raw_s[pl.ds(i * quick, quick)], 0, 1)
        if i == 0:
            pl.semaphore_wait(barrier, len(greet))
        exchange(tokp, x_s, 0, i * quick, quick)
    cot_load = load(cot_ref, raw_s, 6)
    for j in range(3):
        for r in range(8):
            load(wu_ref.at[:, :, :, :, pl.ds(384 * r + 128 * j, 128)], wu.at[j, :, :, :, :, pl.ds(128 * r, 128)], 7 + j)
    for j in range(3):
        load(wd_ref.at[:, :, :, j], wd.at[j], 10)

    vec_s[1:2, :] = jnp.zeros((1, CHUNK), F32)
    for i, row in enumerate((0, 2, 3, 4, 5, 6, 7, 8)):
        vec_s[pl.ds(row, 1), pl.ds(0, width)] = bias_refs[i][...].astype(F32).reshape(1, width)
    for j in range(3):
        for r in range(8):
            part = bias_refs[8][pl.ds(384 * r + 128 * j, 128)]
            vec_s[pl.ds(10 + j, 1), pl.ds(128 * r, 128)] = part.astype(F32).reshape(1, 128)

    state = [dict(stage=0, copies=[]) for _ in UNITS]

    def region(unit, kinds, last_other=False, at_y=None):
        kind = unit[0]
        many, r, c = unit_dims(unit, rows, width)
        r0, c0 = (unit[2] if kind == "d" else 0), (256 * unit[3] if kind == "p" else unit[2] if kind == "u" else 0)
        lead = [slice(None)] * 3
        for i, step in enumerate(kinds):
            flip = last_other and i == len(kinds) - 1
            if step == "c":
                at = 1 - core if flip else core
                if kind == "d":
                    r //= 2
                    r0 = r0 + at * r
                else:
                    c //= 2
                    c0 = c0 + at * c
            elif step == "y":
                r //= 2
                r0 = r0 + (1 - ybit if flip else ybit if at_y is None else at_y) * r
            elif step != "Y":
                b = bits[int(step)]
                lead[2 - int(step)] = 1 - b if flip else b
        span = (pl.ds(r0 if isinstance(r0, int) else aligned(r0, 16), r), pl.ds(c0 if isinstance(c0, int) else aligned(c0), c))
        if kind == "d":
            return gd_s, (unit[1], *lead, *span)
        if kind == "u":
            return wu, (unit[1], *lead, *span)
        if kind == "o":
            return wa, (3, *lead, *span)
        return wd, (pl.ds(unit[1], many), *lead, *span)

    def out_region(unit, path, at_y=None):
        ref, at = region(unit, path, at_y=at_y)
        kind = unit[0]
        if kind == "d":
            return gd_out.at[unit[1], at[4], at[5]]
        if kind == "u":
            return gu_out.at[unit[1], at[4], at[5]]
        if kind == "o":
            return go_out.at[at[4], at[5]]
        return gp_out.at[at[0], at[4], at[5]]

    def send(n, stage, src, dst, to, last=False):
        copy = pltpu.make_async_remote_copy(
            src_ref=src,
            dst_ref=dst,
            send_sem=usend.at[n],
            recv_sem=ufin.at[0] if last else urecv.at[n, stage],
            device_id=to,
            device_id_type=MESH_ID,
        )
        copy.start()
        state[n]["copies"].append(copy)

    def advance(n):
        unit, path = UNITS[n], PATH[n]
        stage = state[n]["stage"]
        state[n]["stage"] += 1
        if stage > len(path):
            state[n]["copies"][stage - 1].wait_recv()
            dst = out_region(unit, path, 1 - ybit)
            send(n, stage, tails[n], dst, peer("c"), last=True)
            pltpu.make_async_copy(tails[n], dst, lsem.at[0]).start()
            return
        if stage > 0:
            state[n]["copies"][stage - 1].wait_recv()
            ref, at = region(unit, path[:stage])
            if path[stage - 1] == "Y":
                lands[n][stage - 1][...] = ref[at] + lands[n][stage - 1][...]
            else:
                ref[at] = ref[at] + lands[n][stage - 1][...]
        if stage < len(path):
            ref, at = region(unit, path[: stage + 1], last_other=True)
            send(n, stage, ref.at[at], lands[n][stage], peer(path[stage]))
            return
        dst = out_region(unit, path)
        if "Y" in path:
            src = lands[n][-1]
            send(n, stage, src, dst, peer("c"), last=True)
        else:
            ref, at = region(unit, path)
            src = ref.at[at]
            send(n, stage, src, tails[n], peer("y"))
            send(n, stage, src, dst, peer("c"), last=True)
        pltpu.make_async_copy(src, dst, lsem.at[0]).start()

    def finish(n):
        many, r, c = unit_dims(UNITS[n], rows, width)
        wide = (many or 1) * 8 * r * c // 256
        cols = next(b for b in (512, 384, 256, 128) if wide % b == 0 and wide // b <= HEADS)
        landed(p_s.at[pl.ds(0, wide // cols), pl.ds(0, 272), pl.ds(0, cols)], usend.at[n])

    def vec(row):
        return vec_s[pl.ds(row, 1), pl.ds(0, width)]

    def put_vec(row, value):
        vs[0, pl.ds(row, 1), pl.ds(0, value.shape[1])] = value

    vs[0] = jnp.zeros(vs.shape[1:], F32)
    length = len_ref[sp]
    dead = lax.broadcasted_iota(jnp.int32, (total, 128), 0) >= length
    km_s[...] = jnp.where(dead, -1e30, 0.0).astype(BF)
    ones = jnp.ones((16, total), BF)
    for ref in (x_t, hl_t, df_t):
        ref[pl.ds(width, 16), :] = ones

    def qkv(start):
        def one(w, carry):
            r = nn(x_s[pl.ds(start, half), :], wa[w].reshape(width, width)) + vec_s[pl.ds(w, 1), pl.ds(0, width)]
            r = r * jnp.where(w == 0, HD ** (-0.5), 1.0)
            qkv_s[w, pl.ds(start, half), :] = r.astype(BF)
            return carry

        lax.fori_loop(0, 3, one, 0)

    for copy in attn_loads[:3]:
        copy.wait()
    landed(x_s.at[pl.ds(0, rows_loc)], arecv.at[0])
    qkv(aligned(ybit * half))
    cot_load.wait()
    cotp[...] = jnp.swapaxes(raw_s[...], 0, 1)
    landed(x_s.at[pl.ds(0, half)], arecv.at[1])
    exchange(cotp, cot_s, 1)
    qkv(aligned((1 - ybit) * half))

    lane = lax.broadcasted_iota(jnp.int32, (total, 128), 1)
    low = lane < HD
    zeros = jnp.zeros((total, 128), BF)
    ones2 = jnp.ones((total, 128), BF)

    def attend(g):
        cols = pl.ds(aligned(g * 128), 128)
        q2, k2, v2 = qkv_s[0, :, cols], qkv_s[1, :, cols], qkv_s[2, :, cols]
        outs = []
        for h in range(2):
            mine = low if h == 0 else jnp.logical_not(low)
            qh = jnp.where(mine, q2, jnp.where(lane == HD * (1 - h), ones2, zeros))
            kh = jnp.where(mine, k2, km_s[...])
            vh = jnp.where(mine, v2, ones2)
            s = nt(qh, kh)
            e = jnp.exp(s - jnp.max(s, axis=-1, keepdims=True)).astype(BF)
            p_s[g * 2 + h] = e
            outs.append(nn(e, vh))
        num = jnp.where(low, outs[0], outs[1])
        den = pltpu.roll(jnp.where(low, outs[1], outs[0]), HD, axis=1)
        inv = 1.0 / den
        linv_s[:, cols] = inv.astype(BF)
        att_s[:, cols] = (num * inv).astype(BF)

    def attend_some(i, carry):
        for g in range(ATTEND):
            attend(i * ATTEND + g)
        return carry

    lax.fori_loop(0, HEADS // 2 // ATTEND, attend_some, 0)

    attn_loads[3].wait()

    def first_norm(i, carry):
        at = pl.ds(aligned(256 * i, 256), 256)
        r = nn(att_s[at, :], wa[3].reshape(width, width)) + vec(3) + x_s[at, :].astype(F32)
        mean = jnp.mean(r, axis=-1, keepdims=True)
        center = r - mean
        rs = lax.rsqrt(jnp.mean(center * center, axis=-1, keepdims=True) + EPS)
        xh = center * rs
        hidden = xh * vec(4) + vec(5)
        rs_s[at, :] = rs
        xh_s[at, :] = xh.astype(BF)
        acc_s[at, :] = hidden
        hl_s[at, :] = hidden.astype(BF)
        return carry

    lax.fori_loop(0, total // 256, first_norm, 0)

    for j in range(3):
        landed(wu.at[j], wsem.at[7 + j])

    def up(j, carry):
        inner = nn(hl_s[...], wu[j].reshape(width, CHUNK)) + vec_s[pl.ds(10 + j, 1), :]
        value, slope = gelu_parts(inner)
        act_s[j] = value.astype(BF)
        gp_s[j] = slope.astype(BF)
        return carry

    lax.fori_loop(0, 3, up, 0)

    landed(wd, wsem.at[10])

    def down(i, carry):
        cols = pl.ds(aligned(i * 256), 256)
        r = acc_s[:, cols] + vec_s[pl.ds(6, 1), cols]
        for j in range(3):
            r = r + nn(act_s[j], wd[j, :, :, :, :, cols].reshape(CHUNK, 256))
        acc_s[:, cols] = r
        return carry

    lax.fori_loop(0, width // 256, down, 0)

    away = cot_s.at[pl.ds(0, 3 * rows_loc)]
    landed(away, arecv.at[2])
    landed(away, asend.at[0])
    landed(away, asend.at[1])

    def second_norm(i, carry):
        at = pl.ds(aligned(128 * i, 128), 128)
        r = acc_s[at, :]
        mean = jnp.mean(r, axis=-1, keepdims=True)
        center = r - mean
        rs = lax.rsqrt(jnp.mean(center * center, axis=-1, keepdims=True) + EPS)
        xh = center * rs
        tokp[i] = (xh * vec(7) + vec(8)).astype(BF)
        dy = cot_s[at, :].astype(F32)
        dxh = dy * vec(7)
        d2 = rs * (dxh - jnp.mean(dxh, axis=-1, keepdims=True) - xh * jnp.mean(dxh * xh, axis=-1, keepdims=True))
        acc_s[at, :] = d2
        low2 = d2.astype(BF)
        cot_s[at, :] = low2
        df_t[:width, at] = low2.T
        adds = (
            jnp.sum(dy * xh, axis=0, keepdims=True),
            jnp.sum(dy, axis=0, keepdims=True),
            jnp.sum(low2.astype(F32), axis=0, keepdims=True),
        )
        return tuple(c + a for c, a in zip(carry, adds))

    zero = jnp.zeros((1, width), F32)
    g_gain, g_shift, g_bdown = lax.fori_loop(0, total // 128, second_norm, (zero, zero, zero))
    put_vec(6, g_gain)
    put_vec(7, g_shift)
    put_vec(5, g_bdown)

    given = []

    def give_back(src, dst, group):
        for k in (2, 3, 1):
            other = sp_xor(k)
            pltpu.make_async_remote_copy(
                src_ref=src.at[other],
                dst_ref=dst.at[sp],
                send_sem=asend.at[group],
                recv_sem=arecv.at[group + 1],
                device_id=(dp, other),
                device_id_type=MESH_ID,
            ).start()
        own = pltpu.make_async_copy(src.at[sp], dst.at[sp], lsem.at[group - 1])
        own.start()
        given.append((group, dst, own))

    def grad_down(j, first, size):
        r = nn(df_t[pl.ds(first, size), :], act_s[j]).astype(BF)
        for k in range(8):
            gd_s[j, k // 4, k // 2 % 2, k % 2, pl.ds(first, size), :] = r[:, 128 * k : 128 * k + 128]

    def inner_back(first, count):
        def body(j, carry):
            gp_s[j] = nt(cot_s[...], wd[j].reshape(CHUNK, width)).astype(BF) * gp_s[j]
            return carry

        lax.fori_loop(first, first + count, body, 0)

    def hidden_back(first, count):
        def body(j, carry):
            acc_s[...] += nt(gp_s[j], wu[j].reshape(width, CHUNK))
            return carry

        lax.fori_loop(first, first + count, body, 0)

    def grad_up(first, count):
        def body(j, carry):
            r = nn(hl_t[...], gp_s[j])
            wu[j] = r[:width].astype(BF).reshape(2, 2, 2, rows, CHUNK)
            vs[0, pl.ds(10 + j, 1), :] = r[width : width + 1]
            return carry

        lax.fori_loop(first, first + count, body, 0)

    def first_back():
        def body(i, carry):
            at = pl.ds(aligned(128 * i, 128), 128)
            dy = acc_s[at, :]
            xh = xh_s[at, :].astype(F32)
            dxh = dy * vec(4)
            d1 = rs_s[at, :] * (
                dxh - jnp.mean(dxh, axis=-1, keepdims=True) - xh * jnp.mean(dxh * xh, axis=-1, keepdims=True)
            )
            acc_s[at, :] = d1
            dh_s[at, :] = d1.astype(BF)
            adds = (jnp.sum(dy * xh, axis=0, keepdims=True), jnp.sum(dy, axis=0, keepdims=True))
            return tuple(c + a for c, a in zip(carry, adds))

        g_gain, g_shift = lax.fori_loop(0, total // 128, body, (zero, zero))
        put_vec(3, g_gain)
        put_vec(4, g_shift)

    def attended_back():
        d = nt(dh_s[...], wa[3].reshape(width, width))
        da_s[...] = (d * linv_s[...].astype(F32)).astype(BF)

    da_s = linv_s

    def grad_out():
        df_t[:width, :] = att_s[...].T
        r = nn(df_t[...], dh_s[...])
        wa[3] = r[:width].astype(BF).reshape(2, 2, 2, rows, width)
        vs[0, 2:3, :width] = r[width : width + 1]

    def attend_back(g):
        cols = slice(g * 128, g * 128 + 128)
        q2, k2, v2, d2 = qkv_s[0, :, cols], qkv_s[1, :, cols], qkv_s[2, :, cols], da_s[:, cols]
        prod = d2.astype(F32) * att_s[:, cols].astype(F32)
        dqs, dks, dvs = [], [], []
        for h in range(2):
            mine = low if h == 0 else jnp.logical_not(low)
            delta = -jnp.sum(jnp.where(mine, prod, 0.0), axis=-1, keepdims=True)
            upper = delta.astype(BF)
            lower = (delta - upper.astype(F32)).astype(BF)
            other = HD * (1 - h)
            fill = jnp.where(lane == other, upper, jnp.where(lane == other + 1, lower, zeros))
            e = p_s[g * 2 + h]
            ds = e * nt(jnp.where(mine, d2, fill), jnp.where(mine, v2, ones2)).astype(BF)
            dqs.append(nn(ds, k2))
            dks.append(tn(ds, q2))
            dvs.append(tn(e, d2))
        qkv_s[0, :, cols] = (jnp.where(low, dqs[0], dqs[1]) * HD ** (-0.5)).astype(BF)
        qkv_s[1, :, cols] = jnp.where(low, dks[0], dks[1]).astype(BF)
        qkv_s[2, :, cols] = jnp.where(low, dvs[0], dvs[1]).astype(BF)

    def grad_proj(n):
        cols = slice(256 * n, 256 * n + 256)

        def body(w, carry):
            r = nn(x_t[...], qkv_s[w, :, cols])
            wd[w, :, :, :, :rows, cols] = r[:width].astype(BF).reshape(2, 2, 2, rows, 256)
            vs[0, pl.ds(lax.rem(w * 14, 27), 1), cols] = r[width : width + 1]
            return carry

        lax.fori_loop(0, 3, body, 0)

    def tokens_back():
        def body(w, carry):
            acc_s[...] += nt(qkv_s[w], wa[w].reshape(width, width))
            return carry

        lax.fori_loop(0, 3, body, 0)
        cotp[...] = acc_s[...].astype(BF).reshape(4, rows_loc, width)

    vec_copies = []

    def vec_step(i):
        if i == 0:
            vl[0] = vs[0].astype(BF)
        else:
            vec_copies[i - 1].wait_recv()
            vl[i] = vl[i - 1] + vl[i]
        if i == 5:
            load(vl.at[5], gv_out, 11)
        if i < 5:
            copy = pltpu.make_async_remote_copy(
                src_ref=vl.at[i],
                dst_ref=vl.at[i + 1],
                send_sem=vsend.at[0],
                recv_sem=vrecv.at[i],
                device_id=peer(VEC_PATH[i]),
                device_id_type=MESH_ID,
            )
            copy.start()
            vec_copies.append(copy)

    def transpose_tokens():
        x_t[:width, :] = x_s[...].T
        hl_t[:width, :] = hl_s[...].T

    dh_s = hl_s

    made = set()

    def produce(n):
        unit = UNITS[n]
        if unit[0] == "d" and unit[1] == 0:
            grad_down(0, unit[2], unit[3])
            return
        key = (unit[0], unit[3]) if unit[0] == "p" else (unit[0], min(unit[1], 1)) if unit[0] in "du" else unit
        if key in made:
            return
        made.add(key)
        if key == ("d", 1):

            def both(j, carry):
                grad_down(j, 0, width)
                return carry

            lax.fori_loop(1, 3, both, 0)
        elif key[0] == "u":
            grad_up(key[1], 1 + key[1])
        elif key[0] == "o":
            grad_out()
        else:
            grad_proj(unit[3])

    for step in ORDER:
        if isinstance(step, int):
            if state[step]["stage"] == 0:
                produce(step)
            advance(step)
            continue
        name, at = step[0], int(step[1:] or 0)
        if name == "I":
            inner_back(at, 1 + at)
        elif name == "H":
            hidden_back(at, 3)
        elif name == "F":
            first_back()
        elif name == "A":
            attended_back()
        elif name == "B":
            attend_back(at)
            attend_back(at + 1)
        elif name == "T":
            tokens_back()
        elif name == "X":
            transpose_tokens()
        elif name == "M":
            give_back(tokp, mix_out, 2)
        elif name == "K":
            give_back(cotp, dtok_out, 3)
        elif name == "V":
            vec_step(at)
    landed(gv_out, wsem.at[11])
    final = p_s.at[pl.ds(0, 2), pl.ds(0, width * 9 // 16)]
    landed(final, ufin.at[0])
    landed(final, lsem.at[0])
    for n in range(len(UNITS)):
        finish(n)
    landed(vl.at[pl.ds(0, 5)], vsend.at[0])
    for group, dst, own in given:
        landed(tokp.at[pl.ds(0, 3)], asend.at[group])
        landed(dst.at[pl.ds(0, 3)], arecv.at[group + 1])
        own.wait()


def finish_kernel(*refs):
    it = iter(refs)
    sources = [next(it) for _ in range(7)]
    (o_mix, o_dtok, o_wq, o_bq, o_wk, o_wv, o_bv, o_wo, o_bo, o_ga, o_sa, o_up, o_bup, o_down, o_bdown, o_gf, o_sf) = (
        next(it) for _ in range(17)
    )
    held = [next(it) for _ in range(7)]
    staged = [next(it) for _ in range(5)]
    isem, osem = next(it), next(it)
    mix, dtok, go, gp, gu, gd, gv = held
    s_mix, s_dtok, s_sq, s_up, s_down = staged
    part = gu.shape[1] // 2
    pieces = [(4, (slice(None), pl.ds(i * part, part))) for i in range(2)] + [(5, (j,)) for j in range(3)]
    pieces += [(3, (w,)) for w in range(3)] + [(i, ()) for i in (2, 0, 1, 6)]
    loads = []
    for i, at in pieces:
        src, dst = (sources[i].at[at], held[i].at[at]) if at else (sources[i], held[i])
        copy = pltpu.make_async_copy(src, dst, isem.at[len(loads)])
        copy.start()
        loads.append(copy)
    width = mix.shape[2]
    rows = width // 8
    dp = lax.axis_index("dp")
    stores = []

    def store(src, dst):
        copy = pltpu.make_async_copy(src, dst, osem.at[len(stores)])
        copy.start()
        stores.append(copy)

    for i in range(2):
        loads[i].wait()
        at = slice(part * i, part * i + part)
        for j in range(3):
            for r in range(8):
                s_up[at, 384 * r + 128 * j : 384 * r + 128 * j + 128] = gu[j, at, 128 * r : 128 * r + 128].astype(F32)
        store(s_up.at[pl.ds(part * i, part)], o_up.at[pl.ds(part * i, part)])
    for j in range(3):
        loads[2 + j].wait()
        s_down[128 * j : 128 * j + 128, :] = gd[j].astype(F32).T
        store(s_down.at[pl.ds(128 * j, 128)], o_down.at[pl.ds(128 * j, 128)])
    for w in range(4):
        loads[5 + w].wait()
        s_sq[w] = (go[...] if w == 3 else gp[w]).astype(F32)
        store(s_sq.at[w], (o_wq, o_wk, o_wv, o_wo)[w])
    loads[9].wait()
    s_mix[...] = jnp.swapaxes(mix[...], 0, 1)
    store(s_mix, o_mix)
    loads[10].wait()
    s_dtok[...] = jnp.swapaxes(dtok[...], 0, 1)
    store(s_dtok, o_dtok)
    loads[11].wait()
    for j in range(3):
        o_bup[pl.ds(128 * j, 128)] = gv[pl.ds(10 + j, 1), pl.ds(aligned(dp * 128), 128)].astype(F32).reshape(128)
    turned = pltpu.roll(gv[pl.ds(0, 8), pl.ds(0, width)].astype(F32), lax.rem(width - rows * dp, width), axis=1)
    for i, ref in enumerate((o_bq, o_bv, o_bo, o_ga, o_sa, o_bdown, o_gf, o_sf)):
        ref[...] = turned[i : i + 1, :rows].reshape(rows)
    for copy in stores:
        copy.wait()


def fused(
    tokens, lengths, w_query, b_query, w_key, w_value, b_value, w_out, b_out, gain_attn, shift_attn,
    w_up, b_up, w_down, b_down, gain_ffn, shift_ffn, cotangent,
):
    rows_loc, pairs, width = tokens.shape
    total = rows_loc * 4
    rows = width // 8
    square = lambda w: w.reshape(2, 2, 2, rows, w.shape[1])
    args = (
        lengths, b_query, b_value, b_out, gain_attn, shift_attn, b_down, gain_ffn, shift_ffn, b_up, tokens, cotangent,
        square(w_query), square(w_key), square(w_value), square(w_out), square(w_up),
        w_down.reshape(2, 2, 2, 3, 128, width),
    )
    vm = lambda shape, dtype=BF: pltpu.VMEM(shape, dtype)
    full = (total, width)
    swapped = (4, rows_loc, width)
    turned = (width + 16, total)
    scratch = [
        vm((rows_loc, 4, width)), vm(swapped), vm(swapped), vm(full), vm(full), vm(turned), vm(turned), vm(turned),
        vm((4, 2, 2, 2, rows, width)), vm((3, 2, 2, 2, rows, CHUNK)), vm((3, 2, 2, 2, 128, width)),
        vm((3, 2, 2, 2, width, 128)),
        vm((3, total, width)), vm((HEADS, total, total)), vm(full), vm(full),
        vm(full), vm((total, 1), F32), vm(full), vm((3, total, CHUNK)), vm((3, total, CHUNK)),
        vm(full, F32), vm((total, 128)), vm((ROWS_VEC, CHUNK), F32),
        vm((1, ROWS_VEC, CHUNK), F32), vm((6, ROWS_VEC, CHUNK)),
    ]
    for unit, path in zip(UNITS, PATH):
        scratch += [vm(land_shape(unit, path, s, rows, width)) for s in range(len(path))]
    for unit, path in zip(UNITS, PATH):
        if "y" in path:
            scratch.append(vm(land_shape(unit, path, 4, rows, width)))
    dma = pltpu.SemaphoreType.DMA
    count = len(UNITS)
    scratch += [dma((12,)), dma((3,)), dma((4,)), dma((5,)), dma((count,)), dma((count, 6)), dma((1,)), dma((1,)), dma((5,))]
    anywhere = pl.BlockSpec(memory_space=pl.ANY)
    vmem = pl.BlockSpec(memory_space=pltpu.VMEM)
    got = pl.pallas_call(
        layer_kernel,
        out_shape=(
            jax.ShapeDtypeStruct(swapped, BF),
            jax.ShapeDtypeStruct(swapped, BF),
            jax.ShapeDtypeStruct((rows, width), BF),
            jax.ShapeDtypeStruct((3, rows, width), BF),
            jax.ShapeDtypeStruct((3, rows, CHUNK), BF),
            jax.ShapeDtypeStruct((3, width, 128), BF),
            jax.ShapeDtypeStruct((ROWS_VEC, CHUNK), BF),
        ),
        in_specs=[pl.BlockSpec(memory_space=pltpu.SMEM)] + [vmem] * 9 + [anywhere] * 8,
        out_specs=(anywhere,) * 7,
        scratch_shapes=scratch,
        compiler_params=pltpu.CompilerParams(collective_id=0, has_side_effects=True, vmem_limit_bytes=63 * 2**20),
    )(*args)
    small = jax.ShapeDtypeStruct((rows,), F32)
    flat = jax.ShapeDtypeStruct((rows, width), F32)
    whole = jax.ShapeDtypeStruct((rows_loc, 4, width), BF)
    return pl.pallas_call(
        finish_kernel,
        out_shape=(
            whole, whole, flat, small, flat, flat, small, flat, small, small, small,
            jax.ShapeDtypeStruct((rows, 3 * CHUNK), F32),
            jax.ShapeDtypeStruct((384,), F32),
            jax.ShapeDtypeStruct((384, width), F32),
            small, small, small,
        ),
        in_specs=[anywhere] * 7,
        out_specs=tuple(anywhere if big else vmem for big in (1, 1, 1, 0, 1, 1, 0, 1, 0, 0, 0, 1, 0, 1, 0, 0, 0)),
        scratch_shapes=[vm(value.shape, value.dtype) for value in got]
        + [
            vm((rows_loc, 4, width)), vm((rows_loc, 4, width)), vm((4, rows, width), F32),
            vm((rows, 3 * CHUNK), F32), vm((384, width), F32), dma((12,)), dma((11,)),
        ],
        compiler_params=pltpu.CompilerParams(vmem_limit_bytes=63 * 2**20),
    )(*got)


def norm_layer(resid, gain, shift):
    center = resid - jnp.mean(resid, axis=-1, keepdims=True)
    spread = jnp.mean(center * center, axis=-1, keepdims=True)
    return center * lax.rsqrt(spread + 1e-05) * gain + shift


def exact_gelu(value):
    return jax.nn.gelu(value, approximate=False)


def project(left, weight):
    return jnp.einsum("spd,de->spe", left, weight, preferred_element_type=jnp.float32)


def back_project(grad_in, weight):
    return jnp.einsum("spe,de->spd", grad_in, weight, preferred_element_type=jnp.float32)


def weight_grad(left, right):
    return jnp.einsum("spd,spe->de", left, right, preferred_element_type=jnp.float32)


def column_sum(grad_in):
    return jnp.sum(grad_in.astype(jnp.float32), axis=(0, 1))


def shards(
    tokens,
    lengths,
    w_query,
    b_query,
    w_key,
    w_value,
    b_value,
    w_out,
    b_out,
    gain_attn,
    shift_attn,
    w_up,
    b_up,
    w_down,
    b_down,
    gain_ffn,
    shift_ffn,
    cotangent,
):
    local_rows, pair_count, model_width = tokens.shape
    score_scale = HD ** (-0.5)
    total_len = local_rows * lax.axis_size("sp")
    queries = (project(tokens, w_query) + b_query.astype(jnp.float32)).astype(jnp.bfloat16)
    keys_local = project(tokens, w_key).astype(jnp.bfloat16)
    values_local = (project(tokens, w_value) + b_value.astype(jnp.float32)).astype(jnp.bfloat16)
    keys_all, values_all = (
        lax.all_gather(keys_local, "sp", axis=0, tiled=True),
        lax.all_gather(values_local, "sp", axis=0, tiled=True),
    )
    query_heads = queries.reshape(local_rows, pair_count, HEADS, HD)
    key_heads = keys_all.reshape(total_len, pair_count, HEADS, HD)
    value_heads = values_all.reshape(total_len, pair_count, HEADS, HD)
    scores = (
        jnp.einsum("iphe,jphe->phij", query_heads, key_heads, preferred_element_type=jnp.float32)
        * score_scale
    )
    key_valid = jnp.arange(total_len)[None, :] < lengths[:, None]
    scores = jnp.where(key_valid[:, None, None, :], scores, -1e30)
    top_score = jnp.max(scores, axis=-1, keepdims=True)
    expo = jnp.exp(scores - top_score)
    row_total = jnp.sum(expo, axis=-1, keepdims=True)
    weights_full = expo / row_total
    probs = weights_full.astype(jnp.bfloat16)
    attended = jnp.einsum("phij,jphe->iphe", probs, value_heads, preferred_element_type=jnp.float32)
    attended_low = attended.reshape(local_rows, pair_count, model_width).astype(jnp.bfloat16)
    branch = project(attended_low, w_out) + b_out.astype(jnp.float32)
    first_sum = tokens.astype(jnp.float32) + branch
    hidden, first_back = jax.vjp(
        norm_layer, first_sum, gain_attn.astype(jnp.float32), shift_attn.astype(jnp.float32)
    )
    hidden_low = hidden.astype(jnp.bfloat16)
    inner = project(hidden_low, w_up) + b_up.astype(jnp.float32)
    activated, gelu_back = jax.vjp(exact_gelu, inner)
    activated_low = activated.astype(jnp.bfloat16)
    second_sum = hidden + project(activated_low, w_down) + b_down.astype(jnp.float32)
    mixed, second_back = jax.vjp(
        norm_layer, second_sum, gain_ffn.astype(jnp.float32), shift_ffn.astype(jnp.float32)
    )
    d_second, grad_gain_ffn, grad_shift_ffn = second_back(cotangent.astype(jnp.float32))
    d_ffn = d_second.astype(jnp.bfloat16)
    grad_down = weight_grad(activated_low, d_ffn)
    grad_bdown = column_sum(d_ffn)
    d_inner = gelu_back(back_project(d_ffn, w_down))[0].astype(jnp.bfloat16)
    grad_up = weight_grad(hidden_low, d_inner)
    grad_bup = column_sum(d_inner)
    d_hidden = d_second + back_project(d_inner, w_up)
    d_first, grad_gain_attn, grad_shift_attn = first_back(d_hidden)
    d_branch = d_first.astype(jnp.bfloat16)
    grad_out = weight_grad(attended_low, d_branch)
    grad_bout = column_sum(d_branch)
    d_attended = back_project(d_branch, w_out).astype(jnp.bfloat16)
    d_att_heads = d_attended.reshape(local_rows, pair_count, HEADS, HD)
    d_probs = jnp.einsum(
        "iphe,jphe->phij", d_att_heads, value_heads, preferred_element_type=jnp.float32
    )
    row_delta = jnp.sum(weights_full * d_probs, axis=-1, keepdims=True)
    d_scores = weights_full * (d_probs - row_delta)
    d_scores_low = d_scores.astype(jnp.bfloat16)
    d_query_heads = (
        jnp.einsum("phij,jphe->iphe", d_scores_low, key_heads, preferred_element_type=jnp.float32)
        * score_scale
    )
    d_queries = d_query_heads.reshape(local_rows, pair_count, model_width).astype(jnp.bfloat16)
    row_count = local_rows * lax.axis_size("sp")
    key_part = (
        jnp.einsum("phij,iphe->jphe", d_scores_low, query_heads, preferred_element_type=jnp.float32)
        * score_scale
    )
    value_part = jnp.einsum(
        "phij,iphe->jphe", probs, d_att_heads, preferred_element_type=jnp.float32
    )
    key_grads = lax.psum_scatter(
        jnp.concatenate(
            (
                key_part.reshape(row_count, pair_count, model_width),
                value_part.reshape(row_count, pair_count, model_width),
            ),
            axis=2,
        ).astype(jnp.bfloat16),
        "sp",
        scatter_dimension=0,
        tiled=True,
    ).astype(jnp.float32)
    d_keys = key_grads[:, :, :model_width].astype(jnp.bfloat16)
    d_values = key_grads[:, :, model_width:].astype(jnp.bfloat16)
    grad_query = weight_grad(tokens, d_queries)
    grad_bquery = column_sum(d_queries)
    grad_key = weight_grad(tokens, d_keys)
    grad_value = weight_grad(tokens, d_values)
    grad_bvalue = column_sum(d_values)
    d_tokens = (
        d_first
        + back_project(d_queries, w_query)
        + back_project(d_keys, w_key)
        + back_project(d_values, w_value)
    )
    summed = (
        lax.psum_scatter(grad_query, "dp", scatter_dimension=0, tiled=True),
        lax.psum_scatter(grad_bquery, "dp", scatter_dimension=0, tiled=True),
        lax.psum_scatter(grad_key, "dp", scatter_dimension=0, tiled=True),
        lax.psum_scatter(grad_value, "dp", scatter_dimension=0, tiled=True),
        lax.psum_scatter(grad_bvalue, "dp", scatter_dimension=0, tiled=True),
        lax.psum_scatter(grad_out, "dp", scatter_dimension=0, tiled=True),
        lax.psum_scatter(grad_bout, "dp", scatter_dimension=0, tiled=True),
        lax.psum_scatter(grad_gain_attn, "dp", scatter_dimension=0, tiled=True),
        lax.psum_scatter(grad_shift_attn, "dp", scatter_dimension=0, tiled=True),
        lax.psum_scatter(grad_up, "dp", scatter_dimension=0, tiled=True),
        lax.psum_scatter(grad_bup, "dp", scatter_dimension=0, tiled=True),
        lax.psum_scatter(grad_down, "dp", scatter_dimension=0, tiled=True),
        lax.psum_scatter(grad_bdown, "dp", scatter_dimension=0, tiled=True),
        lax.psum_scatter(grad_gain_ffn, "dp", scatter_dimension=0, tiled=True),
        lax.psum_scatter(grad_shift_ffn, "dp", scatter_dimension=0, tiled=True),
    )
    summed = tuple(
        (
            lax.psum(summed[0].astype(jnp.bfloat16), "sp").astype(jnp.float32),
            lax.psum(summed[1].astype(jnp.bfloat16), "sp").astype(jnp.float32),
            lax.psum(summed[2].astype(jnp.bfloat16), "sp").astype(jnp.float32),
            lax.psum(summed[3].astype(jnp.bfloat16), "sp").astype(jnp.float32),
            lax.psum(summed[4].astype(jnp.bfloat16), "sp").astype(jnp.float32),
            lax.psum(summed[5].astype(jnp.bfloat16), "sp").astype(jnp.float32),
            lax.psum(summed[6].astype(jnp.bfloat16), "sp").astype(jnp.float32),
            lax.psum(summed[7].astype(jnp.bfloat16), "sp").astype(jnp.float32),
            lax.psum(summed[8].astype(jnp.bfloat16), "sp").astype(jnp.float32),
            lax.psum(summed[9].astype(jnp.bfloat16), "sp").astype(jnp.float32),
            lax.psum(summed[10].astype(jnp.bfloat16), "sp").astype(jnp.float32),
            lax.psum(summed[11].astype(jnp.bfloat16), "sp").astype(jnp.float32),
            lax.psum(summed[12].astype(jnp.bfloat16), "sp").astype(jnp.float32),
            lax.psum(summed[13].astype(jnp.bfloat16), "sp").astype(jnp.float32),
            lax.psum(summed[14].astype(jnp.bfloat16), "sp").astype(jnp.float32),
        )
    )
    return (
        mixed.astype(jnp.bfloat16),
        d_tokens.astype(jnp.bfloat16),
        summed[0],
        summed[1],
        summed[2],
        summed[3],
        summed[4],
        summed[5],
        summed[6],
        summed[7],
        summed[8],
        summed[9],
        summed[10],
        summed[11],
        summed[12],
        summed[13],
        summed[14],
    )


def solution(mesh):
    placed = (
        P("sp", "dp", None),
        P("dp"),
        P(),
        P(),
        P(),
        P(),
        P(),
        P(),
        P(),
        P(),
        P(),
        P(),
        P(),
        P(),
        P(),
        P(),
        P(),
        P("sp", "dp", None),
    )
    fits = mesh.shape["dp"] == 8 and mesh.shape["sp"] == 4
    return jax.shard_map(
        fused if fits else shards,
        mesh=mesh,
        in_specs=placed,
        out_specs=(
            P("sp", "dp", None),
            P("sp", "dp", None),
            P("dp", None),
            P("dp"),
            P("dp", None),
            P("dp", None),
            P("dp"),
            P("dp", None),
            P("dp"),
            P("dp"),
            P("dp"),
            P("dp", None),
            P("dp"),
            P("dp", None),
            P("dp"),
            P("dp"),
            P("dp"),
        ),
        check_vma=False,
    )
```

```python
import functools

import jax
import jax.numpy as jnp
from jax import lax
from jax.experimental import pallas as pl
from jax.experimental.pallas import tpu as pltpu
from jax.sharding import PartitionSpec as P

HEADS = 12
HD = 64
EPS = 1e-05
MESH_ID = pl.DeviceIdType.MESH
BF = jnp.bfloat16
F32 = jnp.float32


def nn(left, right):
    return jnp.dot(left, right, preferred_element_type=F32)


def nt(left, right):
    return lax.dot_general(left, right, (((1,), (1,)), ((), ())), preferred_element_type=F32)


def tn(left, right):
    return lax.dot_general(left, right, (((0,), (0,)), ((), ())), preferred_element_type=F32)


def aligned(start, step=128):
    return pl.multiple_of(start, step)


UNITS = (
    ("d", 0, 0, 256), ("d", 0, 256, 256), ("d", 0, 512, 256), ("d", 1, 0, 256), ("d", 1, 256, 256),
    ("d", 1, 512, 256), ("d", 2, 0, 256), ("d", 2, 256, 256), ("d", 2, 512, 256), ("u", 0, 0, 1024),
    ("u", 1, 0, 1024), ("u", 2, 0, 1024), ("o",), ("p", 0, 3, 0), ("p", 0, 1, 1), ("p", 1, 2, 1), ("p", 0, 1, 2),
    ("p", 1, 1, 2), ("p", 2, 1, 2),
)
PATH = (
    "c102Y", "c10y2", "c01y2", "c102y", "cy012", "cy120", "c01y2", "cy102", "c120Y", "c01y2", "c012y", "cy012",
    "c102y", "cy012", "c120Y", "cy012", "c01y2", "c01y2", "c0y12",
)
ORDER = (
    "M", 0, 1, 2, "X", 0, "I0", 1, 2, 3, 4, 5, 6, 7, 8, "I1", 3, 0, 4, 5, 6, 2, 7, "H0", 8, 1, 0, 9, 3, 4, 10, 2, 6,
    1, 9, 5, 11, "F", 8, 3, 10, 0, 4, 7, 6, "A", 11, 2, 1, 5, 12, 0, "B0", 6, 4, 8, 12, 7, 3, 2, 13, 1, "B2", 9, 5, 6,
    13, 4, 14, 11, 3, 2, 15, "B4", 1, 6, 14, 15, 12, 10, "T", "K", 8, 7, 5, 9, 16, 13, 4, 3, 17, 18, "V0", 14, 16, 17,
    11, 18, "V1", 15, 10, 12, 7, 14, 13, 11, 16, 10, 17, 8, 5, 13, 18, 12, "V2", 9, 16, 7, 17, 11, 10, 15, 14, 18,
    "V3", 13, 12, 16, 17, 15, 9, 18, 11, 10, "V4", 14, 16, 17, 13, 12, 15, 18, 9, "V5", 16, 17, 15, 18,
)
VEC_PATH = "c120y"
ROWS_VEC = 16
CHUNK = 1024
ATTEND = 6


def unit_dims(unit, rows, width):
    kind = unit[0]
    if kind == "d":
        return None, unit[3], 128
    if kind == "u":
        return None, rows, unit[3]
    if kind == "o":
        return None, rows, width
    return unit[2], rows, 256


def land_shape(unit, path, stage, rows, width):
    many, r, c = unit_dims(unit, rows, width)
    lead = [2, 2, 2]
    for kind in path[: stage + 1]:
        if kind == "c" and unit[0] != "d":
            c //= 2
        elif kind in "cy":
            r //= 2
        elif kind != "Y":
            lead[2 - int(kind)] = 0
    return (() if many is None else (many,)) + tuple(n for n in lead if n) + (r, c)


def gelu_parts(x):
    cdf = 0.5 + 0.5 * lax.erf(x * (0.5**0.5))
    pdf = jnp.exp(-0.5 * x * x) * 0.3989422804014327
    return x * cdf, cdf + x * pdf


def layer_kernel(*refs):
    it = iter(refs)
    len_ref = next(it)
    bias_refs = [next(it) for _ in range(9)]
    (tok_ref, cot_ref, wq_ref, wk_ref, wv_ref, wo_ref, wu_ref, wd_ref) = (next(it) for _ in range(8))
    (mix_out, dtok_out, go_out, gp_out, gu_out, gd_out, gv_out) = (next(it) for _ in range(7))
    (raw_s, tokp, cotp, x_s, cot_s, x_t, hl_t, df_t) = (next(it) for _ in range(8))
    (wa, wu, wd, gd_s, qkv_s, p_s, att_s, linv_s, xh_s, rs_s, hl_s, act_s, gp_s, acc_s, km_s, vec_s) = (
        next(it) for _ in range(16)
    )
    vs, vl = next(it), next(it)
    lands = [[next(it) for _ in path] for path in PATH]
    tails = [next(it) if "y" in path else None for path in PATH]
    len_s = next(it)
    (wsem, lsem, asend, arecv, usend, urecv, ufin, vsend, vrecv) = (next(it) for _ in range(9))

    rows_loc, width = tok_ref.shape[0], tok_ref.shape[2]
    total = rows_loc * 4
    half = total // 2
    rows = width // 8
    dp, sp = lax.axis_index("dp"), lax.axis_index("sp")
    bits = [lax.rem(lax.div(dp, 2**k), 2) for k in range(3)]
    core, ybit = lax.rem(sp, 2), lax.div(sp, 2)

    def sp_xor(k):
        low, high = core, ybit
        if k & 1:
            low = 1 - low
        if k & 2:
            high = 1 - high
        return high * 2 + low

    def peer(kind):
        if kind == "c":
            return (dp, sp_xor(1))
        if kind in "yY":
            return (dp, sp_xor(2))
        k = int(kind)
        return (dp + 2**k * (1 - 2 * bits[k]), sp)

    barrier = pltpu.get_barrier_semaphore()
    greet = [(dp, sp_xor(k)) for k in (1, 2, 3)] + [peer(k) for k in "012"]
    for other in greet:
        pl.semaphore_signal(barrier, inc=1, device_id=other, device_id_type=MESH_ID)

    def load(src, dst, at):
        copy = pltpu.make_async_copy(src, dst, wsem.at[at])
        copy.start()
        return copy

    def landed(ref, sem):
        pltpu.make_async_copy(ref, ref, sem).wait()

    quick = rows_loc // 2
    tok_loads = [load(tok_ref.at[pl.ds(i * quick, quick)], raw_s.at[pl.ds(i * quick, quick)], i) for i in range(2)]
    len_load = load(len_ref, len_s, 12)
    attn_loads = [load(ref, wa.at[i], 2 + i) for i, ref in enumerate((wq_ref, wk_ref, wv_ref, wo_ref))]

    def exchange(src, dst, group, first=0, size=rows_loc):
        for k in (2, 3, 1):
            other = sp_xor(k)
            pltpu.make_async_remote_copy(
                src_ref=src.at[other, pl.ds(first, size)],
                dst_ref=dst.at[pl.ds(aligned(sp * rows_loc + first, size), size)],
                send_sem=asend.at[group],
                recv_sem=arecv.at[2 if group else 0 if k == 1 else 1],
                device_id=(dp, other),
                device_id_type=MESH_ID,
            ).start()
        dst[pl.ds(aligned(sp * rows_loc + first, size), size), :] = src[sp, pl.ds(first, size)]

    for i in range(2):
        tok_loads[i].wait()
        tokp[:, pl.ds(i * quick, quick)] = jnp.swapaxes(raw_s[pl.ds(i * quick, quick)], 0, 1)
        if i == 0:
            pl.semaphore_wait(barrier, len(greet))
        exchange(tokp, x_s, 0, i * quick, quick)
    cot_load = load(cot_ref, raw_s, 6)
    for j in range(3):
        for r in range(8):
            load(wu_ref.at[:, :, :, :, pl.ds(384 * r + 128 * j, 128)], wu.at[j, :, :, :, :, pl.ds(128 * r, 128)], 7 + j)
    for j in range(3):
        load(wd_ref.at[:, :, :, j], wd.at[j], 10)

    vec_s[1:2, :] = jnp.zeros((1, CHUNK), F32)
    for i, row in enumerate((0, 2, 3, 4, 5, 6, 7, 8)):
        vec_s[pl.ds(row, 1), pl.ds(0, width)] = bias_refs[i][...].astype(F32).reshape(1, width)
    for j in range(3):
        for r in range(8):
            part = bias_refs[8][pl.ds(384 * r + 128 * j, 128)]
            vec_s[pl.ds(10 + j, 1), pl.ds(128 * r, 128)] = part.astype(F32).reshape(1, 128)

    state = [dict(stage=0, copies=[]) for _ in UNITS]

    def region(unit, kinds, last_other=False, at_y=None):
        kind = unit[0]
        many, r, c = unit_dims(unit, rows, width)
        r0, c0 = (unit[2] if kind == "d" else 0), (256 * unit[3] if kind == "p" else unit[2] if kind == "u" else 0)
        lead = [slice(None)] * 3
        for i, step in enumerate(kinds):
            flip = last_other and i == len(kinds) - 1
            if step == "c":
                at = 1 - core if flip else core
                if kind == "d":
                    r //= 2
                    r0 = r0 + at * r
                else:
                    c //= 2
                    c0 = c0 + at * c
            elif step == "y":
                r //= 2
                r0 = r0 + (1 - ybit if flip else ybit if at_y is None else at_y) * r
            elif step != "Y":
                b = bits[int(step)]
                lead[2 - int(step)] = 1 - b if flip else b
        span = (pl.ds(r0 if isinstance(r0, int) else aligned(r0, 16), r), pl.ds(c0 if isinstance(c0, int) else aligned(c0), c))
        if kind == "d":
            return gd_s, (unit[1], *lead, *span)
        if kind == "u":
            return wu, (unit[1], *lead, *span)
        if kind == "o":
            return wa, (3, *lead, *span)
        return wd, (pl.ds(unit[1], many), *lead, *span)

    def out_region(unit, path, at_y=None):
        ref, at = region(unit, path, at_y=at_y)
        kind = unit[0]
        if kind == "d":
            return gd_out.at[unit[1], at[4], at[5]]
        if kind == "u":
            return gu_out.at[unit[1], at[4], at[5]]
        if kind == "o":
            return go_out.at[at[4], at[5]]
        return gp_out.at[at[0], at[4], at[5]]

    def send(n, stage, src, dst, to, last=False):
        copy = pltpu.make_async_remote_copy(
            src_ref=src,
            dst_ref=dst,
            send_sem=usend.at[n],
            recv_sem=ufin.at[0] if last else urecv.at[n, stage],
            device_id=to,
            device_id_type=MESH_ID,
        )
        copy.start()
        state[n]["copies"].append(copy)

    def advance(n):
        unit, path = UNITS[n], PATH[n]
        stage = state[n]["stage"]
        state[n]["stage"] += 1
        if stage > len(path):
            state[n]["copies"][stage - 1].wait_recv()
            dst = out_region(unit, path, 1 - ybit)
            send(n, stage, tails[n], dst, peer("c"), last=True)
            pltpu.make_async_copy(tails[n], dst, lsem.at[0]).start()
            return
        if stage > 0:
            state[n]["copies"][stage - 1].wait_recv()
            ref, at = region(unit, path[:stage])
            if path[stage - 1] == "Y":
                lands[n][stage - 1][...] = ref[at] + lands[n][stage - 1][...]
            else:
                ref[at] = ref[at] + lands[n][stage - 1][...]
        if stage < len(path):
            ref, at = region(unit, path[: stage + 1], last_other=True)
            send(n, stage, ref.at[at], lands[n][stage], peer(path[stage]))
            return
        dst = out_region(unit, path)
        if "Y" in path:
            src = lands[n][-1]
            send(n, stage, src, dst, peer("c"), last=True)
        else:
            ref, at = region(unit, path)
            src = ref.at[at]
            send(n, stage, src, tails[n], peer("y"))
            send(n, stage, src, dst, peer("c"), last=True)
        pltpu.make_async_copy(src, dst, lsem.at[0]).start()

    def finish(n):
        many, r, c = unit_dims(UNITS[n], rows, width)
        wide = (many or 1) * 8 * r * c // 256
        cols = next(b for b in (512, 384, 256, 128) if wide % b == 0 and wide // b <= HEADS)
        landed(p_s.at[pl.ds(0, wide // cols), pl.ds(0, 272), pl.ds(0, cols)], usend.at[n])

    def vec(row):
        return vec_s[pl.ds(row, 1), pl.ds(0, width)]

    def put_vec(row, value):
        vs[0, pl.ds(row, 1), pl.ds(0, value.shape[1])] = value

    vs[0] = jnp.zeros(vs.shape[1:], F32)
    len_load.wait()
    length = len_s[sp]
    dead = lax.broadcasted_iota(jnp.int32, (total, 128), 0) >= length
    km_s[...] = jnp.where(dead, -1e30, 0.0).astype(BF)
    ones = jnp.ones((16, total), BF)
    for ref in (x_t, hl_t, df_t):
        ref[pl.ds(width, 16), :] = ones

    def qkv(start):
        def one(w, carry):
            r = nn(x_s[pl.ds(start, half), :], wa[w].reshape(width, width)) + vec_s[pl.ds(w, 1), pl.ds(0, width)]
            r = r * jnp.where(w == 0, HD ** (-0.5), 1.0)
            qkv_s[w, pl.ds(start, half), :] = r.astype(BF)
            return carry

        lax.fori_loop(0, 3, one, 0)

    for copy in attn_loads[:3]:
        copy.wait()
    landed(x_s.at[pl.ds(0, rows_loc)], arecv.at[0])
    qkv(aligned(ybit * half))
    cot_load.wait()
    cotp[...] = jnp.swapaxes(raw_s[...], 0, 1)
    landed(x_s.at[pl.ds(0, half)], arecv.at[1])
    exchange(cotp, cot_s, 1)
    qkv(aligned((1 - ybit) * half))

    lane = lax.broadcasted_iota(jnp.int32, (total, 128), 1)
    low = lane < HD
    zeros = jnp.zeros((total, 128), BF)
    ones2 = jnp.ones((total, 128), BF)

    def attend(g):
        cols = pl.ds(aligned(g * 128), 128)
        q2, k2, v2 = qkv_s[0, :, cols], qkv_s[1, :, cols], qkv_s[2, :, cols]
        outs = []
        for h in range(2):
            mine = low if h == 0 else jnp.logical_not(low)
            qh = jnp.where(mine, q2, jnp.where(lane == HD * (1 - h), ones2, zeros))
            kh = jnp.where(mine, k2, km_s[...])
            vh = jnp.where(mine, v2, ones2)
            s = nt(qh, kh)
            e = jnp.exp(s - jnp.max(s, axis=-1, keepdims=True)).astype(BF)
            p_s[g * 2 + h] = e
            outs.append(nn(e, vh))
        num = jnp.where(low, outs[0], outs[1])
        den = pltpu.roll(jnp.where(low, outs[1], outs[0]), HD, axis=1)
        inv = 1.0 / den
        linv_s[:, cols] = inv.astype(BF)
        att_s[:, cols] = (num * inv).astype(BF)

    def attend_some(i, carry):
        for g in range(ATTEND):
            attend(i * ATTEND + g)
        return carry

    lax.fori_loop(0, HEADS // 2 // ATTEND, attend_some, 0)

    attn_loads[3].wait()

    def first_norm(i, carry):
        at = pl.ds(aligned(256 * i, 256), 256)
        r = nn(att_s[at, :], wa[3].reshape(width, width)) + vec(3) + x_s[at, :].astype(F32)
        mean = jnp.mean(r, axis=-1, keepdims=True)
        center = r - mean
        rs = lax.rsqrt(jnp.mean(center * center, axis=-1, keepdims=True) + EPS)
        xh = center * rs
        hidden = xh * vec(4) + vec(5)
        rs_s[at, :] = rs
        xh_s[at, :] = xh.astype(BF)
        acc_s[at, :] = hidden
        hl_s[at, :] = hidden.astype(BF)
        return carry

    lax.fori_loop(0, total // 256, first_norm, 0)

    for j in range(3):
        landed(wu.at[j], wsem.at[7 + j])

    def up(j, carry):
        inner = nn(hl_s[...], wu[j].reshape(width, CHUNK)) + vec_s[pl.ds(10 + j, 1), :]
        value, slope = gelu_parts(inner)
        act_s[j] = value.astype(BF)
        gp_s[j] = slope.astype(BF)
        return carry

    lax.fori_loop(0, 3, up, 0)

    landed(wd, wsem.at[10])

    def down(i, carry):
        cols = pl.ds(aligned(i * 256), 256)
        r = acc_s[:, cols] + vec_s[pl.ds(6, 1), cols]
        for j in range(3):
            r = r + nn(act_s[j], wd[j, :, :, :, :, cols].reshape(CHUNK, 256))
        acc_s[:, cols] = r
        return carry

    lax.fori_loop(0, width // 256, down, 0)

    away = cot_s.at[pl.ds(0, 3 * rows_loc)]
    landed(away, arecv.at[2])
    landed(away, asend.at[0])
    landed(away, asend.at[1])

    def second_norm(i, carry):
        at = pl.ds(aligned(128 * i, 128), 128)
        r = acc_s[at, :]
        mean = jnp.mean(r, axis=-1, keepdims=True)
        center = r - mean
        rs = lax.rsqrt(jnp.mean(center * center, axis=-1, keepdims=True) + EPS)
        xh = center * rs
        tokp[i] = (xh * vec(7) + vec(8)).astype(BF)
        dy = cot_s[at, :].astype(F32)
        dxh = dy * vec(7)
        d2 = rs * (dxh - jnp.mean(dxh, axis=-1, keepdims=True) - xh * jnp.mean(dxh * xh, axis=-1, keepdims=True))
        acc_s[at, :] = d2
        low2 = d2.astype(BF)
        cot_s[at, :] = low2
        df_t[:width, at] = low2.T
        adds = (
            jnp.sum(dy * xh, axis=0, keepdims=True),
            jnp.sum(dy, axis=0, keepdims=True),
            jnp.sum(low2.astype(F32), axis=0, keepdims=True),
        )
        return tuple(c + a for c, a in zip(carry, adds))

    zero = jnp.zeros((1, width), F32)
    g_gain, g_shift, g_bdown = lax.fori_loop(0, total // 128, second_norm, (zero, zero, zero))
    put_vec(6, g_gain)
    put_vec(7, g_shift)
    put_vec(5, g_bdown)

    given = []

    def give_back(src, dst, group):
        for k in (2, 3, 1):
            other = sp_xor(k)
            pltpu.make_async_remote_copy(
                src_ref=src.at[other],
                dst_ref=dst.at[sp],
                send_sem=asend.at[group],
                recv_sem=arecv.at[group + 1],
                device_id=(dp, other),
                device_id_type=MESH_ID,
            ).start()
        own = pltpu.make_async_copy(src.at[sp], dst.at[sp], lsem.at[group - 1])
        own.start()
        given.append((group, dst, own))

    def grad_down(j, first, size):
        r = nn(df_t[pl.ds(first, size), :], act_s[j]).astype(BF)
        for k in range(8):
            gd_s[j, k // 4, k // 2 % 2, k % 2, pl.ds(first, size), :] = r[:, 128 * k : 128 * k + 128]

    def inner_back(first, count):
        def body(j, carry):
            gp_s[j] = nt(cot_s[...], wd[j].reshape(CHUNK, width)).astype(BF) * gp_s[j]
            return carry

        lax.fori_loop(first, first + count, body, 0)

    def hidden_back(first, count):
        def body(j, carry):
            acc_s[...] += nt(gp_s[j], wu[j].reshape(width, CHUNK))
            return carry

        lax.fori_loop(first, first + count, body, 0)

    def grad_up(first, count):
        def body(j, carry):
            r = nn(hl_t[...], gp_s[j])
            wu[j] = r[:width].astype(BF).reshape(2, 2, 2, rows, CHUNK)
            vs[0, pl.ds(10 + j, 1), :] = r[width : width + 1]
            return carry

        lax.fori_loop(first, first + count, body, 0)

    def first_back():
        def body(i, carry):
            at = pl.ds(aligned(128 * i, 128), 128)
            dy = acc_s[at, :]
            xh = xh_s[at, :].astype(F32)
            dxh = dy * vec(4)
            d1 = rs_s[at, :] * (
                dxh - jnp.mean(dxh, axis=-1, keepdims=True) - xh * jnp.mean(dxh * xh, axis=-1, keepdims=True)
            )
            acc_s[at, :] = d1
            dh_s[at, :] = d1.astype(BF)
            adds = (jnp.sum(dy * xh, axis=0, keepdims=True), jnp.sum(dy, axis=0, keepdims=True))
            return tuple(c + a for c, a in zip(carry, adds))

        g_gain, g_shift = lax.fori_loop(0, total // 128, body, (zero, zero))
        put_vec(3, g_gain)
        put_vec(4, g_shift)

    def attended_back():
        d = nt(dh_s[...], wa[3].reshape(width, width))
        da_s[...] = (d * linv_s[...].astype(F32)).astype(BF)

    da_s = linv_s

    def grad_out():
        df_t[:width, :] = att_s[...].T
        r = nn(df_t[...], dh_s[...])
        wa[3] = r[:width].astype(BF).reshape(2, 2, 2, rows, width)
        vs[0, 2:3, :width] = r[width : width + 1]

    def attend_back(g):
        cols = slice(g * 128, g * 128 + 128)
        q2, k2, v2, d2 = qkv_s[0, :, cols], qkv_s[1, :, cols], qkv_s[2, :, cols], da_s[:, cols]
        prod = d2.astype(F32) * att_s[:, cols].astype(F32)
        dqs, dks, dvs = [], [], []
        for h in range(2):
            mine = low if h == 0 else jnp.logical_not(low)
            delta = -jnp.sum(jnp.where(mine, prod, 0.0), axis=-1, keepdims=True)
            upper = delta.astype(BF)
            lower = (delta - upper.astype(F32)).astype(BF)
            other = HD * (1 - h)
            fill = jnp.where(lane == other, upper, jnp.where(lane == other + 1, lower, zeros))
            e = p_s[g * 2 + h]
            ds = e * nt(jnp.where(mine, d2, fill), jnp.where(mine, v2, ones2)).astype(BF)
            dqs.append(nn(ds, k2))
            dks.append(tn(ds, q2))
            dvs.append(tn(e, d2))
        qkv_s[0, :, cols] = (jnp.where(low, dqs[0], dqs[1]) * HD ** (-0.5)).astype(BF)
        qkv_s[1, :, cols] = jnp.where(low, dks[0], dks[1]).astype(BF)
        qkv_s[2, :, cols] = jnp.where(low, dvs[0], dvs[1]).astype(BF)

    def grad_proj(n):
        cols = slice(256 * n, 256 * n + 256)

        def body(w, carry):
            r = nn(x_t[...], qkv_s[w, :, cols])
            wd[w, :, :, :, :rows, cols] = r[:width].astype(BF).reshape(2, 2, 2, rows, 256)
            vs[0, pl.ds(lax.rem(w * 14, 27), 1), cols] = r[width : width + 1]
            return carry

        lax.fori_loop(0, 3, body, 0)

    def tokens_back():
        def body(w, carry):
            acc_s[...] += nt(qkv_s[w], wa[w].reshape(width, width))
            return carry

        lax.fori_loop(0, 3, body, 0)
        cotp[...] = acc_s[...].astype(BF).reshape(4, rows_loc, width)

    vec_copies = []

    def vec_step(i):
        if i == 0:
            vl[0] = vs[0].astype(BF)
        else:
            vec_copies[i - 1].wait_recv()
            vl[i] = vl[i - 1] + vl[i]
        if i == 5:
            load(vl.at[5], gv_out, 11)
        if i < 5:
            copy = pltpu.make_async_remote_copy(
                src_ref=vl.at[i],
                dst_ref=vl.at[i + 1],
                send_sem=vsend.at[0],
                recv_sem=vrecv.at[i],
                device_id=peer(VEC_PATH[i]),
                device_id_type=MESH_ID,
            )
            copy.start()
            vec_copies.append(copy)

    def transpose_tokens():
        x_t[:width, :] = x_s[...].T
        hl_t[:width, :] = hl_s[...].T

    dh_s = hl_s

    made = set()

    def produce(n):
        unit = UNITS[n]
        if unit[0] == "d" and unit[1] == 0:
            grad_down(0, unit[2], unit[3])
            return
        key = (unit[0], unit[3]) if unit[0] == "p" else (unit[0], min(unit[1], 1)) if unit[0] in "du" else unit
        if key in made:
            return
        made.add(key)
        if key == ("d", 1):

            def both(j, carry):
                grad_down(j, 0, width)
                return carry

            lax.fori_loop(1, 3, both, 0)
        elif key[0] == "u":
            grad_up(key[1], 1 + key[1])
        elif key[0] == "o":
            grad_out()
        else:
            grad_proj(unit[3])

    for step in ORDER:
        if isinstance(step, int):
            if state[step]["stage"] == 0:
                produce(step)
            advance(step)
            continue
        name, at = step[0], int(step[1:] or 0)
        if name == "I":
            inner_back(at, 1 + at)
        elif name == "H":
            hidden_back(at, 3)
        elif name == "F":
            first_back()
        elif name == "A":
            attended_back()
        elif name == "B":
            attend_back(at)
            attend_back(at + 1)
        elif name == "T":
            tokens_back()
        elif name == "X":
            transpose_tokens()
        elif name == "M":
            give_back(tokp, mix_out, 2)
        elif name == "K":
            give_back(cotp, dtok_out, 3)
        elif name == "V":
            vec_step(at)
    landed(gv_out, wsem.at[11])
    final = p_s.at[pl.ds(0, 2), pl.ds(0, width * 9 // 16)]
    landed(final, ufin.at[0])
    landed(final, lsem.at[0])
    for n in range(len(UNITS)):
        finish(n)
    landed(vl.at[pl.ds(0, 5)], vsend.at[0])
    for group, dst, own in given:
        landed(tokp.at[pl.ds(0, 3)], asend.at[group])
        landed(dst.at[pl.ds(0, 3)], arecv.at[group + 1])
        own.wait()


def finish_kernel(*refs):
    it = iter(refs)
    sources = [next(it) for _ in range(7)]
    (o_mix, o_dtok, o_wq, o_bq, o_wk, o_wv, o_bv, o_wo, o_bo, o_ga, o_sa, o_up, o_bup, o_down, o_bdown, o_gf, o_sf) = (
        next(it) for _ in range(17)
    )
    held = [next(it) for _ in range(7)]
    staged = [next(it) for _ in range(5)]
    isem, osem = next(it), next(it)
    mix, dtok, go, gp, gu, gd, gv = held
    s_mix, s_dtok, s_sq, s_up, s_down = staged
    part = gu.shape[1] // 2
    pieces = [(4, (slice(None), pl.ds(i * part, part))) for i in range(2)] + [(5, (j,)) for j in range(3)]
    pieces += [(3, (w,)) for w in range(3)] + [(i, ()) for i in (2, 0, 1, 6)]
    loads = []
    for i, at in pieces:
        src, dst = (sources[i].at[at], held[i].at[at]) if at else (sources[i], held[i])
        copy = pltpu.make_async_copy(src, dst, isem.at[len(loads)])
        copy.start()
        loads.append(copy)
    width = mix.shape[2]
    rows = width // 8
    dp = lax.axis_index("dp")
    stores = []

    def store(src, dst):
        copy = pltpu.make_async_copy(src, dst, osem.at[len(stores)])
        copy.start()
        stores.append(copy)

    for i in range(2):
        loads[i].wait()
        at = slice(part * i, part * i + part)
        for j in range(3):
            for r in range(8):
                s_up[at, 384 * r + 128 * j : 384 * r + 128 * j + 128] = gu[j, at, 128 * r : 128 * r + 128].astype(F32)
        store(s_up.at[pl.ds(part * i, part)], o_up.at[pl.ds(part * i, part)])
    for j in range(3):
        loads[2 + j].wait()
        s_down[128 * j : 128 * j + 128, :] = gd[j].astype(F32).T
        store(s_down.at[pl.ds(128 * j, 128)], o_down.at[pl.ds(128 * j, 128)])
    for w in range(4):
        loads[5 + w].wait()
        s_sq[w] = (go[...] if w == 3 else gp[w]).astype(F32)
        store(s_sq.at[w], (o_wq, o_wk, o_wv, o_wo)[w])
    loads[9].wait()
    s_mix[...] = jnp.swapaxes(mix[...], 0, 1)
    store(s_mix, o_mix)
    loads[10].wait()
    s_dtok[...] = jnp.swapaxes(dtok[...], 0, 1)
    store(s_dtok, o_dtok)
    loads[11].wait()
    for j in range(3):
        o_bup[pl.ds(128 * j, 128)] = gv[pl.ds(10 + j, 1), pl.ds(aligned(dp * 128), 128)].astype(F32).reshape(128)
    turned = pltpu.roll(gv[pl.ds(0, 8), pl.ds(0, width)].astype(F32), lax.rem(width - rows * dp, width), axis=1)
    for i, ref in enumerate((o_bq, o_bv, o_bo, o_ga, o_sa, o_bdown, o_gf, o_sf)):
        ref[...] = turned[i : i + 1, :rows].reshape(rows)
    for copy in stores:
        copy.wait()


def fused(
    tokens, lengths, w_query, b_query, w_key, w_value, b_value, w_out, b_out, gain_attn, shift_attn,
    w_up, b_up, w_down, b_down, gain_ffn, shift_ffn, cotangent,
):
    rows_loc, pairs, width = tokens.shape
    total = rows_loc * 4
    rows = width // 8
    square = lambda w: w.reshape(2, 2, 2, rows, w.shape[1])
    args = (
        lengths, b_query, b_value, b_out, gain_attn, shift_attn, b_down, gain_ffn, shift_ffn, b_up, tokens, cotangent,
        square(w_query), square(w_key), square(w_value), square(w_out), square(w_up),
        w_down.reshape(2, 2, 2, 3, 128, width),
    )
    vm = lambda shape, dtype=BF: pltpu.VMEM(shape, dtype)
    full = (total, width)
    swapped = (4, rows_loc, width)
    turned = (width + 16, total)
    scratch = [
        vm((rows_loc, 4, width)), vm(swapped), vm(swapped), vm(full), vm(full), vm(turned), vm(turned), vm(turned),
        vm((4, 2, 2, 2, rows, width)), vm((3, 2, 2, 2, rows, CHUNK)), vm((3, 2, 2, 2, 128, width)),
        vm((3, 2, 2, 2, width, 128)),
        vm((3, total, width)), vm((HEADS, total, total)), vm(full), vm(full),
        vm(full), vm((total, 1), F32), vm(full), vm((3, total, CHUNK)), vm((3, total, CHUNK)),
        vm(full, F32), vm((total, 128)), vm((ROWS_VEC, CHUNK), F32),
        vm((1, ROWS_VEC, CHUNK), F32), vm((6, ROWS_VEC, CHUNK)),
    ]
    for unit, path in zip(UNITS, PATH):
        scratch += [vm(land_shape(unit, path, s, rows, width)) for s in range(len(path))]
    for unit, path in zip(UNITS, PATH):
        if "y" in path:
            scratch.append(vm(land_shape(unit, path, 4, rows, width)))
    dma = pltpu.SemaphoreType.DMA
    count = len(UNITS)
    scratch.append(pltpu.SMEM((4,), jnp.int32))
    scratch += [dma((13,)), dma((3,)), dma((4,)), dma((5,)), dma((count,)), dma((count, 6)), dma((1,)), dma((1,)), dma((5,))]
    anywhere = pl.BlockSpec(memory_space=pl.ANY)
    vmem = pl.BlockSpec(memory_space=pltpu.VMEM)
    got = pl.pallas_call(
        layer_kernel,
        out_shape=(
            jax.ShapeDtypeStruct(swapped, BF),
            jax.ShapeDtypeStruct(swapped, BF),
            jax.ShapeDtypeStruct((rows, width), BF),
            jax.ShapeDtypeStruct((3, rows, width), BF),
            jax.ShapeDtypeStruct((3, rows, CHUNK), BF),
            jax.ShapeDtypeStruct((3, width, 128), BF),
            jax.ShapeDtypeStruct((ROWS_VEC, CHUNK), BF),
        ),
        in_specs=[anywhere] + [vmem] * 9 + [anywhere] * 8,
        out_specs=(anywhere,) * 7,
        scratch_shapes=scratch,
        compiler_params=pltpu.CompilerParams(collective_id=0, has_side_effects=True, vmem_limit_bytes=63 * 2**20),
    )(*args)
    small = jax.ShapeDtypeStruct((rows,), F32)
    flat = jax.ShapeDtypeStruct((rows, width), F32)
    whole = jax.ShapeDtypeStruct((rows_loc, 4, width), BF)
    return pl.pallas_call(
        finish_kernel,
        out_shape=(
            whole, whole, flat, small, flat, flat, small, flat, small, small, small,
            jax.ShapeDtypeStruct((rows, 3 * CHUNK), F32),
            jax.ShapeDtypeStruct((384,), F32),
            jax.ShapeDtypeStruct((384, width), F32),
            small, small, small,
        ),
        in_specs=[anywhere] * 7,
        out_specs=tuple(anywhere if big else vmem for big in (1, 1, 1, 0, 1, 1, 0, 1, 0, 0, 0, 1, 0, 1, 0, 0, 0)),
        scratch_shapes=[vm(value.shape, value.dtype) for value in got]
        + [
            vm((rows_loc, 4, width)), vm((rows_loc, 4, width)), vm((4, rows, width), F32),
            vm((rows, 3 * CHUNK), F32), vm((384, width), F32), dma((12,)), dma((11,)),
        ],
        compiler_params=pltpu.CompilerParams(vmem_limit_bytes=63 * 2**20),
    )(*got)


def norm_layer(resid, gain, shift):
    center = resid - jnp.mean(resid, axis=-1, keepdims=True)
    spread = jnp.mean(center * center, axis=-1, keepdims=True)
    return center * lax.rsqrt(spread + 1e-05) * gain + shift


def exact_gelu(value):
    return jax.nn.gelu(value, approximate=False)


def project(left, weight):
    return jnp.einsum("spd,de->spe", left, weight, preferred_element_type=jnp.float32)


def back_project(grad_in, weight):
    return jnp.einsum("spe,de->spd", grad_in, weight, preferred_element_type=jnp.float32)


def weight_grad(left, right):
    return jnp.einsum("spd,spe->de", left, right, preferred_element_type=jnp.float32)


def column_sum(grad_in):
    return jnp.sum(grad_in.astype(jnp.float32), axis=(0, 1))


def shards(
    tokens,
    lengths,
    w_query,
    b_query,
    w_key,
    w_value,
    b_value,
    w_out,
    b_out,
    gain_attn,
    shift_attn,
    w_up,
    b_up,
    w_down,
    b_down,
    gain_ffn,
    shift_ffn,
    cotangent,
):
    local_rows, pair_count, model_width = tokens.shape
    score_scale = HD ** (-0.5)
    total_len = local_rows * lax.axis_size("sp")
    queries = (project(tokens, w_query) + b_query.astype(jnp.float32)).astype(jnp.bfloat16)
    keys_local = project(tokens, w_key).astype(jnp.bfloat16)
    values_local = (project(tokens, w_value) + b_value.astype(jnp.float32)).astype(jnp.bfloat16)
    keys_all, values_all = (
        lax.all_gather(keys_local, "sp", axis=0, tiled=True),
        lax.all_gather(values_local, "sp", axis=0, tiled=True),
    )
    query_heads = queries.reshape(local_rows, pair_count, HEADS, HD)
    key_heads = keys_all.reshape(total_len, pair_count, HEADS, HD)
    value_heads = values_all.reshape(total_len, pair_count, HEADS, HD)
    scores = (
        jnp.einsum("iphe,jphe->phij", query_heads, key_heads, preferred_element_type=jnp.float32)
        * score_scale
    )
    key_valid = jnp.arange(total_len)[None, :] < lengths[:, None]
    scores = jnp.where(key_valid[:, None, None, :], scores, -1e30)
    top_score = jnp.max(scores, axis=-1, keepdims=True)
    expo = jnp.exp(scores - top_score)
    row_total = jnp.sum(expo, axis=-1, keepdims=True)
    weights_full = expo / row_total
    probs = weights_full.astype(jnp.bfloat16)
    attended = jnp.einsum("phij,jphe->iphe", probs, value_heads, preferred_element_type=jnp.float32)
    attended_low = attended.reshape(local_rows, pair_count, model_width).astype(jnp.bfloat16)
    branch = project(attended_low, w_out) + b_out.astype(jnp.float32)
    first_sum = tokens.astype(jnp.float32) + branch
    hidden, first_back = jax.vjp(
        norm_layer, first_sum, gain_attn.astype(jnp.float32), shift_attn.astype(jnp.float32)
    )
    hidden_low = hidden.astype(jnp.bfloat16)
    inner = project(hidden_low, w_up) + b_up.astype(jnp.float32)
    activated, gelu_back = jax.vjp(exact_gelu, inner)
    activated_low = activated.astype(jnp.bfloat16)
    second_sum = hidden + project(activated_low, w_down) + b_down.astype(jnp.float32)
    mixed, second_back = jax.vjp(
        norm_layer, second_sum, gain_ffn.astype(jnp.float32), shift_ffn.astype(jnp.float32)
    )
    d_second, grad_gain_ffn, grad_shift_ffn = second_back(cotangent.astype(jnp.float32))
    d_ffn = d_second.astype(jnp.bfloat16)
    grad_down = weight_grad(activated_low, d_ffn)
    grad_bdown = column_sum(d_ffn)
    d_inner = gelu_back(back_project(d_ffn, w_down))[0].astype(jnp.bfloat16)
    grad_up = weight_grad(hidden_low, d_inner)
    grad_bup = column_sum(d_inner)
    d_hidden = d_second + back_project(d_inner, w_up)
    d_first, grad_gain_attn, grad_shift_attn = first_back(d_hidden)
    d_branch = d_first.astype(jnp.bfloat16)
    grad_out = weight_grad(attended_low, d_branch)
    grad_bout = column_sum(d_branch)
    d_attended = back_project(d_branch, w_out).astype(jnp.bfloat16)
    d_att_heads = d_attended.reshape(local_rows, pair_count, HEADS, HD)
    d_probs = jnp.einsum(
        "iphe,jphe->phij", d_att_heads, value_heads, preferred_element_type=jnp.float32
    )
    row_delta = jnp.sum(weights_full * d_probs, axis=-1, keepdims=True)
    d_scores = weights_full * (d_probs - row_delta)
    d_scores_low = d_scores.astype(jnp.bfloat16)
    d_query_heads = (
        jnp.einsum("phij,jphe->iphe", d_scores_low, key_heads, preferred_element_type=jnp.float32)
        * score_scale
    )
    d_queries = d_query_heads.reshape(local_rows, pair_count, model_width).astype(jnp.bfloat16)
    row_count = local_rows * lax.axis_size("sp")
    key_part = (
        jnp.einsum("phij,iphe->jphe", d_scores_low, query_heads, preferred_element_type=jnp.float32)
        * score_scale
    )
    value_part = jnp.einsum(
        "phij,iphe->jphe", probs, d_att_heads, preferred_element_type=jnp.float32
    )
    key_grads = lax.psum_scatter(
        jnp.concatenate(
            (
                key_part.reshape(row_count, pair_count, model_width),
                value_part.reshape(row_count, pair_count, model_width),
            ),
            axis=2,
        ).astype(jnp.bfloat16),
        "sp",
        scatter_dimension=0,
        tiled=True,
    ).astype(jnp.float32)
    d_keys = key_grads[:, :, :model_width].astype(jnp.bfloat16)
    d_values = key_grads[:, :, model_width:].astype(jnp.bfloat16)
    grad_query = weight_grad(tokens, d_queries)
    grad_bquery = column_sum(d_queries)
    grad_key = weight_grad(tokens, d_keys)
    grad_value = weight_grad(tokens, d_values)
    grad_bvalue = column_sum(d_values)
    d_tokens = (
        d_first
        + back_project(d_queries, w_query)
        + back_project(d_keys, w_key)
        + back_project(d_values, w_value)
    )
    summed = (
        lax.psum_scatter(grad_query, "dp", scatter_dimension=0, tiled=True),
        lax.psum_scatter(grad_bquery, "dp", scatter_dimension=0, tiled=True),
        lax.psum_scatter(grad_key, "dp", scatter_dimension=0, tiled=True),
        lax.psum_scatter(grad_value, "dp", scatter_dimension=0, tiled=True),
        lax.psum_scatter(grad_bvalue, "dp", scatter_dimension=0, tiled=True),
        lax.psum_scatter(grad_out, "dp", scatter_dimension=0, tiled=True),
        lax.psum_scatter(grad_bout, "dp", scatter_dimension=0, tiled=True),
        lax.psum_scatter(grad_gain_attn, "dp", scatter_dimension=0, tiled=True),
        lax.psum_scatter(grad_shift_attn, "dp", scatter_dimension=0, tiled=True),
        lax.psum_scatter(grad_up, "dp", scatter_dimension=0, tiled=True),
        lax.psum_scatter(grad_bup, "dp", scatter_dimension=0, tiled=True),
        lax.psum_scatter(grad_down, "dp", scatter_dimension=0, tiled=True),
        lax.psum_scatter(grad_bdown, "dp", scatter_dimension=0, tiled=True),
        lax.psum_scatter(grad_gain_ffn, "dp", scatter_dimension=0, tiled=True),
        lax.psum_scatter(grad_shift_ffn, "dp", scatter_dimension=0, tiled=True),
    )
    summed = tuple(
        (
            lax.psum(summed[0].astype(jnp.bfloat16), "sp").astype(jnp.float32),
            lax.psum(summed[1].astype(jnp.bfloat16), "sp").astype(jnp.float32),
            lax.psum(summed[2].astype(jnp.bfloat16), "sp").astype(jnp.float32),
            lax.psum(summed[3].astype(jnp.bfloat16), "sp").astype(jnp.float32),
            lax.psum(summed[4].astype(jnp.bfloat16), "sp").astype(jnp.float32),
            lax.psum(summed[5].astype(jnp.bfloat16), "sp").astype(jnp.float32),
            lax.psum(summed[6].astype(jnp.bfloat16), "sp").astype(jnp.float32),
            lax.psum(summed[7].astype(jnp.bfloat16), "sp").astype(jnp.float32),
            lax.psum(summed[8].astype(jnp.bfloat16), "sp").astype(jnp.float32),
            lax.psum(summed[9].astype(jnp.bfloat16), "sp").astype(jnp.float32),
            lax.psum(summed[10].astype(jnp.bfloat16), "sp").astype(jnp.float32),
            lax.psum(summed[11].astype(jnp.bfloat16), "sp").astype(jnp.float32),
            lax.psum(summed[12].astype(jnp.bfloat16), "sp").astype(jnp.float32),
            lax.psum(summed[13].astype(jnp.bfloat16), "sp").astype(jnp.float32),
            lax.psum(summed[14].astype(jnp.bfloat16), "sp").astype(jnp.float32),
        )
    )
    return (
        mixed.astype(jnp.bfloat16),
        d_tokens.astype(jnp.bfloat16),
        summed[0],
        summed[1],
        summed[2],
        summed[3],
        summed[4],
        summed[5],
        summed[6],
        summed[7],
        summed[8],
        summed[9],
        summed[10],
        summed[11],
        summed[12],
        summed[13],
        summed[14],
    )


def solution(mesh):
    placed = (
        P("sp", "dp", None),
        P("dp"),
        P(),
        P(),
        P(),
        P(),
        P(),
        P(),
        P(),
        P(),
        P(),
        P(),
        P(),
        P(),
        P(),
        P(),
        P(),
        P("sp", "dp", None),
    )
    fits = mesh.shape["dp"] == 8 and mesh.shape["sp"] == 4
    return jax.shard_map(
        fused if fits else shards,
        mesh=mesh,
        in_specs=placed,
        out_specs=(
            P("sp", "dp", None),
            P("sp", "dp", None),
            P("dp", None),
            P("dp"),
            P("dp", None),
            P("dp", None),
            P("dp"),
            P("dp", None),
            P("dp"),
            P("dp"),
            P("dp"),
            P("dp", None),
            P("dp"),
            P("dp", None),
            P("dp"),
            P("dp"),
            P("dp"),
        ),
        check_vma=False,
    )
```
